32 devices in a mesh: dp: 4 (over y, x), tensor: 8 (over z, core).
Axes of the slice: x: 2, y: 2, z: 4, core: 2. Of those that a mesh axis runs over, the one named last changes fastest.
Arguments:
- tokens: bfloat16 [8192, 2048], P(('dp', 'tensor')), may hold values from -6 to 6
- out_grad: bfloat16 [8192, 2048], P(('dp', 'tensor')), may hold values from -6 to 6
- query_two: bfloat16 [8192, 2048], P('dp', 'tensor'), may hold values from -6 to 6
- grad_two: bfloat16 [8192, 2048], P('dp', 'tensor'), may hold values from -6 to 6
- doc_split: int32 [4], P('dp'), may hold values from 0 to 1, as said below
- attn_gain: float32 [2048], replicated, may hold values from 0.5 to 1.5
- mlp_gain: float32 [2048], replicated, may hold values from 0.5 to 1.5
- w_query: bfloat16 [2048, 2048], P(None, 'tensor'), may hold values from -0.125 to 0.125
- w_kv: bfloat16 [2048, 256], replicated, may hold values from -0.125 to 0.125
- w_out: bfloat16 [2048, 2048], P('tensor'), may hold values from -1.5 to 1.5
- w_gate: bfloat16 [2048, 5632], P(None, 'tensor'), may hold values from -0.125 to 0.125
- w_up: bfloat16 [2048, 5632], P(None, 'tensor'), may hold values from -0.125 to 0.125
- w_down: bfloat16 [5632, 2048], P('tensor'), may hold values from -0.078125 to 0.078125
Outputs:
- block_output: bfloat16 [8192, 2048], P(('dp', 'tensor'))
- tokens_grad: bfloat16 [8192, 2048], P(('dp', 'tensor'))
- attn_gain_grad: float32 [2048], replicated
- mlp_gain_grad: float32 [2048], replicated
- query_w_grad: float32 [2048, 2048], P(None, 'tensor')
- kv_w_grad: float32 [2048, 256], replicated
- out_w_grad: float32 [2048, 2048], P('tensor')
- gate_w_grad: float32 [2048, 5632], P(None, 'tensor')
- up_w_grad: float32 [2048, 5632], P(None, 'tensor')
- down_w_grad: float32 [5632, 2048], P('tensor')
The draws below stay inside these ranges and needn't reach their ends.
Inputs may be any that keep to these rules, and one draw needn't show every extreme that they name: `doc_split`: each entry is 0 or 1; every draw has a shard of each kind.
All inputs are finite; a program needn't handle non-finite values.
Results may differ from the reference program's by a relative error of at most 0.024.
Values may be sent and summed in bfloat16 or wider, within the bound.
A program may use at most 256 MiB of HBM per device.

```python
import jax
import jax.numpy as jnp
from jax import lax

D = 2048
H = 16
HD = 128
FF = 5632
SEQ_LONG = 2048
SEQ_SHORT = 1024
TOKENS = 8192
N_DP = 4


def draw_doc_split(key, part):
    bit_key, one_key, zero_key = jax.random.split(jax.random.fold_in(key, 7), 3)
    shard_bits = jax.random.randint(bit_key, (N_DP,), 0, 2)
    one_shard = jax.random.randint(one_key, (), 0, N_DP)
    zero_shard = (one_shard + 1 + jax.random.randint(zero_key, (), 0, N_DP - 1)) % N_DP
    shard_bits = shard_bits.at[one_shard].set(1).at[zero_shard].set(0)
    return shard_bits.astype(jnp.int32)


def block_levels(stream_key, shape, cuts, least, largest):
    level, own = 1.0, jax.random.fold_in(stream_key, 6)
    for dim, parts in cuts:
        heights = jnp.exp(jax.random.uniform(jax.random.fold_in(own, dim), (parts,), jnp.float32, least / len(cuts), largest / len(cuts)))
        level = level * jnp.repeat(heights, shape[dim] // parts).reshape([-1 if axis == dim else 1 for axis in range(len(shape))])
    return level


def gaussian(stream_key, shape, deviation, reach, shards=(), held_as=jnp.bfloat16):
    values = jax.random.normal(stream_key, shape, jnp.float32) * deviation
    if len(shards) > 0:
        values = block_levels(stream_key, shape, shards, -0.22, 0.18) * values
    return jnp.clip(values, min=-reach, max=reach).astype(held_as)


def setup_inputs(seed: int = 0) -> dict:
    keys = jax.random.split(jax.random.key(seed), 14)
    tokens = gaussian(keys[0], (TOKENS, D), 1.0, 6.0, ((0, 32),))
    out_grad = gaussian(keys[1], (TOKENS, D), 1.0, 6.0, ((0, 32),))
    query_two = gaussian(keys[2], (TOKENS, H * HD), 1.0, 6.0, ((0, 4), (1, 8)))
    grad_two = gaussian(keys[3], (TOKENS, H * HD), 1.0, 6.0, ((0, 4), (1, 8)))
    doc_split = draw_doc_split(jax.random.fold_in(keys[13], 71), 0)
    attn_gain = jnp.clip(1.0 + 0.1 * jax.random.normal(keys[5], (D,), jnp.float32), 0.5, 1.5)
    mlp_gain = jnp.clip(1.0 + 0.1 * jax.random.normal(keys[6], (D,), jnp.float32), 0.5, 1.5)
    w_query = gaussian(keys[7], (D, H * HD), D ** -0.5, 0.125, ((1, 8),))
    w_kv = gaussian(keys[8], (D, 2 * HD), D ** -0.5, 0.125)
    w_out = gaussian(keys[9], (H * HD, D), (max(1, 16 * H * HD // SEQ_LONG)) ** -0.5, 1.5, ((0, 8),))
    w_gate = gaussian(keys[10], (D, FF), D ** -0.5, 0.125, ((1, 8),))
    w_up = gaussian(keys[11], (D, FF), D ** -0.5, 0.125, ((1, 8),))
    w_down = gaussian(keys[12], (FF, D), FF ** -0.5, 0.078125, ((0, 8),))
    return dict(tokens=tokens, out_grad=out_grad, query_two=query_two, grad_two=grad_two, doc_split=doc_split, attn_gain=attn_gain, mlp_gain=mlp_gain, w_query=w_query, w_kv=w_kv, w_out=w_out, w_gate=w_gate, w_up=w_up, w_down=w_down)


EPSILON = 1e-05
MASKED = -1e+30
HIGHEST = lax.Precision.HIGHEST

@jax.custom_vjp
def low(v):
    return lax.optimization_barrier(v.astype(jnp.bfloat16)).astype(jnp.float32)

@jax.custom_vjp
def low_back(v):
    return v

def low_keep(v):
    return (low(v), None)

def low_pass(kept, grad):
    return (grad,)

def back_keep(v):
    return (v, None)

def back_low(kept, grad):
    return (low(grad),)
low.defvjp(low_keep, low_pass)
low_back.defvjp(back_keep, back_low)

def matmul(left, right):
    return jnp.dot(left, right, precision=HIGHEST)

def rms_norm(values, gain):
    return values * lax.rsqrt(lax.optimization_barrier(jnp.mean(values * values, axis=-1, keepdims=True)) + EPSILON) * gain

def rotate(values, cosine, sine):
    middle = values.shape[-1] // 2
    leading = values[..., :middle]
    trailing = values[..., middle:]
    return jnp.concatenate([leading * cosine - trailing * sine, trailing * cosine + leading * sine], axis=-1)

def doc_mask(two_docs):
    position = jnp.arange(SEQ_LONG, dtype=jnp.int32)
    document = jnp.where(two_docs > 0, position // SEQ_SHORT, 0)
    return (position[:, None] >= position[None, :]) & (document[:, None] == document[None, :])

def phase_tables(two_docs):
    position = jnp.arange(SEQ_LONG, dtype=jnp.int32)
    in_sequence = jnp.where(two_docs > 0, position % SEQ_SHORT, position)
    frequency = 10000.0 ** (-jnp.arange(HD // 2, dtype=jnp.float32) * 2.0 / HD)
    phases = in_sequence.astype(jnp.float32)[:, None] * frequency[None, :]
    return (jnp.cos(phases), jnp.sin(phases))

def head_attention(query, key_rows, value_rows, allowed):
    scores = low_back(matmul(query, key_rows.T) * HD ** (-0.5))
    scores = jnp.where(allowed, scores, MASKED)
    row_max = lax.optimization_barrier(jnp.max(scores, axis=-1, keepdims=True))
    lifted = jnp.exp(scores - row_max)
    weights = low(lifted / lax.optimization_barrier(jnp.sum(lifted, axis=-1, keepdims=True)))
    return matmul(weights, value_rows)

def sequence_attention(queries, key_rows, value_rows, query_two, two_docs):
    allowed = doc_mask(two_docs)
    per_head = jax.checkpoint(lambda query: head_attention(query, key_rows, value_rows, allowed))
    context = lax.map(per_head, jnp.swapaxes(queries, 0, 1))
    output_two = lax.map(per_head, jnp.swapaxes(query_two, 0, 1))
    return (jnp.swapaxes(context, 0, 1), jnp.swapaxes(output_two, 0, 1))

def layer_forward(tokens, attn_gain, mlp_gain, w_query, w_kv, w_out, w_gate, w_up, w_down, query_two, doc_split):
    normed = low(rms_norm(tokens, attn_gain))
    query_lin = low_back(matmul(normed, w_query))
    kv_lin = low_back(matmul(normed, w_kv))
    cosine, sine = jax.vmap(phase_tables)(doc_split)
    cosine = cosine.reshape(TOKENS, HD // 2)
    sine = sine.reshape(TOKENS, HD // 2)
    queries = low(rotate(query_lin.reshape(TOKENS, H, HD), cosine[:, None, :], sine[:, None, :]))
    key_rows = low(rotate(kv_lin[:, :HD], cosine, sine))
    value_rows = low(kv_lin[:, HD:])
    groups = (queries.reshape(N_DP, SEQ_LONG, H, HD), key_rows.reshape(N_DP, SEQ_LONG, HD), value_rows.reshape(N_DP, SEQ_LONG, HD), query_two.reshape(N_DP, SEQ_LONG, H, HD), doc_split)
    context, output_two = lax.map(lambda group: sequence_attention(*group), groups)
    context = low(low_back(context.reshape(TOKENS, H * HD)))
    branch = low_back(matmul(context, w_out))
    hidden = tokens + branch
    hidden_normed = low(rms_norm(hidden, mlp_gain))
    gate = low_back(matmul(hidden_normed, w_gate))
    upward = low_back(matmul(hidden_normed, w_up))
    activated = low(jax.nn.silu(gate) * upward)
    mlp_out = low_back(matmul(activated, w_down))
    return (hidden + mlp_out, output_two.reshape(TOKENS, H * HD))

def reference(tokens, out_grad, query_two, grad_two, doc_split, attn_gain, mlp_gain, w_query, w_kv, w_out, w_gate, w_up, w_down):
    wide = jnp.float32
    primals = tuple((array.astype(wide) for array in (tokens, attn_gain, mlp_gain, w_query, w_kv, w_out, w_gate, w_up, w_down)))
    fixed_two = query_two.astype(wide)

    def forward(*params):
        return layer_forward(*params, fixed_two, doc_split)
    outputs, pullback = jax.vjp(forward, *primals)
    grads = pullback((out_grad.astype(wide), grad_two.astype(wide)))
    return (outputs[0].astype(jnp.bfloat16), grads[0].astype(jnp.bfloat16), grads[1], grads[2], grads[3], grads[4], grads[5], grads[6], grads[7], grads[8])
```

```python
import functools

import jax
import jax.numpy as jnp
from jax import lax
from jax.experimental import pallas as pl
from jax.experimental.pallas import tpu as pltpu
from jax.sharding import PartitionSpec as P

HD = 128
SEQ_SHORT = 1024
EPSILON = 1e-05
MASKED = -1e30
SCALE = HD ** (-0.5)
SCALE2 = SCALE * 1.4426950408889634
F32 = jnp.float32
BF16 = jnp.bfloat16
VMEM_LIMIT = 56 * 2**20


def mm(left, right, dims):
    return lax.dot_general(left, right, (dims, ((), ())), preferred_element_type=F32)


NN = ((1,), (0,))
NT = ((1,), (1,))
TN = ((0,), (0,))


class Links:
    def __init__(self, n_tensor, n_dp):
        self.n_tensor, self.n_dp = n_tensor, n_dp
        self.chips = n_tensor // 2
        odd = list(range(1, self.chips, 2))
        even = list(range(2, self.chips, 2))
        self.order = [0] + odd + even[::-1]
        nxt = {c: self.order[(i + 1) % self.chips] for i, c in enumerate(self.order)}
        self.place = [self.order.index(c) for c in range(self.chips)]
        self.ring_pairs = [(2 * c + k, 2 * nxt[c] + k) for c in range(self.chips) for k in (0, 1)]
        self.swap_pairs = [(i, i ^ 1) for i in range(n_tensor)]
        self.bits = [1 << b for b in range(n_dp.bit_length() - 1)]

    def ring(self, x):
        return lax.ppermute(x, "tensor", self.ring_pairs)

    def swap(self, x):
        return lax.ppermute(x, "tensor", self.swap_pairs)

    def across(self, x, bit):
        return lax.ppermute(x, "dp", [(i, i ^ bit) for i in range(self.n_dp)])

    def across_tensor(self, x, bit):
        return lax.ppermute(x, "tensor", [(i, i ^ bit) for i in range(self.n_tensor)])

    def orders(self, rows, unit):
        ways = len(self.bits)
        if ways < 2 or rows % (ways * unit):
            return [self.bits]
        return [self.bits[i:] + self.bits[:i] for i in range(ways)]


def take_rows(x, index, size):
    return lax.dynamic_slice_in_dim(x, index * size, size, 0)


def gather_dp(links, piece, me):
    orders = links.orders(piece.shape[0], 8)
    part_rows = piece.shape[0] // len(orders)
    parts = []
    for number, bits in enumerate(orders):
        stack = lax.slice_in_dim(piece, number * part_rows, (number + 1) * part_rows, axis=0)
        held = [0]
        for bit in bits:
            stack = jnp.concatenate([stack, links.across(stack, bit)], axis=0)
            held = held + [h ^ bit for h in held]
        where = jnp.array([held.index(rel) for rel in range(links.n_dp)], jnp.int32)
        parts.append((stack, where))
    out = []
    for j in range(links.n_dp):
        for stack, where in parts:
            out.append(take_rows(stack, where[me ^ j], part_rows))
    return jnp.concatenate(out, axis=0)


def gather_weight(links, block, me):
    rows = block.shape[0] // links.n_dp
    blocks = [block]
    piece = take_rows(block, me, rows)
    for _ in range(links.chips - 1):
        piece = links.ring(piece)
        blocks.append(gather_dp(links, piece, me))
    return blocks


def sum_dp(links, x, me):
    orders = links.orders(x.shape[0], 8 * links.n_dp)
    part_rows = x.shape[0] // len(orders)
    size = part_rows // links.n_dp
    outs = []
    for number, bits in enumerate(orders):
        held = lax.slice_in_dim(x, number * part_rows, (number + 1) * part_rows, axis=0)
        pieces = [held.reshape((links.n_dp, size) + x.shape[1:])]
        array = pieces[0]
        axes = [links.n_dp]
        nbits = len(links.bits)
        array = array.reshape((2,) * nbits + (size,) + x.shape[1:])
        left = list(reversed(links.bits))
        for bit in bits:
            axis = left.index(bit)
            mine = jnp.minimum(me & bit, 1)
            keep = lax.dynamic_index_in_dim(array, mine, axis, keepdims=False)
            send = lax.dynamic_index_in_dim(array, 1 - mine, axis, keepdims=False)
            got = links.across(send, bit)
            array = (keep.astype(F32) + got.astype(F32)).astype(BF16)
            left.remove(bit)
        stack = array.reshape((size,) + x.shape[1:])
        rel = [0]
        for bit in reversed(bits):
            stack = jnp.concatenate([stack, links.across(stack, bit)], axis=0)
            rel = rel + [r ^ bit for r in rel]
        where = jnp.array([rel.index(r) for r in range(links.n_dp)], jnp.int32)
        for j in range(links.n_dp):
            outs.append(take_rows(stack, where[me ^ j], size))
    return jnp.concatenate(outs, axis=0).astype(F32)


def ring_gather(links, own):
    out = [own]
    for _ in range(links.chips - 1):
        out.append(links.ring(out[-1]))
    return out


def ring_scatter(links, terms):
    got = None
    for term in terms[1:] + terms[:1]:
        total = term if got is None else term.astype(F32) + got.astype(F32)
        if term is terms[0]:
            return total.astype(F32)
        got = links.ring(total.astype(BF16))
    return got


def both(links, own):
    return jnp.concatenate([own, links.swap(own)], axis=0)


def pair_sum(links, part):
    rows = part.shape[0] // 2
    return part[:rows].astype(F32) + links.swap(part[rows:].astype(BF16)).astype(F32)


def sum_all(links, x):
    bit = 1
    while bit < links.n_tensor:
        x = x + links.across_tensor(x, bit)
        bit *= 2
    for bit in links.bits:
        x = x + links.across(x, bit)
    return x


def diagonal(shape, row_axis, shift):
    size = shape[row_axis]
    row = lax.broadcasted_iota(jnp.int32, shape, row_axis) + shift
    row = jnp.where(row >= size, row - size, row)
    return lax.broadcasted_iota(jnp.int32, shape, 1 - row_axis) <= row


def span(block, two_docs, rows):
    per_doc = SEQ_SHORT // rows
    inner = jnp.where(two_docs > 0, lax.rem(block, per_doc), block)
    return inner + 1, pl.multiple_of((block - inner) * rows, rows)


def fwd_kernel(blocks, sp_ref, q_ref, c_ref, s_ref, k_ref, v_ref, qo_ref, ctx_ref, lse_ref):
    rows = q_ref.shape[0]
    chip, two_docs, core = sp_ref[0], sp_ref[1], sp_ref[2]
    x = q_ref[...]
    q = (x * c_ref[...] + pltpu.roll(x, HD // 2, 1) * s_ref[...]).astype(BF16)
    qo_ref[...] = q
    count, low = span(chip, two_docs, rows)
    mask = diagonal((rows, rows), 0, core * (rows // 2))
    for n in range(1, blocks + 1):

        @pl.when(count == n)
        def _(n=n):
            near = (n - 1) * rows
            diag = pl.ds(low + near, rows)
            s_diag = jnp.where(mask, mm(q, k_ref[diag, :], NT) * SCALE2, MASKED)
            top = jnp.max(s_diag, axis=1, keepdims=True)
            if n > 1:
                main = pl.ds(low, near)
                s_main = mm(q, k_ref[main, :], NT) * SCALE2
                top = jnp.maximum(top, jnp.max(s_main, axis=1, keepdims=True))
            p_diag = jnp.exp2(s_diag - top)
            total = jnp.sum(p_diag, axis=1, keepdims=True)
            out = mm(p_diag.astype(BF16), v_ref[diag, :], NN)
            if n > 1:
                p_main = jnp.exp2(s_main - top)
                total = total + jnp.sum(p_main, axis=1, keepdims=True)
                out = out + mm(p_main.astype(BF16), v_ref[main, :], NN)
            ctx_ref[...] = (out / total).astype(BF16)
            lse = jnp.broadcast_to(top + jnp.log2(total), (rows, HD))
            lse_ref[0] = lse.T[:8]


def bwd_kernel(
    blocks, sp_ref, q_ref, do_ref, ctx_ref, lse_ref, c_ref, s_ref, k_ref, kt_ref, v_ref, dk0_ref, dv0_ref,
    dq_ref, dk_ref, dv_ref,
):
    rows = q_ref.shape[0]
    chip, two_docs, core = sp_ref[0], sp_ref[1], sp_ref[2]

    @pl.when(pl.program_id(0) == 0)
    def _():
        dk_ref[...] = dk0_ref[...]
        dv_ref[...] = dv0_ref[...]

    q, do = q_ref[...], do_ref[...]
    dot = jnp.sum(do.astype(F32) * ctx_ref[...].astype(F32), axis=1, keepdims=True)
    dot = jnp.broadcast_to(dot, (rows, HD)).T[:1]
    lse = lse_ref[0, :1]
    count, low = span(chip, two_docs, rows)
    mask = diagonal((rows, rows), 1, core * (rows // 2))
    for n in range(1, blocks + 1):

        @pl.when(count == n)
        def _(n=n):
            near = (n - 1) * rows
            dqt = jnp.zeros((HD, rows), F32)
            for keys, masked in ((pl.ds(low, near), False), (pl.ds(low + near, rows), True)):
                if not masked and n == 1:
                    continue
                p = jnp.exp2(mm(k_ref[keys, :], q, NT) * SCALE2 - lse)
                if masked:
                    p = jnp.where(mask, p, 0.0)
                ds = (p * (mm(v_ref[keys, :], do, NT) - dot)).astype(BF16)
                dv_ref[keys, :] += mm(p.astype(BF16), do, NN)
                dk_ref[keys, :] += mm(ds, q, NN)
                dqt = dqt + mm(kt_ref[:, keys], ds, NN)
            g = dqt.T * SCALE
            dq_ref[...] = (g * c_ref[...] - pltpu.roll(g, HD // 2, 1) * s_ref[...]).astype(BF16)


def second_kernel(blocks, sp_ref, q_ref, do_ref, k_ref, v_ref, dk_ref, dv_ref):
    rows = q_ref.shape[0]
    block, two_docs = pl.program_id(0), sp_ref[1]

    @pl.when((block == 0) & (pl.program_id(1) == 0))
    def _():
        dk_ref[...] = jnp.zeros_like(dk_ref)
        dv_ref[...] = jnp.zeros_like(dv_ref)

    q, do = q_ref[...], do_ref[...]
    count, low = span(block, two_docs, rows)
    mask = diagonal((rows, rows), 1, 0)
    for n in range(1, blocks + 1):

        @pl.when(count == n)
        def _(n=n):
            near = (n - 1) * rows
            parts = [pl.ds(low + near, rows)] + ([pl.ds(low, near)] if n > 1 else [])
            scores = [mm(k_ref[keys, :], q, NT) * SCALE2 for keys in parts]
            scores[0] = jnp.where(mask, scores[0], MASKED)
            top = functools.reduce(jnp.maximum, [jnp.max(s, axis=0, keepdims=True) for s in scores])
            lifted = [jnp.exp2(s - top) for s in scores]
            total = sum(jnp.sum(p, axis=0, keepdims=True) for p in lifted)
            inverse = 1.0 / total
            back = [mm(v_ref[keys, :], do, NT) for keys in parts]
            dot = sum(jnp.sum(p * b, axis=0, keepdims=True) for p, b in zip(lifted, back)) * inverse
            for keys, p, b in zip(parts, lifted, back):
                p = p * inverse
                dv_ref[keys, :] += mm(p.astype(BF16), do, NN)
                dk_ref[keys, :] += mm((p * (b - dot)).astype(BF16), q, NN)


def whole(shape):
    return pl.BlockSpec(shape, lambda *_: (0,) * len(shape))


def attend(sp, q_lin, cosine, sine, key_rows, value_rows):
    rows, width = q_lin.shape
    seq = key_rows.shape[0]
    heads = width // HD
    column = pl.BlockSpec((rows, HD), lambda h, *_: (0, h))
    return pl.pallas_call(
        functools.partial(fwd_kernel, seq // rows),
        grid_spec=pltpu.PrefetchScalarGridSpec(
            num_scalar_prefetch=1,
            grid=(heads,),
            in_specs=[column, whole((rows, HD)), whole((rows, HD)), whole((seq, HD)), whole((seq, HD))],
            out_specs=[column, column, pl.BlockSpec((1, 8, rows), lambda h, *_: (h, 0, 0))],
        ),
        out_shape=[
            jax.ShapeDtypeStruct((rows, width), BF16),
            jax.ShapeDtypeStruct((rows, width), BF16),
            jax.ShapeDtypeStruct((heads, 8, rows), F32),
        ],
        compiler_params=pltpu.CompilerParams(vmem_limit_bytes=VMEM_LIMIT),
        cost_estimate=pl.CostEstimate(
            flops=8 * heads * rows * seq * HD, bytes_accessed=16 * rows * width, transcendentals=heads * rows * seq
        ),
        name="attend",
    )(sp, q_lin, cosine, sine, key_rows, value_rows)


def attend_back(sp, queries, grad_context, context, lse, cosine, sine, key_rows, value_rows, dk0, dv0):
    rows, width = queries.shape
    seq = key_rows.shape[0]
    heads = width // HD
    column = pl.BlockSpec((rows, HD), lambda h, *_: (0, h))
    return pl.pallas_call(
        functools.partial(bwd_kernel, seq // rows),
        grid_spec=pltpu.PrefetchScalarGridSpec(
            num_scalar_prefetch=1,
            grid=(heads,),
            in_specs=[
                column, column, column, pl.BlockSpec((1, 8, rows), lambda h, *_: (h, 0, 0)),
                whole((rows, HD)), whole((rows, HD)), whole((seq, HD)), whole((HD, seq)), whole((seq, HD)),
                whole((seq, HD)), whole((seq, HD)),
            ],
            out_specs=[column, whole((seq, HD)), whole((seq, HD))],
        ),
        out_shape=[
            jax.ShapeDtypeStruct((rows, width), BF16),
            jax.ShapeDtypeStruct((seq, HD), F32),
            jax.ShapeDtypeStruct((seq, HD), F32),
        ],
        compiler_params=pltpu.CompilerParams(vmem_limit_bytes=VMEM_LIMIT),
        cost_estimate=pl.CostEstimate(
            flops=20 * heads * rows * seq * HD, bytes_accessed=16 * rows * width, transcendentals=heads * rows * seq
        ),
        name="attend_back",
    )(sp, queries, grad_context, context, lse, cosine, sine, key_rows, key_rows.T, value_rows, dk0, dv0)


def second_back(sp, query_two, grad_two, key_rows, value_rows):
    seq, width = query_two.shape
    rows = min(512, SEQ_SHORT)
    heads = width // HD
    column = pl.BlockSpec((rows, HD), lambda i, h, *_: (i, h))
    return pl.pallas_call(
        functools.partial(second_kernel, seq // rows),
        grid_spec=pltpu.PrefetchScalarGridSpec(
            num_scalar_prefetch=1,
            grid=(seq // rows, heads),
            in_specs=[column, column, whole((seq, HD)), whole((seq, HD))],
            out_specs=[whole((seq, HD)), whole((seq, HD))],
        ),
        out_shape=[jax.ShapeDtypeStruct((seq, HD), F32), jax.ShapeDtypeStruct((seq, HD), F32)],
        compiler_params=pltpu.CompilerParams(vmem_limit_bytes=VMEM_LIMIT),
        cost_estimate=pl.CostEstimate(
            flops=8 * heads * seq * seq * HD, bytes_accessed=4 * seq * width, transcendentals=heads * seq * seq // 2
        ),
        name="second_back",
    )(sp, query_two, grad_two, key_rows, value_rows)


def rms_factor(values):
    return lax.rsqrt(jnp.mean(values * values, axis=-1, keepdims=True) + EPSILON)


def local(
    n_tensor, n_dp,
    tokens, out_grad, query_two, grad_two, doc_split, attn_gain, mlp_gain, w_query, w_kv, w_out, w_gate, w_up, w_down,
):
    links = Links(n_tensor, n_dp)
    chips = links.chips
    own = tokens.shape[0]
    rows = 2 * own
    seq = own * n_tensor
    width = w_query.shape[1]
    me_dp = lax.axis_index("dp")
    me_t = lax.axis_index("tensor")
    chip, core = me_t // 2, me_t % 2
    two_docs = doc_split[0]
    sp = jnp.stack([chip, two_docs, core]).astype(jnp.int32)
    place = jnp.array(links.place, jnp.int32)
    order = jnp.array(links.order, jnp.int32)

    spot = jnp.arange(rows, dtype=jnp.int32) + core * own
    spot = chip * rows + jnp.where(spot >= rows, spot - rows, spot)
    position = jnp.where(two_docs > 0, spot % SEQ_SHORT, spot)
    frequency = 10000.0 ** (-jnp.arange(HD // 2, dtype=F32) * 2.0 / HD)
    phases = position.astype(F32)[:, None] * frequency[None, :]
    cos, sin = jnp.cos(phases), jnp.sin(phases)
    cosine = jnp.concatenate([cos, cos], axis=1)
    sine = jnp.concatenate([-sin, sin], axis=1)

    residual = tokens.astype(F32)
    attn_scale = rms_factor(residual)
    attn_pre = residual * attn_scale
    normed_own = (attn_pre * attn_gain).astype(BF16)

    kv_lin = mm(normed_own, w_kv, NN)
    half = HD // 2
    key_lin = kv_lin[:, :HD]
    key_own = key_lin * cosine[:own] + jnp.concatenate([key_lin[:, half:], key_lin[:, :half]], axis=1) * sine[:own]
    kv_own = jnp.concatenate([key_own, kv_lin[:, HD:]], axis=1).astype(BF16)
    kv_mine = jnp.stack(ring_gather(links, kv_own))
    kv_other = links.swap(kv_mine)
    kv_first = jnp.where(core == 0, kv_mine, kv_other)
    kv_second = jnp.where(core == 0, kv_other, kv_mine)
    kv_rel = jnp.concatenate([kv_first, kv_second], axis=1)
    kv_all = jnp.concatenate(
        [
            lax.dynamic_index_in_dim(kv_rel, (place[chip] - links.place[j] + chips) % chips, 0, keepdims=False)
            for j in range(chips)
        ],
        axis=0,
    )
    key_rows, value_rows = kv_all[:, :HD], kv_all[:, HD:]

    wq_blocks = gather_weight(links, w_query, me_dp)
    wo_blocks = gather_weight(links, w_out, me_dp)
    wq = jnp.concatenate(wq_blocks, axis=1)
    wo = jnp.concatenate(wo_blocks, axis=0)
    grad_chunks = [both(links, piece) for piece in ring_gather(links, out_grad)]

    dk2, dv2 = second_back(sp, query_two, grad_two, key_rows, value_rows)

    normed = both(links, normed_own)
    q_lin = mm(normed, wq, NN)
    queries, context, lse = attend(sp, q_lin, cosine, sine, key_rows, value_rows)
    branch = pair_sum(links, mm(context, wo, NN))
    hidden = residual + branch
    mlp_scale = rms_factor(hidden)
    mlp_pre = hidden * mlp_scale
    hidden_own = (mlp_pre * mlp_gain).astype(BF16)

    hidden_chunks, act_chunks, gate_chunks, up_chunks = [], [], [], []
    mlp_parts, back_parts = [], []
    for piece, grad in zip(ring_gather(links, hidden_own), grad_chunks):
        chunk = both(links, piece)
        gate = mm(chunk, w_gate, NN)
        upward = mm(chunk, w_up, NN)
        grad_act = mm(grad, w_down, NT)
        sigma = jax.nn.sigmoid(gate)
        swish = gate * sigma
        activated = (swish * upward).astype(BF16)
        grad_gate = (grad_act * upward * sigma * (1.0 + gate * (1.0 - sigma))).astype(BF16)
        grad_up = (grad_act * swish).astype(BF16)
        back_parts.append((mm(grad_gate, w_gate, NT) + mm(grad_up, w_up, NT)).astype(BF16))
        mlp_parts.append(mm(activated, w_down, NN).astype(BF16))
        hidden_chunks.append(chunk)
        act_chunks.append(activated)
        gate_chunks.append(grad_gate)
        up_chunks.append(grad_up)

    grad_hn = ring_scatter(links, [pair_sum(links, part) for part in back_parts])
    mlp_out = ring_scatter(links, [pair_sum(links, part) for part in mlp_parts])
    block_output = (hidden + mlp_out).astype(BF16)

    hidden_all = jnp.concatenate(hidden_chunks, axis=0)
    act_all = jnp.concatenate(act_chunks, axis=0)
    gate_all = jnp.concatenate(gate_chunks, axis=0)
    up_all = jnp.concatenate(up_chunks, axis=0)
    grad_all = jnp.concatenate(grad_chunks, axis=0)
    gate_w_grad = sum_dp(links, mm(gate_all, hidden_all, TN).astype(BF16), me_dp).T
    up_w_grad = sum_dp(links, mm(up_all, hidden_all, TN).astype(BF16), me_dp).T
    down_w_grad = sum_dp(links, mm(act_all, grad_all, TN).astype(BF16), me_dp)

    mlp_gain_part = jnp.sum(grad_hn * mlp_pre, axis=0)
    scaled_mlp = grad_hn * mlp_gain
    grad_hidden = out_grad.astype(F32) + mlp_scale * (
        scaled_mlp - mlp_pre * jnp.mean(scaled_mlp * mlp_pre, axis=-1, keepdims=True)
    )

    grad_branch = both(links, grad_hidden.astype(BF16))
    grad_context = mm(grad_branch, wo, NT).astype(BF16)
    query_grad, dk, dv = attend_back(
        sp, queries, grad_context, context, lse, cosine, sine, key_rows, value_rows, dk2, dv2
    )
    out_w_parts = [
        mm(context[:, k * width : (k + 1) * width], grad_branch, TN).astype(BF16) for k in range(chips)
    ]
    out_w_grad = sum_dp(links, ring_scatter(links, out_w_parts).astype(BF16), me_dp)

    kv_part = jnp.concatenate([dk * SCALE, dv], axis=1).astype(BF16).reshape(chips, 2, own, 2 * HD)
    kv_keep = lax.dynamic_index_in_dim(kv_part, core, 1, keepdims=False)
    kv_send = lax.dynamic_index_in_dim(kv_part, 1 - core, 1, keepdims=False)
    kv_sum = kv_keep.astype(F32) + links.swap(kv_send).astype(F32)
    kv_terms = [
        lax.dynamic_index_in_dim(kv_sum, order[(place[chip] - k + chips) % chips], 0, keepdims=False)
        for k in range(chips)
    ]
    kv_grad = ring_scatter(links, kv_terms)
    key_grad = kv_grad[:, :HD]
    key_grad = key_grad * cosine[:own] - jnp.concatenate([key_grad[:, half:], key_grad[:, :half]], axis=1) * sine[:own]
    kv_grad_lin = jnp.concatenate([key_grad, kv_grad[:, HD:]], axis=1).astype(BF16)

    query_w_parts = [
        mm(normed, query_grad[:, k * width : (k + 1) * width], TN).astype(BF16) for k in range(chips)
    ]
    query_w_grad = sum_dp(links, ring_scatter(links, query_w_parts).astype(BF16), me_dp)

    grad_normed = pair_sum(links, mm(query_grad, wq, NT)) + mm(kv_grad_lin, w_kv, NT)
    attn_gain_part = jnp.sum(grad_normed * attn_pre, axis=0)
    scaled_attn = grad_normed * attn_gain
    tokens_grad = (
        grad_hidden
        + attn_scale * (scaled_attn - attn_pre * jnp.mean(scaled_attn * attn_pre, axis=-1, keepdims=True))
    ).astype(BF16)

    kv_w = mm(kv_grad_lin, normed_own, TN).astype(BF16).reshape(chips, 2, HD // chips, -1)
    kv_w_keep = lax.dynamic_index_in_dim(kv_w, core, 1, keepdims=False)
    kv_w_send = lax.dynamic_index_in_dim(kv_w, 1 - core, 1, keepdims=False)
    kv_w_sum = kv_w_keep.astype(F32) + links.swap(kv_w_send).astype(F32)
    kv_w_terms = [
        lax.dynamic_index_in_dim(kv_w_sum, order[(place[chip] - k + chips) % chips], 0, keepdims=False)
        for k in range(chips)
    ]
    kv_w_own = sum_dp(links, ring_scatter(links, kv_w_terms).astype(BF16), me_dp)
    kv_w_mine = jnp.stack(ring_gather(links, kv_w_own.astype(BF16)))
    kv_w_other = links.swap(kv_w_mine)
    kv_w_pair = jnp.stack(
        [jnp.where(core == 0, kv_w_mine, kv_w_other), jnp.where(core == 0, kv_w_other, kv_w_mine)], axis=1
    )
    kv_w_grad = (
        jnp.concatenate(
            [
                lax.dynamic_index_in_dim(kv_w_pair, (place[chip] - links.place[j] + chips) % chips, 0, keepdims=False)
                for j in range(chips)
            ],
            axis=0,
        )
        .reshape(2 * HD, -1)
        .astype(F32)
        .T
    )

    attn_gain_grad = sum_all(links, attn_gain_part)
    mlp_gain_grad = sum_all(links, mlp_gain_part)
    return (
        block_output,
        tokens_grad,
        attn_gain_grad,
        mlp_gain_grad,
        query_w_grad,
        kv_w_grad,
        out_w_grad,
        gate_w_grad,
        up_w_grad,
        down_w_grad,
    )


def solution(mesh):
    both_axes = P(("dp", "tensor"), None)
    return jax.shard_map(
        functools.partial(local, mesh.shape["tensor"], mesh.shape["dp"]),
        mesh=mesh,
        in_specs=(
            both_axes,
            both_axes,
            P("dp", "tensor"),
            P("dp", "tensor"),
            P("dp"),
            P(),
            P(),
            P(None, "tensor"),
            P(),
            P("tensor", None),
            P(None, "tensor"),
            P(None, "tensor"),
            P("tensor", None),
        ),
        out_specs=(
            both_axes,
            both_axes,
            P(),
            P(),
            P(None, "tensor"),
            P(),
            P("tensor", None),
            P(None, "tensor"),
            P(None, "tensor"),
            P("tensor", None),
        ),
        check_vma=False,
    )
```

```python
import functools

import jax
import jax.numpy as jnp
from jax import lax
from jax.experimental import pallas as pl
from jax.experimental.pallas import tpu as pltpu
from jax.sharding import PartitionSpec as P

HD = 128
SEQ_SHORT = 1024
EPSILON = 1e-05
MASKED = -1e30
SCALE = HD ** (-0.5)
SCALE2 = SCALE * 1.4426950408889634
F32 = jnp.float32
BF16 = jnp.bfloat16
VMEM_LIMIT = 56 * 2**20


def mm(left, right, dims):
    return lax.dot_general(left, right, (dims, ((), ())), preferred_element_type=F32)


NN = ((1,), (0,))
NT = ((1,), (1,))
TN = ((0,), (0,))


class Links:
    def __init__(self, n_tensor, n_dp):
        self.n_tensor, self.n_dp = n_tensor, n_dp
        self.chips = n_tensor // 2
        odd = list(range(1, self.chips, 2))
        even = list(range(2, self.chips, 2))
        self.order = [0] + odd + even[::-1]
        nxt = {c: self.order[(i + 1) % self.chips] for i, c in enumerate(self.order)}
        self.place = [self.order.index(c) for c in range(self.chips)]
        self.ring_pairs = [(2 * c + k, 2 * nxt[c] + k) for c in range(self.chips) for k in (0, 1)]
        self.swap_pairs = [(i, i ^ 1) for i in range(n_tensor)]
        self.bits = [1 << b for b in range(n_dp.bit_length() - 1)]

    def ring(self, x):
        return lax.ppermute(x, "tensor", self.ring_pairs)

    def swap(self, x):
        return lax.ppermute(x, "tensor", self.swap_pairs)

    def across(self, x, bit):
        return lax.ppermute(x, "dp", [(i, i ^ bit) for i in range(self.n_dp)])

    def across_tensor(self, x, bit):
        return lax.ppermute(x, "tensor", [(i, i ^ bit) for i in range(self.n_tensor)])

    def neighbours(self, chip):
        ahead, behind = chip * 0, chip * 0
        for i, c in enumerate(self.order):
            ahead = jnp.where(chip == c, self.order[(i + 1) % self.chips], ahead)
            behind = jnp.where(chip == c, self.order[i - 1], behind)
        return ahead, behind

    def orders(self, rows, unit):
        ways = len(self.bits)
        if ways < 2 or rows % (ways * unit):
            return [self.bits]
        return [self.bits[i:] + self.bits[:i] for i in range(ways)]


def take_rows(x, index, size):
    return lax.dynamic_slice_in_dim(x, index * size, size, 0)


def gather_dp(links, piece, me):
    orders = links.orders(piece.shape[0], 8)
    part_rows = piece.shape[0] // len(orders)
    parts = []
    for number, bits in enumerate(orders):
        stack = lax.slice_in_dim(piece, number * part_rows, (number + 1) * part_rows, axis=0)
        held = [0]
        for bit in bits:
            stack = jnp.concatenate([stack, links.across(stack, bit)], axis=0)
            held = held + [h ^ bit for h in held]
        where = jnp.array([held.index(rel) for rel in range(links.n_dp)], jnp.int32)
        parts.append((stack, where))
    out = []
    for j in range(links.n_dp):
        for stack, where in parts:
            out.append(take_rows(stack, where[me ^ j], part_rows))
    return jnp.concatenate(out, axis=0)


def gather_weight(links, block, me):
    rows = block.shape[0] // links.n_dp
    blocks = [block]
    piece = take_rows(block, me, rows)
    for _ in range(links.chips - 1):
        piece = links.ring(piece)
        blocks.append(gather_dp(links, piece, me))
    return blocks


def sum_dp(links, x, me):
    orders = links.orders(x.shape[0], 8 * links.n_dp)
    part_rows = x.shape[0] // len(orders)
    size = part_rows // links.n_dp
    outs = []
    for number, bits in enumerate(orders):
        held = lax.slice_in_dim(x, number * part_rows, (number + 1) * part_rows, axis=0)
        pieces = [held.reshape((links.n_dp, size) + x.shape[1:])]
        array = pieces[0]
        axes = [links.n_dp]
        nbits = len(links.bits)
        array = array.reshape((2,) * nbits + (size,) + x.shape[1:])
        left = list(reversed(links.bits))
        for bit in bits:
            axis = left.index(bit)
            mine = jnp.minimum(me & bit, 1)
            keep = lax.dynamic_index_in_dim(array, mine, axis, keepdims=False)
            send = lax.dynamic_index_in_dim(array, 1 - mine, axis, keepdims=False)
            got = links.across(send, bit)
            array = (keep.astype(F32) + got.astype(F32)).astype(BF16)
            left.remove(bit)
        stack = array.reshape((size,) + x.shape[1:])
        rel = [0]
        for bit in reversed(bits):
            stack = jnp.concatenate([stack, links.across(stack, bit)], axis=0)
            rel = rel + [r ^ bit for r in rel]
        where = jnp.array([rel.index(r) for r in range(links.n_dp)], jnp.int32)
        for j in range(links.n_dp):
            outs.append(take_rows(stack, where[me ^ j], size))
    return jnp.concatenate(outs, axis=0).astype(F32)


def ring_gather(links, own):
    out = [own]
    for _ in range(links.chips - 1):
        out.append(links.ring(out[-1]))
    return out


def ring_scatter(links, terms):
    got = None
    for term in terms[1:] + terms[:1]:
        total = term if got is None else term.astype(F32) + got.astype(F32)
        if term is terms[0]:
            return total.astype(F32)
        got = links.ring(total.astype(BF16))
    return got


def both(links, own):
    return jnp.concatenate([own, links.swap(own)], axis=0)


def pair_sum(links, part):
    rows = part.shape[0] // 2
    return part[:rows].astype(F32) + links.swap(part[rows:].astype(BF16)).astype(F32)


def sum_all(links, x):
    bit = 1
    while bit < links.n_tensor:
        x = x + links.across_tensor(x, bit)
        bit *= 2
    for bit in links.bits:
        x = x + links.across(x, bit)
    return x


def diagonal(shape, row_axis, shift):
    size = shape[row_axis]
    row = lax.broadcasted_iota(jnp.int32, shape, row_axis) + shift
    row = jnp.where(row >= size, row - size, row)
    return lax.broadcasted_iota(jnp.int32, shape, 1 - row_axis) <= row


def span(block, two_docs, rows):
    per_doc = SEQ_SHORT // rows
    inner = jnp.where(two_docs > 0, lax.rem(block, per_doc), block)
    return inner + 1, pl.multiple_of((block - inner) * rows, rows)


def fwd_kernel(blocks, sp_ref, q_ref, c_ref, s_ref, k_ref, v_ref, qo_ref, ctx_ref, lse_ref):
    rows = q_ref.shape[0]
    chip, two_docs, core = sp_ref[0], sp_ref[1], sp_ref[2]
    x = q_ref[...]
    q = (x * c_ref[...] + pltpu.roll(x, HD // 2, 1) * s_ref[...]).astype(BF16)
    qo_ref[...] = q
    count, low = span(chip, two_docs, rows)
    mask = diagonal((rows, rows), 0, core * (rows // 2))
    for n in range(1, blocks + 1):

        @pl.when(count == n)
        def _(n=n):
            near = (n - 1) * rows
            diag = pl.ds(low + near, rows)
            s_diag = jnp.where(mask, mm(q, k_ref[diag, :], NT) * SCALE2, MASKED)
            top = jnp.max(s_diag, axis=1, keepdims=True)
            if n > 1:
                main = pl.ds(low, near)
                s_main = mm(q, k_ref[main, :], NT) * SCALE2
                top = jnp.maximum(top, jnp.max(s_main, axis=1, keepdims=True))
            p_diag = jnp.exp2(s_diag - top)
            total = jnp.sum(p_diag, axis=1, keepdims=True)
            out = mm(p_diag.astype(BF16), v_ref[diag, :], NN)
            if n > 1:
                p_main = jnp.exp2(s_main - top)
                total = total + jnp.sum(p_main, axis=1, keepdims=True)
                out = out + mm(p_main.astype(BF16), v_ref[main, :], NN)
            ctx_ref[...] = (out / total).astype(BF16)
            lse = jnp.broadcast_to(top + jnp.log2(total), (rows, HD))
            lse_ref[0] = lse.T[:8]


def bwd_kernel(
    blocks, sp_ref, q_ref, do_ref, ctx_ref, lse_ref, c_ref, s_ref, k_ref, kt_ref, v_ref, dk0_ref, dv0_ref,
    dq_ref, dk_ref, dv_ref,
):
    rows = q_ref.shape[0]
    chip, two_docs, core = sp_ref[0], sp_ref[1], sp_ref[2]

    @pl.when(pl.program_id(0) == 0)
    def _():
        dk_ref[...] = dk0_ref[...]
        dv_ref[...] = dv0_ref[...]

    q, do = q_ref[...], do_ref[...]
    dot = jnp.sum(do.astype(F32) * ctx_ref[...].astype(F32), axis=1, keepdims=True)
    dot = jnp.broadcast_to(dot, (rows, HD)).T[:1]
    lse = lse_ref[0, :1]
    count, low = span(chip, two_docs, rows)
    mask = diagonal((rows, rows), 1, core * (rows // 2))
    for n in range(1, blocks + 1):

        @pl.when(count == n)
        def _(n=n):
            near = (n - 1) * rows
            dqt = jnp.zeros((HD, rows), F32)
            for keys, masked in ((pl.ds(low, near), False), (pl.ds(low + near, rows), True)):
                if not masked and n == 1:
                    continue
                p = jnp.exp2(mm(k_ref[keys, :], q, NT) * SCALE2 - lse)
                if masked:
                    p = jnp.where(mask, p, 0.0)
                ds = (p * (mm(v_ref[keys, :], do, NT) - dot)).astype(BF16)
                dv_ref[keys, :] += mm(p.astype(BF16), do, NN)
                dk_ref[keys, :] += mm(ds, q, NN)
                dqt = dqt + mm(kt_ref[:, keys], ds, NN)
            g = dqt.T * SCALE
            dq_ref[...] = (g * c_ref[...] - pltpu.roll(g, HD // 2, 1) * s_ref[...]).astype(BF16)


def second_kernel(blocks, sp_ref, q_ref, do_ref, k_ref, v_ref, dk_ref, dv_ref):
    rows = q_ref.shape[0]
    block, two_docs = pl.program_id(0), sp_ref[1]

    @pl.when((block == 0) & (pl.program_id(1) == 0))
    def _():
        dk_ref[...] = jnp.zeros_like(dk_ref)
        dv_ref[...] = jnp.zeros_like(dv_ref)

    q, do = q_ref[...], do_ref[...]
    count, low = span(block, two_docs, rows)
    mask = diagonal((rows, rows), 1, 0)
    for n in range(1, blocks + 1):

        @pl.when(count == n)
        def _(n=n):
            near = (n - 1) * rows
            parts = [pl.ds(low + near, rows)] + ([pl.ds(low, near)] if n > 1 else [])
            scores = [mm(k_ref[keys, :], q, NT) * SCALE2 for keys in parts]
            scores[0] = jnp.where(mask, scores[0], MASKED)
            top = functools.reduce(jnp.maximum, [jnp.max(s, axis=0, keepdims=True) for s in scores])
            lifted = [jnp.exp2(s - top) for s in scores]
            total = sum(jnp.sum(p, axis=0, keepdims=True) for p in lifted)
            inverse = 1.0 / total
            back = [mm(v_ref[keys, :], do, NT) for keys in parts]
            dot = sum(jnp.sum(p * b, axis=0, keepdims=True) for p, b in zip(lifted, back)) * inverse
            for keys, p, b in zip(parts, lifted, back):
                p = p * inverse
                dv_ref[keys, :] += mm(p.astype(BF16), do, NN)
                dk_ref[keys, :] += mm((p * (b - dot)).astype(BF16), q, NN)


def whole(shape):
    return pl.BlockSpec(shape, lambda *_: (0,) * len(shape))


def attend(sp, q_lin, cosine, sine, key_rows, value_rows):
    rows, width = q_lin.shape
    seq = key_rows.shape[0]
    heads = width // HD
    column = pl.BlockSpec((rows, HD), lambda h, *_: (0, h))
    return pl.pallas_call(
        functools.partial(fwd_kernel, seq // rows),
        grid_spec=pltpu.PrefetchScalarGridSpec(
            num_scalar_prefetch=1,
            grid=(heads,),
            in_specs=[column, whole((rows, HD)), whole((rows, HD)), whole((seq, HD)), whole((seq, HD))],
            out_specs=[column, column, pl.BlockSpec((1, 8, rows), lambda h, *_: (h, 0, 0))],
        ),
        out_shape=[
            jax.ShapeDtypeStruct((rows, width), BF16),
            jax.ShapeDtypeStruct((rows, width), BF16),
            jax.ShapeDtypeStruct((heads, 8, rows), F32),
        ],
        compiler_params=pltpu.CompilerParams(vmem_limit_bytes=VMEM_LIMIT),
        cost_estimate=pl.CostEstimate(
            flops=8 * heads * rows * seq * HD, bytes_accessed=16 * rows * width, transcendentals=heads * rows * seq
        ),
        name="attend",
    )(sp, q_lin, cosine, sine, key_rows, value_rows)


def attend_back(sp, queries, grad_context, context, lse, cosine, sine, key_rows, value_rows, dk0, dv0):
    rows, width = queries.shape
    seq = key_rows.shape[0]
    heads = width // HD
    column = pl.BlockSpec((rows, HD), lambda h, *_: (0, h))
    return pl.pallas_call(
        functools.partial(bwd_kernel, seq // rows),
        grid_spec=pltpu.PrefetchScalarGridSpec(
            num_scalar_prefetch=1,
            grid=(heads,),
            in_specs=[
                column, column, column, pl.BlockSpec((1, 8, rows), lambda h, *_: (h, 0, 0)),
                whole((rows, HD)), whole((rows, HD)), whole((seq, HD)), whole((HD, seq)), whole((seq, HD)),
                whole((seq, HD)), whole((seq, HD)),
            ],
            out_specs=[column, whole((seq, HD)), whole((seq, HD))],
        ),
        out_shape=[
            jax.ShapeDtypeStruct((rows, width), BF16),
            jax.ShapeDtypeStruct((seq, HD), F32),
            jax.ShapeDtypeStruct((seq, HD), F32),
        ],
        compiler_params=pltpu.CompilerParams(vmem_limit_bytes=VMEM_LIMIT),
        cost_estimate=pl.CostEstimate(
            flops=20 * heads * rows * seq * HD, bytes_accessed=16 * rows * width, transcendentals=heads * rows * seq
        ),
        name="attend_back",
    )(sp, queries, grad_context, context, lse, cosine, sine, key_rows, key_rows.T, value_rows, dk0, dv0)


def second_back(sp, query_two, grad_two, key_rows, value_rows):
    seq, width = query_two.shape
    rows = min(512, SEQ_SHORT)
    heads = width // HD
    column = pl.BlockSpec((rows, HD), lambda i, h, *_: (i, h))
    return pl.pallas_call(
        functools.partial(second_kernel, seq // rows),
        grid_spec=pltpu.PrefetchScalarGridSpec(
            num_scalar_prefetch=1,
            grid=(seq // rows, heads),
            in_specs=[column, column, whole((seq, HD)), whole((seq, HD))],
            out_specs=[whole((seq, HD)), whole((seq, HD))],
        ),
        out_shape=[jax.ShapeDtypeStruct((seq, HD), F32), jax.ShapeDtypeStruct((seq, HD), F32)],
        compiler_params=pltpu.CompilerParams(vmem_limit_bytes=VMEM_LIMIT),
        cost_estimate=pl.CostEstimate(
            flops=8 * heads * seq * seq * HD, bytes_accessed=4 * seq * width, transcendentals=heads * seq * seq // 2
        ),
        name="second_back",
    )(sp, query_two, grad_two, key_rows, value_rows)


def mlp_kernel(
    links, h_hbm, g_hbm, wg_hbm, wu_hbm, wd_hbm, ghn_ref, mlp_hbm, gw_hbm, uw_hbm, dw_hbm,
    h_all, g_all, wg, wu, wd, act_t, gg_t, gu_t, keep, stage, pair_out, pair_in, ring_out, ring_in,
    load_sem, ring_s, ring_r, swap_s, swap_r, pair_s, pair_r, rs_s, rs_r, stage_sem, store_sem,
):
    chips = links.chips
    own, depth = h_hbm.shape
    seq = chips * 2 * own
    me = lax.axis_index("tensor")
    chip, core = me // 2, lax.rem(me, 2)
    ahead, behind = links.neighbours(chip)
    right = {"tensor": ahead * 2 + core}
    left = {"tensor": behind * 2 + core}
    sibling = {"tensor": chip * 2 + 1 - core}

    loads = [
        pltpu.make_async_copy(h_hbm, h_all.at[0, 0], load_sem.at[0]),
        pltpu.make_async_copy(wg_hbm, wg, load_sem.at[1]),
        pltpu.make_async_copy(wu_hbm, wu, load_sem.at[2]),
        pltpu.make_async_copy(wd_hbm, wd, load_sem.at[3]),
        pltpu.make_async_copy(g_hbm, g_all, load_sem.at[4]),
    ]
    for load in loads:
        load.start()
    barrier = pltpu.get_barrier_semaphore()
    for peer in (right, left, sibling):
        pl.semaphore_signal(barrier, inc=1, device_id=peer, device_id_type=pl.DeviceIdType.MESH)
    pl.semaphore_wait(barrier, 3)

    def remote(src, dst, send, recv, peer):
        return pltpu.make_async_remote_copy(
            src_ref=src, dst_ref=dst, send_sem=send, recv_sem=recv, device_id=peer,
            device_id_type=pl.DeviceIdType.MESH,
        )

    def ring(k):
        return remote(h_all.at[k, 0], h_all.at[k + 1, 0], ring_s.at[k], ring_r.at[k], right)

    def swap(k):
        return remote(h_all.at[k, 0], h_all.at[k, 1], swap_s.at[k], swap_r.at[k], sibling)

    def pair(k):
        slot = lax.rem(k, 2)
        return remote(pair_out.at[slot], pair_in.at[slot], pair_s.at[slot], pair_r.at[slot], sibling)

    def scatter(k):
        slot = lax.rem(k, 2)
        return remote(ring_out.at[slot], ring_in.at[k], rs_s.at[k], rs_r.at[k], right)

    def store(k, half):
        return pltpu.make_async_copy(stage.at[half], mlp_hbm.at[k, half], stage_sem.at[half])

    loads[0].wait()
    ring(0).start()
    swap(0).start()
    for load in loads[1:]:
        load.wait()

    def half_chunk(k, half):
        h, g = h_all[k, half], g_all[k, half]
        gate = mm(h, wg[...], NT)
        upward = mm(h, wu[...], NT)
        grad_act = mm(g, wd[...], NT)
        sigma = jax.nn.sigmoid(gate)
        swish = gate * sigma
        act = (swish * upward).astype(BF16)
        gg = (grad_act * upward * sigma * (1.0 + gate * (1.0 - sigma))).astype(BF16)
        gu = (grad_act * swish).astype(BF16)
        columns = pl.ds(pl.multiple_of((2 * k + half) * own, own), own)
        act_t[:, columns] = act.T
        gg_t[:, columns] = gg.T
        gu_t[:, columns] = gu.T
        if half == 1:

            @pl.when(k >= 2)
            def _():
                pair(k - 2).wait_send()

        part = mm(gg, wg[...], NN) + mm(gu, wu[...], NN)
        if half == 1:
            pair_out[lax.rem(k, 2)] = part.astype(BF16)
            pair(k).start()
        else:
            keep[...] = part

        @pl.when(k >= 1)
        def _():
            store(k - 1, half).wait()

        stage[half] = mm(act, wd[...], NN).astype(BF16)
        store(k, half).start()

    def chunk(k, _):
        @pl.when(k >= 1)
        def _():
            ring(k - 1).wait_recv()

            @pl.when(k < chips - 1)
            def _():
                ring(k).start()

            swap(k).start()

        swap(k).wait_recv()
        half_chunk(k, 1)
        half_chunk(k, 0)
        pair(k).wait_recv()
        total = keep[...] + pair_in[lax.rem(k, 2)].astype(F32)

        @pl.when(k == 0)
        def _():
            ghn_ref[...] = total

        @pl.when(k == 1)
        def _():
            ring_out[1] = total.astype(BF16)
            scatter(k).start()

        @pl.when(k >= 2)
        def _():
            scatter(k - 1).wait_recv()

            @pl.when(k >= 3)
            def _():
                scatter(k - 2).wait_send()

            ring_out[lax.rem(k, 2)] = (total + ring_in[k - 1].astype(F32)).astype(BF16)
            scatter(k).start()

        return 0

    lax.fori_loop(0, chips, chunk, 0)

    tile = 512

    def columns_of(j, _):
        at = pl.ds(pl.multiple_of(j * tile, tile), tile)
        h = h_all[:, :, :, at].reshape(seq, tile)
        g = g_all[:, :, :, at].reshape(seq, tile)
        wg[:, at] = mm(gg_t[...], h, NN).astype(BF16)
        wu[:, at] = mm(gu_t[...], h, NN).astype(BF16)
        wd[:, at] = mm(act_t[...], g, NN).astype(BF16)
        return 0

    lax.fori_loop(0, depth // tile, columns_of, 0)
    stores = [
        pltpu.make_async_copy(wg, gw_hbm, store_sem.at[0]),
        pltpu.make_async_copy(wu, uw_hbm, store_sem.at[1]),
        pltpu.make_async_copy(wd, dw_hbm, store_sem.at[2]),
    ]
    for copy in stores:
        copy.start()
    scatter(chips - 1).wait_recv()
    ghn_ref[...] += ring_in[chips - 1].astype(F32)

    for copy in stores:
        copy.wait()
    for half in (0, 1):
        store(chips - 1, half).wait()
    for k in (chips - 2, chips - 1):
        pair(k).wait_send()
        scatter(k).wait_send()
    for k in range(chips):
        swap(k).wait_send()
    for k in range(chips - 1):
        ring(k).wait_send()


def feed_forward(links, hidden_own, grad_chunks, gate_t, up_t, down):
    own, depth = hidden_own.shape
    chips, units = links.chips, down.shape[0]
    seq = chips * 2 * own
    anywhere = pl.BlockSpec(memory_space=pl.ANY)
    dma = pltpu.SemaphoreType.DMA
    return pl.pallas_call(
        functools.partial(mlp_kernel, links),
        in_specs=[anywhere] * 5,
        out_specs=[pl.BlockSpec(memory_space=pltpu.VMEM)] + [anywhere] * 4,
        out_shape=[
            jax.ShapeDtypeStruct((own, depth), F32),
            jax.ShapeDtypeStruct((chips, 2, own, depth), BF16),
            jax.ShapeDtypeStruct((units, depth), BF16),
            jax.ShapeDtypeStruct((units, depth), BF16),
            jax.ShapeDtypeStruct((units, depth), BF16),
        ],
        scratch_shapes=[
            pltpu.VMEM((chips, 2, own, depth), BF16),
            pltpu.VMEM((chips, 2, own, depth), BF16),
            pltpu.VMEM((units, depth), BF16),
            pltpu.VMEM((units, depth), BF16),
            pltpu.VMEM((units, depth), BF16),
            pltpu.VMEM((units, seq), BF16),
            pltpu.VMEM((units, seq), BF16),
            pltpu.VMEM((units, seq), BF16),
            pltpu.VMEM((own, depth), F32),
            pltpu.VMEM((2, own, depth), BF16),
            pltpu.VMEM((2, own, depth), BF16),
            pltpu.VMEM((2, own, depth), BF16),
            pltpu.VMEM((2, own, depth), BF16),
            pltpu.VMEM((chips, own, depth), BF16),
            dma((5,)),
            dma((chips,)), dma((chips,)), dma((chips,)), dma((chips,)), dma((2,)), dma((2,)),
            dma((chips,)), dma((chips,)), dma((2,)), dma((3,)),
        ],
        compiler_params=pltpu.CompilerParams(
            collective_id=1, has_side_effects=True, vmem_limit_bytes=60 * 2**20
        ),
        cost_estimate=pl.CostEstimate(
            flops=18 * seq * depth * units, bytes_accessed=64 * 2**20, transcendentals=seq * units
        ),
        name="feed_forward",
    )(hidden_own, grad_chunks, gate_t, up_t, down)


def rms_factor(values):
    return lax.rsqrt(jnp.mean(values * values, axis=-1, keepdims=True) + EPSILON)


def local(
    n_tensor, n_dp,
    tokens, out_grad, query_two, grad_two, doc_split, attn_gain, mlp_gain, w_query, w_kv, w_out, w_gate, w_up, w_down,
):
    links = Links(n_tensor, n_dp)
    chips = links.chips
    own = tokens.shape[0]
    rows = 2 * own
    seq = own * n_tensor
    width = w_query.shape[1]
    me_dp = lax.axis_index("dp")
    me_t = lax.axis_index("tensor")
    chip, core = me_t // 2, me_t % 2
    two_docs = doc_split[0]
    sp = jnp.stack([chip, two_docs, core]).astype(jnp.int32)
    place = jnp.array(links.place, jnp.int32)
    order = jnp.array(links.order, jnp.int32)

    spot = jnp.arange(rows, dtype=jnp.int32) + core * own
    spot = chip * rows + jnp.where(spot >= rows, spot - rows, spot)
    position = jnp.where(two_docs > 0, spot % SEQ_SHORT, spot)
    frequency = 10000.0 ** (-jnp.arange(HD // 2, dtype=F32) * 2.0 / HD)
    phases = position.astype(F32)[:, None] * frequency[None, :]
    cos, sin = jnp.cos(phases), jnp.sin(phases)
    cosine = jnp.concatenate([cos, cos], axis=1)
    sine = jnp.concatenate([-sin, sin], axis=1)

    residual = tokens.astype(F32)
    attn_scale = rms_factor(residual)
    attn_pre = residual * attn_scale
    normed_own = (attn_pre * attn_gain).astype(BF16)

    kv_lin = mm(normed_own, w_kv, NN)
    half = HD // 2
    key_lin = kv_lin[:, :HD]
    key_own = key_lin * cosine[:own] + jnp.concatenate([key_lin[:, half:], key_lin[:, :half]], axis=1) * sine[:own]
    kv_own = jnp.concatenate([key_own, kv_lin[:, HD:]], axis=1).astype(BF16)
    kv_mine = jnp.stack(ring_gather(links, kv_own))
    kv_other = links.swap(kv_mine)
    kv_first = jnp.where(core == 0, kv_mine, kv_other)
    kv_second = jnp.where(core == 0, kv_other, kv_mine)
    kv_rel = jnp.concatenate([kv_first, kv_second], axis=1)
    kv_all = jnp.concatenate(
        [
            lax.dynamic_index_in_dim(kv_rel, (place[chip] - links.place[j] + chips) % chips, 0, keepdims=False)
            for j in range(chips)
        ],
        axis=0,
    )
    key_rows, value_rows = kv_all[:, :HD], kv_all[:, HD:]

    wq_blocks = gather_weight(links, w_query, me_dp)
    wo_blocks = gather_weight(links, w_out, me_dp)
    wq = jnp.concatenate(wq_blocks, axis=1)
    wo = jnp.concatenate(wo_blocks, axis=0)
    grad_chunks = [both(links, piece) for piece in ring_gather(links, out_grad)]

    dk2, dv2 = second_back(sp, query_two, grad_two, key_rows, value_rows)

    normed = both(links, normed_own)
    q_lin = mm(normed, wq, NN)
    queries, context, lse = attend(sp, q_lin, cosine, sine, key_rows, value_rows)
    branch = pair_sum(links, mm(context, wo, NN))
    hidden = residual + branch
    mlp_scale = rms_factor(hidden)
    mlp_pre = hidden * mlp_scale
    hidden_own = (mlp_pre * mlp_gain).astype(BF16)

    grad_stack = jnp.stack(grad_chunks).reshape(chips, 2, own, -1)
    grad_hn, mlp_parts, gate_w, up_w, down_w = feed_forward(
        links, hidden_own, grad_stack, w_gate.T, w_up.T, w_down
    )
    gate_w, up_w, down_w = lax.psum((gate_w, up_w, down_w), "dp")
    gate_w_grad = gate_w.astype(F32).T
    up_w_grad = up_w.astype(F32).T
    down_w_grad = down_w.astype(F32)
    mlp_sums = mlp_parts[:, 0].astype(F32) + links.swap(mlp_parts[:, 1]).astype(F32)
    mlp_out = ring_scatter(links, [mlp_sums[k] for k in range(chips)])
    block_output = (hidden + mlp_out).astype(BF16)

    mlp_gain_part = jnp.sum(grad_hn * mlp_pre, axis=0)
    scaled_mlp = grad_hn * mlp_gain
    grad_hidden = out_grad.astype(F32) + mlp_scale * (
        scaled_mlp - mlp_pre * jnp.mean(scaled_mlp * mlp_pre, axis=-1, keepdims=True)
    )

    grad_branch = both(links, grad_hidden.astype(BF16))
    grad_context = mm(grad_branch, wo, NT).astype(BF16)
    query_grad, dk, dv = attend_back(
        sp, queries, grad_context, context, lse, cosine, sine, key_rows, value_rows, dk2, dv2
    )
    out_w_parts = [
        mm(context[:, k * width : (k + 1) * width], grad_branch, TN).astype(BF16) for k in range(chips)
    ]
    out_w_grad = sum_dp(links, ring_scatter(links, out_w_parts).astype(BF16), me_dp)

    kv_part = jnp.concatenate([dk * SCALE, dv], axis=1).astype(BF16).reshape(chips, 2, own, 2 * HD)
    kv_keep = lax.dynamic_index_in_dim(kv_part, core, 1, keepdims=False)
    kv_send = lax.dynamic_index_in_dim(kv_part, 1 - core, 1, keepdims=False)
    kv_sum = kv_keep.astype(F32) + links.swap(kv_send).astype(F32)
    kv_terms = [
        lax.dynamic_index_in_dim(kv_sum, order[(place[chip] - k + chips) % chips], 0, keepdims=False)
        for k in range(chips)
    ]
    kv_grad = ring_scatter(links, kv_terms)
    key_grad = kv_grad[:, :HD]
    key_grad = key_grad * cosine[:own] - jnp.concatenate([key_grad[:, half:], key_grad[:, :half]], axis=1) * sine[:own]
    kv_grad_lin = jnp.concatenate([key_grad, kv_grad[:, HD:]], axis=1).astype(BF16)

    query_w_parts = [
        mm(normed, query_grad[:, k * width : (k + 1) * width], TN).astype(BF16) for k in range(chips)
    ]
    query_w_grad = sum_dp(links, ring_scatter(links, query_w_parts).astype(BF16), me_dp)

    grad_normed = pair_sum(links, mm(query_grad, wq, NT)) + mm(kv_grad_lin, w_kv, NT)
    attn_gain_part = jnp.sum(grad_normed * attn_pre, axis=0)
    scaled_attn = grad_normed * attn_gain
    tokens_grad = (
        grad_hidden
        + attn_scale * (scaled_attn - attn_pre * jnp.mean(scaled_attn * attn_pre, axis=-1, keepdims=True))
    ).astype(BF16)

    kv_w = mm(kv_grad_lin, normed_own, TN).astype(BF16).reshape(chips, 2, HD // chips, -1)
    kv_w_keep = lax.dynamic_index_in_dim(kv_w, core, 1, keepdims=False)
    kv_w_send = lax.dynamic_index_in_dim(kv_w, 1 - core, 1, keepdims=False)
    kv_w_sum = kv_w_keep.astype(F32) + links.swap(kv_w_send).astype(F32)
    kv_w_terms = [
        lax.dynamic_index_in_dim(kv_w_sum, order[(place[chip] - k + chips) % chips], 0, keepdims=False)
        for k in range(chips)
    ]
    kv_w_own = sum_dp(links, ring_scatter(links, kv_w_terms).astype(BF16), me_dp)
    kv_w_mine = jnp.stack(ring_gather(links, kv_w_own.astype(BF16)))
    kv_w_other = links.swap(kv_w_mine)
    kv_w_pair = jnp.stack(
        [jnp.where(core == 0, kv_w_mine, kv_w_other), jnp.where(core == 0, kv_w_other, kv_w_mine)], axis=1
    )
    kv_w_grad = (
        jnp.concatenate(
            [
                lax.dynamic_index_in_dim(kv_w_pair, (place[chip] - links.place[j] + chips) % chips, 0, keepdims=False)
                for j in range(chips)
            ],
            axis=0,
        )
        .reshape(2 * HD, -1)
        .astype(F32)
        .T
    )

    attn_gain_grad = sum_all(links, attn_gain_part)
    mlp_gain_grad = sum_all(links, mlp_gain_part)
    return (
        block_output,
        tokens_grad,
        attn_gain_grad,
        mlp_gain_grad,
        query_w_grad,
        kv_w_grad,
        out_w_grad,
        gate_w_grad,
        up_w_grad,
        down_w_grad,
    )


def solution(mesh):
    both_axes = P(("dp", "tensor"), None)
    return jax.shard_map(
        functools.partial(local, mesh.shape["tensor"], mesh.shape["dp"]),
        mesh=mesh,
        in_specs=(
            both_axes,
            both_axes,
            P("dp", "tensor"),
            P("dp", "tensor"),
            P("dp"),
            P(),
            P(),
            P(None, "tensor"),
            P(),
            P("tensor", None),
            P(None, "tensor"),
            P(None, "tensor"),
            P("tensor", None),
        ),
        out_specs=(
            both_axes,
            both_axes,
            P(),
            P(),
            P(None, "tensor"),
            P(),
            P("tensor", None),
            P(None, "tensor"),
            P(None, "tensor"),
            P("tensor", None),
        ),
        check_vma=False,
    )
```

```python
import functools

import jax
import jax.numpy as jnp
from jax import lax
from jax.experimental import pallas as pl
from jax.experimental.pallas import tpu as pltpu
from jax.sharding import PartitionSpec as P

HD = 128
SEQ_SHORT = 1024
EPSILON = 1e-05
MASKED = -1e30
SCALE = HD ** (-0.5)
SCALE2 = SCALE * 1.4426950408889634
F32 = jnp.float32
BF16 = jnp.bfloat16
VMEM_LIMIT = 56 * 2**20


def mm(left, right, dims):
    return lax.dot_general(left, right, (dims, ((), ())), preferred_element_type=F32)


NN = ((1,), (0,))
NT = ((1,), (1,))
TN = ((0,), (0,))


class Links:
    def __init__(self, n_tensor, n_dp):
        self.n_tensor, self.n_dp = n_tensor, n_dp
        self.chips = n_tensor // 2
        odd = list(range(1, self.chips, 2))
        even = list(range(2, self.chips, 2))
        self.order = [0] + odd + even[::-1]
        nxt = {c: self.order[(i + 1) % self.chips] for i, c in enumerate(self.order)}
        self.place = [self.order.index(c) for c in range(self.chips)]
        self.ring_pairs = [(2 * c + k, 2 * nxt[c] + k) for c in range(self.chips) for k in (0, 1)]
        self.swap_pairs = [(i, i ^ 1) for i in range(n_tensor)]
        self.bits = [1 << b for b in range(n_dp.bit_length() - 1)]

    def ring(self, x):
        return lax.ppermute(x, "tensor", self.ring_pairs)

    def swap(self, x):
        return lax.ppermute(x, "tensor", self.swap_pairs)

    def across(self, x, bit):
        return lax.ppermute(x, "dp", [(i, i ^ bit) for i in range(self.n_dp)])

    def across_tensor(self, x, bit):
        return lax.ppermute(x, "tensor", [(i, i ^ bit) for i in range(self.n_tensor)])

    def neighbours(self, chip):
        ahead, behind = chip * 0, chip * 0
        for i, c in enumerate(self.order):
            ahead = jnp.where(chip == c, self.order[(i + 1) % self.chips], ahead)
            behind = jnp.where(chip == c, self.order[i - 1], behind)
        return ahead, behind

    def orders(self, rows, unit):
        ways = len(self.bits)
        if ways < 2 or rows % (ways * unit):
            return [self.bits]
        return [self.bits[i:] + self.bits[:i] for i in range(ways)]


def take_rows(x, index, size):
    return lax.dynamic_slice_in_dim(x, index * size, size, 0)


def gather_dp(links, piece, me):
    orders = links.orders(piece.shape[0], 8)
    part_rows = piece.shape[0] // len(orders)
    parts = []
    for number, bits in enumerate(orders):
        stack = lax.slice_in_dim(piece, number * part_rows, (number + 1) * part_rows, axis=0)
        held = [0]
        for bit in bits:
            stack = jnp.concatenate([stack, links.across(stack, bit)], axis=0)
            held = held + [h ^ bit for h in held]
        where = jnp.array([held.index(rel) for rel in range(links.n_dp)], jnp.int32)
        parts.append((stack, where))
    out = []
    for j in range(links.n_dp):
        for stack, where in parts:
            out.append(take_rows(stack, where[me ^ j], part_rows))
    return jnp.concatenate(out, axis=0)


def gather_weight(links, block, me):
    rows = block.shape[0] // links.n_dp
    blocks = [block]
    piece = take_rows(block, me, rows)
    for _ in range(links.chips - 1):
        piece = links.ring(piece)
        blocks.append(gather_dp(links, piece, me))
    return blocks


def sum_dp(links, x, me):
    orders = links.orders(x.shape[0], 8 * links.n_dp)
    part_rows = x.shape[0] // len(orders)
    size = part_rows // links.n_dp
    outs = []
    for number, bits in enumerate(orders):
        held = lax.slice_in_dim(x, number * part_rows, (number + 1) * part_rows, axis=0)
        pieces = [held.reshape((links.n_dp, size) + x.shape[1:])]
        array = pieces[0]
        axes = [links.n_dp]
        nbits = len(links.bits)
        array = array.reshape((2,) * nbits + (size,) + x.shape[1:])
        left = list(reversed(links.bits))
        for bit in bits:
            axis = left.index(bit)
            mine = jnp.minimum(me & bit, 1)
            keep = lax.dynamic_index_in_dim(array, mine, axis, keepdims=False)
            send = lax.dynamic_index_in_dim(array, 1 - mine, axis, keepdims=False)
            got = links.across(send, bit)
            array = (keep.astype(F32) + got.astype(F32)).astype(BF16)
            left.remove(bit)
        stack = array.reshape((size,) + x.shape[1:])
        rel = [0]
        for bit in reversed(bits):
            stack = jnp.concatenate([stack, links.across(stack, bit)], axis=0)
            rel = rel + [r ^ bit for r in rel]
        where = jnp.array([rel.index(r) for r in range(links.n_dp)], jnp.int32)
        for j in range(links.n_dp):
            outs.append(take_rows(stack, where[me ^ j], size))
    return jnp.concatenate(outs, axis=0).astype(F32)


def ring_gather(links, own):
    out = [own]
    for _ in range(links.chips - 1):
        out.append(links.ring(out[-1]))
    return out


def ring_scatter(links, terms):
    got = None
    for term in terms[1:] + terms[:1]:
        total = term if got is None else term.astype(F32) + got.astype(F32)
        if term is terms[0]:
            return total.astype(F32)
        got = links.ring(total.astype(BF16))
    return got


def both(links, own):
    return jnp.concatenate([own, links.swap(own)], axis=0)


def pair_sum(links, part):
    rows = part.shape[0] // 2
    return part[:rows].astype(F32) + links.swap(part[rows:].astype(BF16)).astype(F32)


def sum_all(links, x):
    bit = 1
    while bit < links.n_tensor:
        x = x + links.across_tensor(x, bit)
        bit *= 2
    for bit in links.bits:
        x = x + links.across(x, bit)
    return x


def diagonal(shape, row_axis, shift):
    size = shape[row_axis]
    row = lax.broadcasted_iota(jnp.int32, shape, row_axis) + shift
    row = jnp.where(row >= size, row - size, row)
    return lax.broadcasted_iota(jnp.int32, shape, 1 - row_axis) <= row


def span(block, two_docs, rows):
    per_doc = SEQ_SHORT // rows
    inner = jnp.where(two_docs > 0, lax.rem(block, per_doc), block)
    return inner + 1, pl.multiple_of((block - inner) * rows, rows)


def fwd_kernel(blocks, sp_ref, q_ref, c_ref, s_ref, k_ref, v_ref, qo_ref, ctx_ref, lse_ref):
    rows = q_ref.shape[0]
    chip, two_docs, core = sp_ref[0], sp_ref[1], sp_ref[2]
    x = q_ref[...]
    q = (x * c_ref[...] + pltpu.roll(x, HD // 2, 1) * s_ref[...]).astype(BF16)
    qo_ref[...] = q
    count, low = span(chip, two_docs, rows)
    mask = diagonal((rows, rows), 0, core * (rows // 2))
    for n in range(1, blocks + 1):

        @pl.when(count == n)
        def _(n=n):
            near = (n - 1) * rows
            diag = pl.ds(low + near, rows)
            s_diag = jnp.where(mask, mm(q, k_ref[diag, :], NT) * SCALE2, MASKED)
            top = jnp.max(s_diag, axis=1, keepdims=True)
            if n > 1:
                main = pl.ds(low, near)
                s_main = mm(q, k_ref[main, :], NT) * SCALE2
                top = jnp.maximum(top, jnp.max(s_main, axis=1, keepdims=True))
            p_diag = jnp.exp2(s_diag - top)
            total = jnp.sum(p_diag, axis=1, keepdims=True)
            out = mm(p_diag.astype(BF16), v_ref[diag, :], NN)
            if n > 1:
                p_main = jnp.exp2(s_main - top)
                total = total + jnp.sum(p_main, axis=1, keepdims=True)
                out = out + mm(p_main.astype(BF16), v_ref[main, :], NN)
            ctx_ref[...] = (out / total).astype(BF16)
            lse = jnp.broadcast_to(top + jnp.log2(total), (rows, HD))
            lse_ref[0] = lse.T[:8]


def bwd_kernel(
    blocks, sp_ref, q_ref, do_ref, ctx_ref, lse_ref, c_ref, s_ref, k_ref, kt_ref, v_ref, dk0_ref, dv0_ref,
    dq_ref, dk_ref, dv_ref,
):
    rows = q_ref.shape[0]
    chip, two_docs, core = sp_ref[0], sp_ref[1], sp_ref[2]

    @pl.when(pl.program_id(0) == 0)
    def _():
        dk_ref[...] = dk0_ref[...]
        dv_ref[...] = dv0_ref[...]

    q, do = q_ref[...], do_ref[...]
    dot = jnp.sum(do.astype(F32) * ctx_ref[...].astype(F32), axis=1, keepdims=True)
    dot = jnp.broadcast_to(dot, (rows, HD)).T[:1]
    lse = lse_ref[0, :1]
    count, low = span(chip, two_docs, rows)
    mask = diagonal((rows, rows), 1, core * (rows // 2))
    for n in range(1, blocks + 1):

        @pl.when(count == n)
        def _(n=n):
            near = (n - 1) * rows
            dqt = jnp.zeros((HD, rows), F32)
            for keys, masked in ((pl.ds(low, near), False), (pl.ds(low + near, rows), True)):
                if not masked and n == 1:
                    continue
                p = jnp.exp2(mm(k_ref[keys, :], q, NT) * SCALE2 - lse)
                if masked:
                    p = jnp.where(mask, p, 0.0)
                ds = (p * (mm(v_ref[keys, :], do, NT) - dot)).astype(BF16)
                dv_ref[keys, :] += mm(p.astype(BF16), do, NN)
                dk_ref[keys, :] += mm(ds, q, NN)
                dqt = dqt + mm(kt_ref[:, keys], ds, NN)
            g = dqt.T * SCALE
            dq_ref[...] = (g * c_ref[...] - pltpu.roll(g, HD // 2, 1) * s_ref[...]).astype(BF16)


def whole(shape):
    return pl.BlockSpec(shape, lambda *_: (0,) * len(shape))


def second_half(seq):
    return pl.BlockSpec((seq, HD), lambda *_: (0, 1))


def attend(sp, q_lin, cosine, sine, kv_all):
    rows, width = q_lin.shape
    seq = kv_all.shape[0]
    heads = width // HD
    column = pl.BlockSpec((rows, HD), lambda h, *_: (0, h))
    return pl.pallas_call(
        functools.partial(fwd_kernel, seq // rows),
        grid_spec=pltpu.PrefetchScalarGridSpec(
            num_scalar_prefetch=1,
            grid=(heads,),
            in_specs=[column, whole((rows, HD)), whole((rows, HD)), whole((seq, HD)), second_half(seq)],
            out_specs=[column, column, pl.BlockSpec((1, 8, rows), lambda h, *_: (h, 0, 0))],
        ),
        out_shape=[
            jax.ShapeDtypeStruct((rows, width), BF16),
            jax.ShapeDtypeStruct((rows, width), BF16),
            jax.ShapeDtypeStruct((heads, 8, rows), F32),
        ],
        compiler_params=pltpu.CompilerParams(vmem_limit_bytes=VMEM_LIMIT),
        cost_estimate=pl.CostEstimate(
            flops=8 * heads * rows * seq * HD, bytes_accessed=16 * rows * width, transcendentals=heads * rows * seq
        ),
        name="attend",
    )(sp, q_lin, cosine, sine, kv_all, kv_all)


def attend_back(sp, queries, grad_context, context, lse, cosine, sine, kv_all, key_rows_t, dk0, dv0):
    rows, width = queries.shape
    seq = kv_all.shape[0]
    heads = width // HD
    column = pl.BlockSpec((rows, HD), lambda h, *_: (0, h))
    return pl.pallas_call(
        functools.partial(bwd_kernel, seq // rows),
        grid_spec=pltpu.PrefetchScalarGridSpec(
            num_scalar_prefetch=1,
            grid=(heads,),
            in_specs=[
                column, column, column, pl.BlockSpec((1, 8, rows), lambda h, *_: (h, 0, 0)),
                whole((rows, HD)), whole((rows, HD)), whole((seq, HD)), whole((HD, seq)), second_half(seq),
                whole((seq, HD)), whole((seq, HD)),
            ],
            out_specs=[column, whole((seq, HD)), whole((seq, HD))],
        ),
        out_shape=[
            jax.ShapeDtypeStruct((rows, width), BF16),
            jax.ShapeDtypeStruct((seq, HD), F32),
            jax.ShapeDtypeStruct((seq, HD), F32),
        ],
        compiler_params=pltpu.CompilerParams(vmem_limit_bytes=VMEM_LIMIT),
        cost_estimate=pl.CostEstimate(
            flops=20 * heads * rows * seq * HD, bytes_accessed=16 * rows * width, transcendentals=heads * rows * seq
        ),
        name="attend_back",
    )(sp, queries, grad_context, context, lse, cosine, sine, kv_all, key_rows_t, kv_all, dk0, dv0)


def second_unit(block, rows, q, do, kv, dk_ref, dv_ref, late):
    mask = diagonal((rows, rows), 1, 0)
    first = block * rows
    parts = [(pl.ds(first, rows), True, False)]
    middle = SEQ_SHORT * (first // SEQ_SHORT)
    if first > middle:
        parts.append((pl.ds(middle, first - middle), False, False))
    if middle:
        parts.append((pl.ds(0, middle), False, True))
    scores = []
    for keys, masked, far in parts:
        score = mm(kv[keys, :HD], q, NT) * SCALE2
        scores.append(jnp.where(mask, score, MASKED) if masked else score + late if far else score)
    top = functools.reduce(jnp.maximum, [jnp.max(score, axis=0, keepdims=True) for score in scores])
    lifted = [jnp.exp2(score - top) for score in scores]
    inverse = 1.0 / sum(jnp.sum(p, axis=0, keepdims=True) for p in lifted)
    back = [mm(kv[keys, HD:], do, NT) for keys, _, _ in parts]
    dot = sum(jnp.sum(p * b, axis=0, keepdims=True) for p, b in zip(lifted, back)) * inverse
    for (keys, _, _), p, b in zip(parts, lifted, back):
        p = p * inverse
        dv_ref[keys, :] += mm(p.astype(BF16), do, NN)
        dk_ref[keys, :] += mm((p * (b - dot)).astype(BF16), q, NN)


FRONT_ORDER = (
    "kv q1 o1 kv", "q1 q2 o1 o2", "kv q1 q2 q3", "kv o1 o2 o3", "kv* s q2 q3", "s o2 o3 s", "q2 q3 s o2",
    "o3 s q3 s", "g s o3 s",
    "q1* o1* q2* o2*", "q3* o3* s* g*",
)


def front_kernel(
    links, docs, tokens, gain, w_kv, cosine, sine, q_two, g_two, wq_hbm, wo_hbm, og_hbm,
    normed, wq_out, wo_out, og_up, og_pair, og_up_pair, kv_out, kt_ref, dk_ref, dv_ref,
    kv, ss, rs, ls,
):
    chips, bits, n_dp = links.chips, links.bits, links.n_dp
    own, depth = tokens.shape
    seq = own * links.n_tensor
    width = wq_hbm.shape[1]
    me = lax.axis_index("tensor")
    me_dp = lax.axis_index("dp")
    chip, core = me // 2, lax.rem(me, 2)
    ahead, behind = links.neighbours(chip)
    right = {"tensor": ahead * 2 + core}
    left = {"tensor": behind * 2 + core}
    sibling = {"tensor": me ^ 1}
    barrier = pltpu.get_barrier_semaphore()
    peers = [right, left, sibling] + [{"dp": me_dp ^ bit} for bit in bits]
    for peer in peers:
        pl.semaphore_signal(barrier, inc=1, device_id=peer, device_id_type=pl.DeviceIdType.MESH)

    copies = []

    def send(src, dst, peer):
        number = len(copies)
        copy = mesh_copy(src, dst, ss.at[number], rs.at[number], peer)
        copy.start()
        copies.append(copy)
        return copy

    def q_piece(ref, k, j, way, size=1):
        rows = depth // n_dp // 2
        at = pl.ds(pl.multiple_of((2 * j + way) * rows, rows), size * rows)
        return ref.at[at, :] if k is None else ref.at[at, pl.ds(k * width, width)]

    def o_piece(ref, k, j, way, size=1):
        rows, half = width // n_dp, depth // 2
        at = pl.ds(pl.multiple_of((k or 0) * width + j * rows, rows), rows)
        return ref.at[at, pl.ds(way * half, size * half)]

    pl.semaphore_wait(barrier, len(peers))
    locals_ = [
        pltpu.make_async_copy(wq_hbm, wq_out.at[:, pl.ds(0, width)], ls.at[0]),
        pltpu.make_async_copy(wo_hbm, wo_out.at[pl.ds(0, width), :], ls.at[1]),
    ]
    for copy in locals_:
        copy.start()
    hops = {}
    for name, piece, src, dst in (("q", q_piece, wq_hbm, wq_out), ("o", o_piece, wo_hbm, wo_out)):
        hops[name, 1] = send(piece(src, None, me_dp, 0, 2), piece(dst, 1, me_dp, 0, 2), right)

    x = tokens[...].astype(F32)
    own_rows = pl.ds(0, own)
    normed[own_rows] = (x * lax.rsqrt(jnp.mean(x * x, axis=1, keepdims=True) + EPSILON) * gain[...]).astype(BF16)
    normed_swap = send(normed.at[own_rows], normed.at[pl.ds(own, own)], sibling)
    lin = mm(normed[own_rows], w_kv[...], NN)
    key = lin[:, :HD] * cosine[...] + pltpu.roll(lin[:, :HD], HD // 2, 1) * sine[...]

    def chip_up(k):
        found = chip * 0
        for i, c in enumerate(links.order):
            found = jnp.where(chip == c, links.order[(i - k) % chips], found)
        return found

    def kv_at(k):
        return kv.at[pl.ds(pl.multiple_of((chip_up(k) * 2 + core) * own, own), own)]

    kv_at(0)[...] = jnp.concatenate([key, lin[:, HD:]], axis=1).astype(BF16)
    late = jnp.where(docs[0] > 0, MASKED, 0.0)
    dk_ref[...] = jnp.zeros_like(dk_ref)
    dv_ref[...] = jnp.zeros_like(dv_ref)

    def kv_chain():
        swaps = []
        for k in range(chips):
            copy = send(kv_at(k), kv_at(k), right) if k + 1 < chips else None
            swaps.append(send(kv_at(k), kv_at(k), sibling))
            yield
            if copy is not None:
                copy.wait_recv()
        for copy in swaps:
            copy.wait_recv()
        store = pltpu.make_async_copy(kv, kv_out, ls.at[2])
        store.start()
        locals_.append(store)
        kt_ref[...] = kv[:, :HD].T

    def block_chain(name, piece, dst, k):
        hops[name, k].wait_recv()
        if k + 1 < chips:
            hops[name, k + 1] = send(piece(dst, k, me_dp, 0, 2), piece(dst, k + 1, me_dp, 0, 2), right)
        held = [[0], [0]]
        for step in range(len(bits)):
            sent = []
            for rank in range(len(held[0])):
                for way, order in enumerate((bits, bits[::-1])):
                    bit, rel = order[step], held[way][rank]
                    where = piece(dst, k, me_dp ^ rel, way)
                    sent.append((send(where, where, {"dp": me_dp ^ bit}), way, rel ^ bit))
            yield
            for copy, way, rel in sent:
                copy.wait_recv()
                held[way].append(rel)

    def grad_chain():
        swap = send(og_hbm, og_pair, sibling)
        hop = send(og_hbm, og_up, right)
        yield
        hop.wait_recv()
        second = send(og_up, og_up_pair, sibling)
        yield
        swap.wait_recv()
        second.wait_recv()

    rows = min(512, SEQ_SHORT)
    heads = q_two.shape[1] // HD

    def second_chain():
        for block in reversed(range(seq // rows)):
            for head in range(heads):
                at = (pl.ds(block * rows, rows), pl.ds(head * HD, HD))
                second_unit(block, rows, q_two[at], g_two[at], kv, dk_ref, dv_ref, late)
                yield

    chains = {"kv": kv_chain(), "s": second_chain(), "g": grad_chain()}
    for k in range(1, chips):
        chains["q%d" % k] = block_chain("q", q_piece, wq_out, k)
        chains["o%d" % k] = block_chain("o", o_piece, wo_out, k)
    take_turns(chains, FRONT_ORDER)
    normed_swap.wait_recv()
    for copy in copies:
        copy.wait_send()
    for copy in locals_:
        copy.wait()


def take_turns(chains, order):
    def turn(name):
        if name in chains and next(chains[name], chains) is chains:
            del chains[name]

    for name in " ".join(order).split():
        turn(name.rstrip("*"))
        while name.endswith("*") and name.rstrip("*") in chains:
            turn(name.rstrip("*"))
    while chains:
        for name in list(chains):
            turn(name)


def front(links, docs, tokens, gain, w_kv, cosine, sine, q_two, g_two, w_query, w_out, out_grad):
    chips = links.chips
    own, depth = tokens.shape
    seq = own * links.n_tensor
    width = w_query.shape[1]
    anywhere = pl.BlockSpec(memory_space=pl.ANY)
    here = pl.BlockSpec(memory_space=pltpu.VMEM)
    dma = pltpu.SemaphoreType.DMA
    shape = jax.ShapeDtypeStruct
    count = 2 * chips * (2 * links.n_dp) + 2 * chips + 8
    return pl.pallas_call(
        functools.partial(front_kernel, links),
        in_specs=[pl.BlockSpec(memory_space=pltpu.SMEM)] + [here] * 7 + [anywhere] * 3,
        out_specs=[here] + [anywhere] * 6 + [here] * 3,
        out_shape=[
            shape((2 * own, depth), BF16), shape((depth, chips * width), BF16), shape((chips * width, depth), BF16),
            shape((own, depth), BF16), shape((own, depth), BF16), shape((own, depth), BF16),
            shape((seq, 2 * HD), BF16), shape((HD, seq), BF16), shape((seq, HD), F32), shape((seq, HD), F32),
        ],
        scratch_shapes=[pltpu.VMEM((seq, 2 * HD), BF16), dma((count,)), dma((count,)), dma((3,))],
        compiler_params=pltpu.CompilerParams(
            collective_id=3, has_side_effects=True, vmem_limit_bytes=VMEM_LIMIT
        ),
        cost_estimate=pl.CostEstimate(flops=10**10, bytes_accessed=64 * 2**20, transcendentals=0),
        name="front",
    )(docs, tokens, gain, w_kv, cosine, sine, q_two, g_two, w_query, w_out, out_grad)


def mlp_kernel(
    links, h_hbm, wg_hbm, wu_hbm, wd_hbm, *refs,
):
    g_hbm, refs = refs[: links.n_tensor], refs[links.n_tensor :]
    (
    ghn_ref, mlp_hbm, grads_hbm, h_all, g_all, wg, wu, wd, act_t, gg_t, gu_t, keep, stage, pair_out, pair_in, ring_out, ring_in,
    load_sem, ring_s, ring_r, swap_s, swap_r, pair_s, pair_r, rs_s, rs_r, stage_sem, store_sem,
    ) = refs
    chips = links.chips
    own, depth = h_hbm.shape
    seq = chips * 2 * own
    me = lax.axis_index("tensor")
    chip, core = me // 2, lax.rem(me, 2)
    ahead, behind = links.neighbours(chip)
    right = {"tensor": ahead * 2 + core}
    left = {"tensor": behind * 2 + core}
    sibling = {"tensor": chip * 2 + 1 - core}

    loads = [
        pltpu.make_async_copy(h_hbm, h_all.at[0, 0], load_sem.at[0]),
        pltpu.make_async_copy(wg_hbm, wg, load_sem.at[1]),
        pltpu.make_async_copy(wu_hbm, wu, load_sem.at[2]),
        pltpu.make_async_copy(wd_hbm, wd, load_sem.at[3]),
    ] + [
        pltpu.make_async_copy(ref, g_all.at[i // 2, i % 2], load_sem.at[4 + i]) for i, ref in enumerate(g_hbm)
    ]
    for load in loads:
        load.start()
    barrier = pltpu.get_barrier_semaphore()
    for peer in (right, left, sibling):
        pl.semaphore_signal(barrier, inc=1, device_id=peer, device_id_type=pl.DeviceIdType.MESH)
    pl.semaphore_wait(barrier, 3)

    def remote(src, dst, send, recv, peer):
        return pltpu.make_async_remote_copy(
            src_ref=src, dst_ref=dst, send_sem=send, recv_sem=recv, device_id=peer,
            device_id_type=pl.DeviceIdType.MESH,
        )

    def ring(k):
        return remote(h_all.at[k, 0], h_all.at[k + 1, 0], ring_s.at[k], ring_r.at[k], right)

    def swap(k):
        return remote(h_all.at[k, 0], h_all.at[k, 1], swap_s.at[k], swap_r.at[k], sibling)

    def pair(k):
        slot = lax.rem(k, 2)
        return remote(pair_out.at[slot], pair_in.at[slot], pair_s.at[slot], pair_r.at[slot], sibling)

    def scatter(k):
        slot = lax.rem(k, 2)
        return remote(ring_out.at[slot], ring_in.at[k], rs_s.at[k], rs_r.at[k], right)

    def store(k, half):
        return pltpu.make_async_copy(stage.at[half], mlp_hbm.at[k, half], stage_sem.at[half])

    loads[0].wait()
    ring(0).start()
    swap(0).start()
    for load in loads[1:]:
        load.wait()

    def half_chunk(k, half):
        h, g = h_all[k, half], g_all[k, half]
        gate = mm(h, wg[...], NT)
        upward = mm(h, wu[...], NT)
        grad_act = mm(g, wd[...], NT)
        sigma = jax.nn.sigmoid(gate)
        swish = gate * sigma
        act = (swish * upward).astype(BF16)
        gg = (grad_act * upward * sigma * (1.0 + gate * (1.0 - sigma))).astype(BF16)
        gu = (grad_act * swish).astype(BF16)
        columns = pl.ds(pl.multiple_of((2 * k + half) * own, own), own)
        act_t[:, columns] = act.T
        gg_t[:, columns] = gg.T
        gu_t[:, columns] = gu.T
        if half == 1:

            @pl.when(k >= 2)
            def _():
                pair(k - 2).wait_send()

        part = mm(gg, wg[...], NN) + mm(gu, wu[...], NN)
        if half == 1:
            pair_out[lax.rem(k, 2)] = part.astype(BF16)
            pair(k).start()
        else:
            keep[...] = part

        @pl.when(k >= 1)
        def _():
            store(k - 1, half).wait()

        stage[half] = mm(act, wd[...], NN).astype(BF16)
        store(k, half).start()

    def chunk(k, _):
        @pl.when(k >= 1)
        def _():
            ring(k - 1).wait_recv()

            @pl.when(k < chips - 1)
            def _():
                ring(k).start()

            swap(k).start()

        swap(k).wait_recv()
        half_chunk(k, 1)
        half_chunk(k, 0)
        pair(k).wait_recv()
        total = keep[...] + pair_in[lax.rem(k, 2)].astype(F32)

        @pl.when(k == 0)
        def _():
            ghn_ref[...] = total

        @pl.when(k == 1)
        def _():
            ring_out[1] = total.astype(BF16)
            scatter(k).start()

        @pl.when(k >= 2)
        def _():
            scatter(k - 1).wait_recv()

            @pl.when(k >= 3)
            def _():
                scatter(k - 2).wait_send()

            ring_out[lax.rem(k, 2)] = (total + ring_in[k - 1].astype(F32)).astype(BF16)
            scatter(k).start()

        return 0

    lax.fori_loop(0, chips, chunk, 0)

    tile = 512

    def columns_of(j, _):
        at = pl.ds(pl.multiple_of(j * tile, tile), tile)
        h = h_all[:, :, :, at].reshape(seq, tile)
        g = g_all[:, :, :, at].reshape(seq, tile)
        wg[:, at] = mm(gg_t[...], h, NN).astype(BF16)
        wu[:, at] = mm(gu_t[...], h, NN).astype(BF16)
        wd[:, at] = mm(act_t[...], g, NN).astype(BF16)
        return 0

    lax.fori_loop(0, depth // tile, columns_of, 0)
    units, (pieces, _, piece) = wg.shape[0], grads_hbm.shape
    stores = [
        pltpu.make_async_copy(
            w.at[:, pl.ds(j * piece, piece)], grads_hbm.at[j, pl.ds(i * units, units)], store_sem.at[i, j]
        )
        for i, w in enumerate((wg, wu, wd))
        for j in range(pieces)
    ]
    for copy in stores:
        copy.start()
    scatter(chips - 1).wait_recv()
    ghn_ref[...] += ring_in[chips - 1].astype(F32)

    for copy in stores:
        copy.wait()
    for half in (0, 1):
        store(chips - 1, half).wait()
    for k in (chips - 2, chips - 1):
        pair(k).wait_send()
        scatter(k).wait_send()
    for k in range(chips):
        swap(k).wait_send()
    for k in range(chips - 1):
        ring(k).wait_send()


def feed_forward(links, hidden_own, grad_chunks, gate_t, up_t, down):
    own, depth = hidden_own.shape
    chips, units = links.chips, down.shape[0]
    seq = chips * 2 * own
    pieces = 2 * links.n_dp
    anywhere = pl.BlockSpec(memory_space=pl.ANY)
    dma = pltpu.SemaphoreType.DMA
    return pl.pallas_call(
        functools.partial(mlp_kernel, links),
        in_specs=[anywhere] * (4 + links.n_tensor),
        out_specs=[pl.BlockSpec(memory_space=pltpu.VMEM)] + [anywhere] * 2,
        out_shape=[
            jax.ShapeDtypeStruct((own, depth), F32),
            jax.ShapeDtypeStruct((chips, 2, own, depth), BF16),
            jax.ShapeDtypeStruct((pieces, 3 * units, depth // pieces), BF16),
        ],
        scratch_shapes=[
            pltpu.VMEM((chips, 2, own, depth), BF16),
            pltpu.VMEM((chips, 2, own, depth), BF16),
            pltpu.VMEM((units, depth), BF16),
            pltpu.VMEM((units, depth), BF16),
            pltpu.VMEM((units, depth), BF16),
            pltpu.VMEM((units, seq), BF16),
            pltpu.VMEM((units, seq), BF16),
            pltpu.VMEM((units, seq), BF16),
            pltpu.VMEM((own, depth), F32),
            pltpu.VMEM((2, own, depth), BF16),
            pltpu.VMEM((2, own, depth), BF16),
            pltpu.VMEM((2, own, depth), BF16),
            pltpu.VMEM((2, own, depth), BF16),
            pltpu.VMEM((chips, own, depth), BF16),
            dma((4 + links.n_tensor,)),
            dma((chips,)), dma((chips,)), dma((chips,)), dma((chips,)), dma((2,)), dma((2,)),
            dma((chips,)), dma((chips,)), dma((2,)), dma((3, pieces)),
        ],
        compiler_params=pltpu.CompilerParams(
            collective_id=1, has_side_effects=True, vmem_limit_bytes=60 * 2**20
        ),
        cost_estimate=pl.CostEstimate(
            flops=18 * seq * depth * units, bytes_accessed=64 * 2**20, transcendentals=seq * units
        ),
        name="feed_forward",
    )(hidden_own, gate_t, up_t, down, *grad_chunks)


def mesh_copy(src, dst, send, recv, peer):
    return pltpu.make_async_remote_copy(
        src_ref=src, dst_ref=dst, send_sem=send, recv_sem=recv, device_id=peer,
        device_id_type=pl.DeviceIdType.MESH,
    )


def add_into(dst, src, rows):
    band = max(b for b in range(16, 353, 16) if rows % b == 0)

    def step(i, _):
        at = pl.ds(pl.multiple_of(i * band, band), band)
        dst[at, :] = (dst[at, :].astype(F32) + src[at, :].astype(F32)).astype(BF16)
        return 0

    lax.fori_loop(0, rows // band, step, 0)


class DpSum:
    def __init__(self, links, send, me, buf, got, free, first=0):
        self.first = first
        self.links, self.send, self.me, self.buf, self.got, self.free = links, send, me, buf, got, free
        self.n = links.n_dp
        self.ways = [links.bits, links.bits[::-1]]
        self.pending = []

    def at(self, way, rel):
        return way * self.n + (self.me ^ rel)

    def kept(self, way, step):
        done = sum(self.ways[way][: step + 1])
        return [r for r in range(self.n) if r & done == 0]

    def first_slot(self, step):
        return sum(self.n >> (i + 1) for i in range(self.first, step))

    def peer(self, bit):
        return {"dp": self.me ^ bit}

    def start_halving(self, step):
        self.pending = []
        for rank in range(self.n >> (step + 1)):
            for way in (0, 1):
                bit = self.ways[way][step]
                rel = self.kept(way, step)[rank]
                slot = self.first_slot(step) + rank
                copy = self.send(self.buf.at[self.at(way, rel ^ bit)], self.got.at[way, slot], self.peer(bit), False)
                self.pending.append((copy, way, rel, slot))
        self.step = step

    def finish_halving(self):
        for copy, way, rel, slot in self.pending:
            copy.wait_recv()
            add_into(self.buf.at[self.at(way, rel)], self.got.at[way, slot], self.buf.shape[1])
        for copy, _, _, _ in self.pending:
            copy.wait_send()
        for way in (0, 1):
            pl.semaphore_signal(
                self.free.at[way, self.step], inc=1, device_id=self.peer(self.ways[way][self.step]),
                device_id_type=pl.DeviceIdType.MESH,
            )

    def start_doubling(self, step):
        self.pending = []
        if step >= self.first:
            for way in (0, 1):
                pl.semaphore_wait(self.free.at[way, step], 1)
        for rank in range(self.n >> (step + 1)):
            for way in (0, 1):
                bit = self.ways[way][step]
                rel = self.kept(way, step)[rank]
                where = self.buf.at[self.at(way, rel)]
                self.pending.append((self.send(where, where, self.peer(bit)), way, rel ^ bit))

    def finish_doubling(self):
        for copy, _, _ in self.pending:
            copy.wait_recv()
        return [(way, rel) for _, way, rel in self.pending]

    def chain(self, done):
        rounds = len(self.links.bits)
        for step in range(self.first, rounds):
            self.start_halving(step)
            yield
            self.finish_halving()
        for step in reversed(range(rounds)):
            self.start_doubling(step)
            if step == rounds - 1:
                done(0, 0)
                done(1, 0)
            yield
            for way, rel in self.finish_doubling():
                done(way, rel)


def first_halving(links, parts, me):
    n = links.n_dp
    out, names = [], []
    for way, bits in enumerate((links.bits, links.bits[::-1])):
        for rel in range(n):
            if rel & bits[0] == 0:
                mine = lax.dynamic_index_in_dim(parts, way * n + (me ^ rel), 0, keepdims=False)
                other = lax.dynamic_index_in_dim(parts, way * n + (me ^ rel ^ bits[0]), 0, keepdims=False)
                out.append((mine.astype(F32) + links.across(other, bits[0]).astype(F32)).astype(BF16))
                names.append((way, rel))
    return out, names


def tail_kernel(
    links, names, *refs,
):
    w_hbm, refs = refs[: len(names)], refs[len(names) :]
    (
        o_hbm, q_hbm, m_hbm, kv_keep, kv_send, gn_keep, gn_send, tokens, normed, w_kv, cosine, sine, gain_part,
        ws_hbm, ow_hbm, qw_hbm, kvw_hbm, got_hbm, gn_ref, gains_ref,
        o_buf, o_in, q_buf, q_in, w_buf, w_in, a_buf, a_in, b_buf, b_in,
        kv_got, kv_ring, kv_in, gn_got, kvw_half, kvw_got, kvw_in, kvw_all, gains_in,
        ss, rs, o_sem, q_sem, w_sem, out_sem, kvw_sem, w_free, a_free, b_free,
    ) = refs
    chips, bits = links.chips, links.bits
    n_dp = links.n_dp
    width = o_buf.shape[1]
    piece = w_buf.shape[2]
    me = lax.axis_index("tensor")
    me_dp = lax.axis_index("dp")
    chip, core = me // 2, lax.rem(me, 2)
    ahead, behind = links.neighbours(chip)
    right = {"tensor": ahead * 2 + core}
    left = {"tensor": behind * 2 + core}
    sibling = {"tensor": me ^ 1}
    chip_bits = [2 << b for b in range(chips.bit_length() - 1)]
    butterfly = [sibling] + [{"tensor": me ^ bit} for bit in chip_bits] + [{"dp": me_dp ^ bit} for bit in bits]

    w_loads = [
        pltpu.make_async_copy(ref, w_buf.at[way * n_dp + (me_dp ^ rel)], w_sem.at[i])
        for i, (ref, (way, rel)) in enumerate(zip(w_hbm, names))
    ]
    loads = {}
    for k in list(range(1, chips)) + [0]:
        loads["o", k] = pltpu.make_async_copy(o_hbm.at[k], o_buf.at[k], o_sem.at[k])
        loads["q", k] = pltpu.make_async_copy(q_hbm.at[k], q_buf.at[k], q_sem.at[k])
    for load in w_loads + list(loads.values()):
        load.start()
    barrier = pltpu.get_barrier_semaphore()
    peers = [right, left] + butterfly
    for peer in peers:
        pl.semaphore_signal(barrier, inc=1, device_id=peer, device_id_type=pl.DeviceIdType.MESH)
    pl.semaphore_wait(barrier, len(peers))

    copies, opened, locals_ = [], [], []

    def send(src, dst, peer, later=True):
        number = len(copies)
        copy = mesh_copy(src, dst, ss.at[number], rs.at[number], peer)
        copy.start()
        copies.append(copy)
        if later:
            opened.append(copy)
        return copy

    def put(src, dst):
        copy = pltpu.make_async_copy(src, dst, out_sem.at[len(locals_)])
        copy.start()
        locals_.append(copy)

    def ring_chain(name, buf, got):
        copy = None
        for k in list(range(1, chips)) + [0]:
            loads[name, k].wait()
            if copy is not None:
                copy.wait_recv()
                add_into(buf.at[k], got.at[(k - 1) % chips - 1], buf.shape[1])
            if k:
                copy = send(buf.at[k], got.at[k - 1], right)
            yield

    kv_swap = send(kv_send, kv_got, sibling)
    gn_swap = send(gn_send, gn_got, sibling)
    held = {}

    def kv_chain():
        kv_swap.wait_recv()
        copy = None
        for k in list(range(1, chips)) + [0]:
            total = kv_keep[k] + kv_got[k].astype(F32)
            if copy is not None:
                copy.wait_recv()
                total = total + kv_in[(k - 1) % chips - 1].astype(F32)
            if k:
                kv_ring[k - 1] = total.astype(BF16)
                copy = send(kv_ring.at[k - 1], kv_in.at[k - 1], right)
                yield
        key_grad = total[:, :HD]
        key_grad = key_grad * cosine[...] - pltpu.roll(key_grad, HD // 2, 1) * sine[...]
        kv_lin = jnp.concatenate([key_grad, total[:, HD:]], axis=1).astype(BF16)
        kv_lin_t = kv_lin.T
        for half in (0, 1):
            kvw_half[half] = mm(kv_lin_t[half * HD : (half + 1) * HD], normed[...], NN).astype(BF16)
        held["swap"] = send(kvw_half.at[1 - core], kvw_got, sibling)
        yield
        gn_swap.wait_recv()
        grad = gn_keep[...] + gn_got[...].astype(F32) + mm(kv_lin, w_kv[...], NT)
        gn_ref[...] = grad
        x = tokens[...].astype(F32)
        factor = lax.rsqrt(jnp.mean(x * x, axis=1, keepdims=True) + EPSILON)
        part = jnp.sum(grad * (x * factor), axis=0, keepdims=True)
        row = lax.broadcasted_iota(jnp.int32, gains_ref.shape, 0)
        gains_ref[...] = jnp.where(row == 0, jnp.broadcast_to(part, gains_ref.shape), gain_part[...])

    def gains_chain():
        for number, peer in enumerate(butterfly):
            copy = send(gains_ref, gains_in.at[number], peer, False)
            yield
            copy.wait_recv()
            copy.wait_send()
            gains_ref[...] += gains_in[number]

    band = HD // chips

    def chip_up(k):
        found = chip * 0
        for i, c in enumerate(links.order):
            found = jnp.where(chip == c, links.order[(i - k) % chips], found)
        return found

    def rows_of(k):
        return pl.ds(pl.multiple_of(chip_up(k) * band, band), band)

    def kvw_chain():
        held["swap"].wait_recv()
        add_into(kvw_half.at[core], kvw_got, HD)
        copy = None
        for k in list(range(1, chips)) + [0]:
            if copy is not None:
                copy.wait_recv()
                mine = kvw_half.at[core, rows_of(k)]
                mine[...] = (mine[...].astype(F32) + kvw_in[(k - 1) % chips - 1].astype(F32)).astype(BF16)
            if k:
                copy = send(kvw_half.at[core, rows_of(k)], kvw_in.at[k - 1], right)
                yield

    sum_w = DpSum(links, send, me_dp, w_buf, w_in, w_free, 1)
    sum_a = DpSum(links, send, me_dp, a_buf, a_in, a_free)
    sum_b = DpSum(links, send, me_dp, b_buf, b_in, b_free)

    def columns(ref, number):
        return ref.at[:, pl.ds(pl.multiple_of(number * piece, piece), piece)]

    def w_chain():
        for load in w_loads:
            load.wait()
        yield from sum_w.chain(lambda way, rel: put(w_buf.at[sum_w.at(way, rel)], columns(ws_hbm, sum_w.at(way, rel))))

    def a_chain():
        for j in range(2 * n_dp):
            a_buf[j, pl.ds(0, width)] = o_buf[0, :, pl.ds(j * piece, piece)]
            a_buf[j, pl.ds(width, band)] = kvw_half[core, rows_of(0), pl.ds(j * piece, piece)]
        yield from sum_a.chain(
            lambda way, rel: put(
                a_buf.at[sum_a.at(way, rel), pl.ds(0, width)], columns(ow_hbm, sum_a.at(way, rel))
            )
        )

    def last_chain():
        for j in range(2 * n_dp):
            kvw_all[0, core, :, pl.ds(j * piece, piece)] = a_buf[j, pl.ds(width, band)]
        for k in range(chips - 1):
            copy = send(kvw_all.at[k, core], kvw_all.at[k + 1, core], right)
            yield
            copy.wait_recv()
        copy = send(kvw_all.at[:, core], kvw_all.at[:, core], sibling)
        yield
        copy.wait_recv()
        for k in range(chips):
            for half in (0, 1):
                to = pl.ds(pl.multiple_of(half * HD + chip_up(k) * band, band), band)
                put(kvw_all.at[k, half], kvw_hbm.at[to])

    def b_chain():
        for j in range(2 * n_dp):
            b_buf[j] = q_buf[0, :, pl.ds(j * piece, piece)]
        yield from sum_b.chain(lambda way, rel: put(b_buf.at[sum_b.at(way, rel)], columns(qw_hbm, sum_b.at(way, rel))))

    def m_chain():
        copy = send(m_hbm, got_hbm, right)
        yield
        copy.wait_recv()

    chains = {
        "w": w_chain(), "o": ring_chain("o", o_buf, o_in), "q": ring_chain("q", q_buf, q_in), "kv": kv_chain(),
        "g": gains_chain(), "kvw": kvw_chain(), "m": m_chain(), "a": a_chain(), "b": b_chain(), "l": last_chain(),
    }

    take_turns(chains, TAIL_ORDER)
    for copy in opened:
        copy.wait_send()
    for copy in locals_:
        copy.wait()


TAIL_ORDER = (
    "w o kv kv", "q kv kv o", "kv* kvw g w", "q kvw g w", "o kvw g kvw*", "g q g m", "o* a g* q*", "a b a b",
    "a b a* l", "b l b l", "b* l* w* m*",
)


def tail(
    links, o_parts, q_parts, m_part, w_pieces, names, kv_keep, kv_send, gn_keep, gn_send, tokens, normed, w_kv, cosine,
    sine, gain_part,
):
    chips, width, depth = o_parts.shape
    own = tokens.shape[0]
    rows, piece = w_pieces[0].shape
    band = HD // chips
    n = links.n_dp
    pieces = 2 * n
    anywhere = pl.BlockSpec(memory_space=pl.ANY)
    here = pl.BlockSpec(memory_space=pltpu.VMEM)
    dma = pltpu.SemaphoreType.DMA
    shape = jax.ShapeDtypeStruct
    count = 16 * chips + 6 * n * 2 + 16
    return pl.pallas_call(
        functools.partial(tail_kernel, links, names),
        in_specs=[anywhere] * (3 + len(names)) + [here] * 10,
        out_specs=[anywhere] * 5 + [here] * 2,
        out_shape=[
            shape((rows, depth), BF16), shape((width, depth), BF16),
            shape((width, depth), BF16), shape((2 * HD, depth), BF16), shape((own, depth), BF16),
            shape((own, depth), F32), shape((8, depth), F32),
        ],
        scratch_shapes=[
            pltpu.VMEM((chips, width, depth), BF16), pltpu.VMEM((chips - 1, width, depth), BF16),
            pltpu.VMEM((chips, width, depth), BF16), pltpu.VMEM((chips - 1, width, depth), BF16),
            pltpu.VMEM((pieces, rows, piece), BF16), pltpu.VMEM((2, max(1, n // 2 - 1), rows, piece), BF16),
            pltpu.VMEM((pieces, width + band, piece), BF16), pltpu.VMEM((2, n - 1, width + band, piece), BF16),
            pltpu.VMEM((pieces, width, piece), BF16), pltpu.VMEM((2, n - 1, width, piece), BF16),
            pltpu.VMEM((chips, own, 2 * HD), BF16),
            pltpu.VMEM((chips - 1, own, 2 * HD), BF16), pltpu.VMEM((chips - 1, own, 2 * HD), BF16),
            pltpu.VMEM((own, depth), BF16),
            pltpu.VMEM((2, HD, depth), BF16), pltpu.VMEM((HD, depth), BF16),
            pltpu.VMEM((chips - 1, band, depth), BF16),
            pltpu.VMEM((chips, 2, band, depth), BF16),
            pltpu.VMEM((len(links.bits) + chips.bit_length(), 8, depth), F32),
            dma((count,)), dma((count,)), dma((chips,)), dma((chips,)), dma((len(names),)),
            dma((3 * pieces + 2 * chips,)), dma((chips, 2)),
        ]
        + [pltpu.SemaphoreType.REGULAR((2, len(links.bits)))] * 3,
        compiler_params=pltpu.CompilerParams(
            collective_id=2, has_side_effects=True, vmem_limit_bytes=60 * 2**20
        ),
        cost_estimate=pl.CostEstimate(flops=10**9, bytes_accessed=64 * 2**20, transcendentals=0),
        name="tail",
    )(
        *w_pieces, o_parts, q_parts, m_part, kv_keep, kv_send, gn_keep, gn_send, tokens, normed, w_kv, cosine, sine,
        gain_part,
    )


def rms_factor(values):
    return lax.rsqrt(jnp.mean(values * values, axis=-1, keepdims=True) + EPSILON)


def local(
    n_tensor, n_dp,
    tokens, out_grad, query_two, grad_two, doc_split, attn_gain, mlp_gain, w_query, w_kv, w_out, w_gate, w_up, w_down,
):
    links = Links(n_tensor, n_dp)
    chips = links.chips
    own = tokens.shape[0]
    rows = 2 * own
    seq = own * n_tensor
    width = w_query.shape[1]
    me_dp = lax.axis_index("dp")
    me_t = lax.axis_index("tensor")
    chip, core = me_t // 2, me_t % 2
    two_docs = doc_split[0]
    sp = jnp.stack([chip, two_docs, core]).astype(jnp.int32)
    place = jnp.array(links.place, jnp.int32)
    order = jnp.array(links.order, jnp.int32)

    spot = jnp.arange(rows, dtype=jnp.int32) + core * own
    spot = chip * rows + jnp.where(spot >= rows, spot - rows, spot)
    position = jnp.where(two_docs > 0, spot % SEQ_SHORT, spot)
    frequency = 10000.0 ** (-jnp.arange(HD // 2, dtype=F32) * 2.0 / HD)
    phases = position.astype(F32)[:, None] * frequency[None, :]
    cos, sin = jnp.cos(phases), jnp.sin(phases)
    cosine = jnp.concatenate([cos, cos], axis=1)
    sine = jnp.concatenate([-sin, sin], axis=1)

    residual = tokens.astype(F32)
    attn_scale = rms_factor(residual)
    attn_pre = residual * attn_scale

    normed, wq, wo, og_up, og_pair, og_up_pair, kv_all, key_rows_t, dk2, dv2 = front(
        links, doc_split, tokens, attn_gain[None], w_kv, cosine[:own], sine[:own], query_two, grad_two, w_query, w_out,
        out_grad,
    )
    normed_own = normed[:own]
    grad_chunks = [out_grad, og_pair, og_up, og_up_pair]
    for _ in range(2, chips):
        og_up = links.ring(og_up)
        grad_chunks += [og_up, links.swap(og_up)]

    q_lin = mm(normed, wq, NN)
    queries, context, lse = attend(sp, q_lin, cosine, sine, kv_all)
    branch = pair_sum(links, mm(context, wo, NN))
    hidden = residual + branch
    mlp_scale = rms_factor(hidden)
    mlp_pre = hidden * mlp_scale
    hidden_own = (mlp_pre * mlp_gain).astype(BF16)

    grad_hn, mlp_parts, ffn_parts = feed_forward(links, hidden_own, grad_chunks, w_gate.T, w_up.T, w_down)
    ffn_pieces, ffn_names = first_halving(links, ffn_parts, me_dp)
    mlp_terms = mlp_parts[:, 0].astype(F32) + links.swap(mlp_parts[:, 1]).astype(F32)
    mlp_sent = mlp_terms[1].astype(BF16)
    for k in range(2, chips):
        mlp_sent = (mlp_terms[k] + links.ring(mlp_sent).astype(F32)).astype(BF16)

    mlp_gain_part = jnp.sum(grad_hn * mlp_pre, axis=0)
    scaled_mlp = grad_hn * mlp_gain
    grad_hidden = out_grad.astype(F32) + mlp_scale * (
        scaled_mlp - mlp_pre * jnp.mean(scaled_mlp * mlp_pre, axis=-1, keepdims=True)
    )

    grad_branch = both(links, grad_hidden.astype(BF16))
    grad_context = mm(grad_branch, wo, NT).astype(BF16)
    query_grad, dk, dv = attend_back(
        sp, queries, grad_context, context, lse, cosine, sine, kv_all, key_rows_t, dk2, dv2
    )
    out_parts = mm(context, grad_branch, TN).astype(BF16).reshape(chips, width, -1)
    query_parts = mm(query_grad, normed, TN).astype(BF16).reshape(chips, width, -1)

    kv_part = jnp.concatenate([dk * SCALE, dv], axis=1).reshape(chips, 2, own, 2 * HD)
    kv_part = jnp.stack(
        [
            lax.dynamic_index_in_dim(kv_part, order[(place[chip] - k + chips) % chips], 0, keepdims=False)
            for k in range(chips)
        ]
    )
    kv_keep = lax.dynamic_index_in_dim(kv_part, core, 1, keepdims=False)
    kv_send = lax.dynamic_index_in_dim(kv_part, 1 - core, 1, keepdims=False).astype(BF16)
    gn_part = mm(query_grad, wq, NT)
    gain_part = jnp.pad(mlp_gain_part[None], ((1, 6), (0, 0)))
    ffn_w, out_w, query_w, kv_w, mlp_got, grad_normed, gains = tail(
        links, out_parts, query_parts, mlp_sent, ffn_pieces, ffn_names, kv_keep, kv_send, gn_part[:own],
        gn_part[own:].astype(BF16), tokens, normed_own, w_kv, cosine[:own], sine[:own], gain_part,
    )
    units = w_down.shape[0]

    gate_w_grad = ffn_w[:units].astype(F32).T
    up_w_grad = ffn_w[units : 2 * units].astype(F32).T
    down_w_grad = ffn_w[2 * units :].astype(F32)
    out_w_grad = out_w.astype(F32)
    query_w_grad = query_w.astype(F32).T
    kv_w_grad = kv_w.astype(F32).T
    attn_gain_grad, mlp_gain_grad = gains[0], gains[1]
    block_output = (hidden + (mlp_terms[0] + mlp_got.astype(F32))).astype(BF16)
    scaled_attn = grad_normed * attn_gain
    tokens_grad = (
        grad_hidden
        + attn_scale * (scaled_attn - attn_pre * jnp.mean(scaled_attn * attn_pre, axis=-1, keepdims=True))
    ).astype(BF16)
    return (
        block_output,
        tokens_grad,
        attn_gain_grad,
        mlp_gain_grad,
        query_w_grad,
        kv_w_grad,
        out_w_grad,
        gate_w_grad,
        up_w_grad,
        down_w_grad,
    )


def solution(mesh):
    both_axes = P(("dp", "tensor"), None)
    return jax.shard_map(
        functools.partial(local, mesh.shape["tensor"], mesh.shape["dp"]),
        mesh=mesh,
        in_specs=(
            both_axes,
            both_axes,
            P("dp", "tensor"),
            P("dp", "tensor"),
            P("dp"),
            P(),
            P(),
            P(None, "tensor"),
            P(),
            P("tensor", None),
            P(None, "tensor"),
            P(None, "tensor"),
            P("tensor", None),
        ),
        out_specs=(
            both_axes,
            both_axes,
            P(),
            P(),
            P(None, "tensor"),
            P(),
            P("tensor", None),
            P(None, "tensor"),
            P(None, "tensor"),
            P("tensor", None),
        ),
        check_vma=False,
    )
```

```python
import functools

import jax
import jax.numpy as jnp
from jax import lax
from jax.experimental import pallas as pl
from jax.experimental.pallas import tpu as pltpu
from jax.sharding import PartitionSpec as P

HD = 128
SEQ_SHORT = 1024
EPSILON = 1e-05
MASKED = -1e30
SCALE = HD ** (-0.5)
SCALE2 = SCALE * 1.4426950408889634
F32 = jnp.float32
BF16 = jnp.bfloat16
VMEM_LIMIT = 56 * 2**20


def mm(left, right, dims):
    return lax.dot_general(left, right, (dims, ((), ())), preferred_element_type=F32)


NN = ((1,), (0,))
NT = ((1,), (1,))
TN = ((0,), (0,))


class Links:
    def __init__(self, n_tensor, n_dp):
        self.n_tensor, self.n_dp = n_tensor, n_dp
        self.chips = n_tensor // 2
        odd = list(range(1, self.chips, 2))
        even = list(range(2, self.chips, 2))
        self.order = [0] + odd + even[::-1]
        nxt = {c: self.order[(i + 1) % self.chips] for i, c in enumerate(self.order)}
        self.place = [self.order.index(c) for c in range(self.chips)]
        self.ring_pairs = [(2 * c + k, 2 * nxt[c] + k) for c in range(self.chips) for k in (0, 1)]
        self.swap_pairs = [(i, i ^ 1) for i in range(n_tensor)]
        self.bits = [1 << b for b in range(n_dp.bit_length() - 1)]

    def ring(self, x):
        return lax.ppermute(x, "tensor", self.ring_pairs)

    def swap(self, x):
        return lax.ppermute(x, "tensor", self.swap_pairs)

    def across(self, x, bit):
        return lax.ppermute(x, "dp", [(i, i ^ bit) for i in range(self.n_dp)])

    def across_tensor(self, x, bit):
        return lax.ppermute(x, "tensor", [(i, i ^ bit) for i in range(self.n_tensor)])

    def neighbours(self, chip):
        ahead, behind = chip * 0, chip * 0
        for i, c in enumerate(self.order):
            ahead = jnp.where(chip == c, self.order[(i + 1) % self.chips], ahead)
            behind = jnp.where(chip == c, self.order[i - 1], behind)
        return ahead, behind

    def orders(self, rows, unit):
        ways = len(self.bits)
        if ways < 2 or rows % (ways * unit):
            return [self.bits]
        return [self.bits[i:] + self.bits[:i] for i in range(ways)]


def take_rows(x, index, size):
    return lax.dynamic_slice_in_dim(x, index * size, size, 0)


def gather_dp(links, piece, me):
    orders = links.orders(piece.shape[0], 8)
    part_rows = piece.shape[0] // len(orders)
    parts = []
    for number, bits in enumerate(orders):
        stack = lax.slice_in_dim(piece, number * part_rows, (number + 1) * part_rows, axis=0)
        held = [0]
        for bit in bits:
            stack = jnp.concatenate([stack, links.across(stack, bit)], axis=0)
            held = held + [h ^ bit for h in held]
        where = jnp.array([held.index(rel) for rel in range(links.n_dp)], jnp.int32)
        parts.append((stack, where))
    out = []
    for j in range(links.n_dp):
        for stack, where in parts:
            out.append(take_rows(stack, where[me ^ j], part_rows))
    return jnp.concatenate(out, axis=0)


def gather_weight(links, block, me):
    rows = block.shape[0] // links.n_dp
    blocks = [block]
    piece = take_rows(block, me, rows)
    for _ in range(links.chips - 1):
        piece = links.ring(piece)
        blocks.append(gather_dp(links, piece, me))
    return blocks


def sum_dp(links, x, me):
    orders = links.orders(x.shape[0], 8 * links.n_dp)
    part_rows = x.shape[0] // len(orders)
    size = part_rows // links.n_dp
    outs = []
    for number, bits in enumerate(orders):
        held = lax.slice_in_dim(x, number * part_rows, (number + 1) * part_rows, axis=0)
        pieces = [held.reshape((links.n_dp, size) + x.shape[1:])]
        array = pieces[0]
        axes = [links.n_dp]
        nbits = len(links.bits)
        array = array.reshape((2,) * nbits + (size,) + x.shape[1:])
        left = list(reversed(links.bits))
        for bit in bits:
            axis = left.index(bit)
            mine = jnp.minimum(me & bit, 1)
            keep = lax.dynamic_index_in_dim(array, mine, axis, keepdims=False)
            send = lax.dynamic_index_in_dim(array, 1 - mine, axis, keepdims=False)
            got = links.across(send, bit)
            array = (keep.astype(F32) + got.astype(F32)).astype(BF16)
            left.remove(bit)
        stack = array.reshape((size,) + x.shape[1:])
        rel = [0]
        for bit in reversed(bits):
            stack = jnp.concatenate([stack, links.across(stack, bit)], axis=0)
            rel = rel + [r ^ bit for r in rel]
        where = jnp.array([rel.index(r) for r in range(links.n_dp)], jnp.int32)
        for j in range(links.n_dp):
            outs.append(take_rows(stack, where[me ^ j], size))
    return jnp.concatenate(outs, axis=0).astype(F32)


def ring_gather(links, own):
    out = [own]
    for _ in range(links.chips - 1):
        out.append(links.ring(out[-1]))
    return out


def ring_scatter(links, terms):
    got = None
    for term in terms[1:] + terms[:1]:
        total = term if got is None else term.astype(F32) + got.astype(F32)
        if term is terms[0]:
            return total.astype(F32)
        got = links.ring(total.astype(BF16))
    return got


def both(links, own):
    return jnp.concatenate([own, links.swap(own)], axis=0)


def pair_sum(links, part):
    rows = part.shape[0] // 2
    return part[:rows].astype(F32) + links.swap(part[rows:].astype(BF16)).astype(F32)


def sum_all(links, x):
    bit = 1
    while bit < links.n_tensor:
        x = x + links.across_tensor(x, bit)
        bit *= 2
    for bit in links.bits:
        x = x + links.across(x, bit)
    return x


def diagonal(shape, row_axis, shift):
    size = shape[row_axis]
    row = lax.broadcasted_iota(jnp.int32, shape, row_axis) + shift
    row = jnp.where(row >= size, row - size, row)
    return lax.broadcasted_iota(jnp.int32, shape, 1 - row_axis) <= row


def span(block, two_docs, rows):
    per_doc = SEQ_SHORT // rows
    inner = jnp.where(two_docs > 0, lax.rem(block, per_doc), block)
    return inner + 1, pl.multiple_of((block - inner) * rows, rows)


def fwd_kernel(blocks, sp_ref, q_ref, c_ref, s_ref, k_ref, v_ref, qo_ref, ctx_ref, lse_ref):
    rows = q_ref.shape[0]
    chip, two_docs, core = sp_ref[0], sp_ref[1], sp_ref[2]
    x = q_ref[...]
    q = (x * c_ref[...] + pltpu.roll(x, HD // 2, 1) * s_ref[...]).astype(BF16)
    qo_ref[...] = q
    count, low = span(chip, two_docs, rows)
    mask = diagonal((rows, rows), 0, core * (rows // 2))
    for n in range(1, blocks + 1):

        @pl.when(count == n)
        def _(n=n):
            near = (n - 1) * rows
            diag = pl.ds(low + near, rows)
            s_diag = jnp.where(mask, mm(q, k_ref[diag, :], NT) * SCALE2, MASKED)
            top = jnp.max(s_diag, axis=1, keepdims=True)
            if n > 1:
                main = pl.ds(low, near)
                s_main = mm(q, k_ref[main, :], NT) * SCALE2
                top = jnp.maximum(top, jnp.max(s_main, axis=1, keepdims=True))
            p_diag = jnp.exp2(s_diag - top)
            total = jnp.sum(p_diag, axis=1, keepdims=True)
            out = mm(p_diag.astype(BF16), v_ref[diag, :], NN)
            if n > 1:
                p_main = jnp.exp2(s_main - top)
                total = total + jnp.sum(p_main, axis=1, keepdims=True)
                out = out + mm(p_main.astype(BF16), v_ref[main, :], NN)
            ctx_ref[...] = (out / total).astype(BF16)
            lse = jnp.broadcast_to(top + jnp.log2(total), (rows, HD))
            lse_ref[0] = lse.T[:8]


def bwd_kernel(
    blocks, sp_ref, q_ref, do_ref, ctx_ref, lse_ref, c_ref, s_ref, k_ref, kt_ref, v_ref, dk0_ref, dv0_ref,
    dq_ref, dk_ref, dv_ref,
):
    rows = q_ref.shape[0]
    chip, two_docs, core = sp_ref[0], sp_ref[1], sp_ref[2]

    @pl.when(pl.program_id(0) == 0)
    def _():
        dk_ref[...] = dk0_ref[...]
        dv_ref[...] = dv0_ref[...]

    q, do = q_ref[...], do_ref[...]
    dot = jnp.sum(do.astype(F32) * ctx_ref[...].astype(F32), axis=1, keepdims=True)
    dot = jnp.broadcast_to(dot, (rows, HD)).T[:1]
    lse = lse_ref[0, :1]
    count, low = span(chip, two_docs, rows)
    mask = diagonal((rows, rows), 1, core * (rows // 2))
    for n in range(1, blocks + 1):

        @pl.when(count == n)
        def _(n=n):
            near = (n - 1) * rows
            dqt = jnp.zeros((HD, rows), F32)
            for keys, masked in ((pl.ds(low, near), False), (pl.ds(low + near, rows), True)):
                if not masked and n == 1:
                    continue
                p = jnp.exp2(mm(k_ref[keys, :], q, NT) * SCALE2 - lse)
                if masked:
                    p = jnp.where(mask, p, 0.0)
                ds = (p * (mm(v_ref[keys, :], do, NT) - dot)).astype(BF16)
                dv_ref[keys, :] += mm(p.astype(BF16), do, NN)
                dk_ref[keys, :] += mm(ds, q, NN)
                dqt = dqt + mm(kt_ref[:, keys], ds, NN)
            g = dqt.T * SCALE
            dq_ref[...] = (g * c_ref[...] - pltpu.roll(g, HD // 2, 1) * s_ref[...]).astype(BF16)


def whole(shape):
    return pl.BlockSpec(shape, lambda *_: (0,) * len(shape))


def second_half(seq):
    return pl.BlockSpec((seq, HD), lambda *_: (0, 1))


def attend(sp, q_lin, cosine, sine, kv_all):
    rows, width = q_lin.shape
    seq = kv_all.shape[0]
    heads = width // HD
    column = pl.BlockSpec((rows, HD), lambda h, *_: (0, h))
    return pl.pallas_call(
        functools.partial(fwd_kernel, seq // rows),
        grid_spec=pltpu.PrefetchScalarGridSpec(
            num_scalar_prefetch=1,
            grid=(heads,),
            in_specs=[column, whole((rows, HD)), whole((rows, HD)), whole((seq, HD)), second_half(seq)],
            out_specs=[column, column, pl.BlockSpec((1, 8, rows), lambda h, *_: (h, 0, 0))],
        ),
        out_shape=[
            jax.ShapeDtypeStruct((rows, width), BF16),
            jax.ShapeDtypeStruct((rows, width), BF16),
            jax.ShapeDtypeStruct((heads, 8, rows), F32),
        ],
        compiler_params=pltpu.CompilerParams(vmem_limit_bytes=VMEM_LIMIT),
        cost_estimate=pl.CostEstimate(
            flops=8 * heads * rows * seq * HD, bytes_accessed=16 * rows * width, transcendentals=heads * rows * seq
        ),
        name="attend",
    )(sp, q_lin, cosine, sine, kv_all, kv_all)


def attend_back(sp, queries, grad_context, context, lse, cosine, sine, kv_all, key_rows_t, dk0, dv0):
    rows, width = queries.shape
    seq = kv_all.shape[0]
    heads = width // HD
    column = pl.BlockSpec((rows, HD), lambda h, *_: (0, h))
    return pl.pallas_call(
        functools.partial(bwd_kernel, seq // rows),
        grid_spec=pltpu.PrefetchScalarGridSpec(
            num_scalar_prefetch=1,
            grid=(heads,),
            in_specs=[
                column, column, column, pl.BlockSpec((1, 8, rows), lambda h, *_: (h, 0, 0)),
                whole((rows, HD)), whole((rows, HD)), whole((seq, HD)), whole((HD, seq)), second_half(seq),
                whole((seq, HD)), whole((seq, HD)),
            ],
            out_specs=[column, whole((seq, HD)), whole((seq, HD))],
        ),
        out_shape=[
            jax.ShapeDtypeStruct((rows, width), BF16),
            jax.ShapeDtypeStruct((seq, HD), F32),
            jax.ShapeDtypeStruct((seq, HD), F32),
        ],
        compiler_params=pltpu.CompilerParams(vmem_limit_bytes=VMEM_LIMIT),
        cost_estimate=pl.CostEstimate(
            flops=20 * heads * rows * seq * HD, bytes_accessed=16 * rows * width, transcendentals=heads * rows * seq
        ),
        name="attend_back",
    )(sp, queries, grad_context, context, lse, cosine, sine, kv_all, key_rows_t, kv_all, dk0, dv0)


def second_unit(block, rows, q, do, kv, dk_ref, dv_ref, late):
    mask = diagonal((rows, rows), 1, 0)
    first = block * rows
    parts = [(pl.ds(first, rows), True, False)]
    middle = SEQ_SHORT * (first // SEQ_SHORT)
    if first > middle:
        parts.append((pl.ds(middle, first - middle), False, False))
    if middle:
        parts.append((pl.ds(0, middle), False, True))
    scores = []
    for keys, masked, far in parts:
        score = mm(kv[keys, :HD], q, NT) * SCALE2
        scores.append(jnp.where(mask, score, MASKED) if masked else score + late if far else score)
    top = functools.reduce(jnp.maximum, [jnp.max(score, axis=0, keepdims=True) for score in scores])
    lifted = [jnp.exp2(score - top) for score in scores]
    inverse = 1.0 / sum(jnp.sum(p, axis=0, keepdims=True) for p in lifted)
    back = [mm(kv[keys, HD:], do, NT) for keys, _, _ in parts]
    dot = sum(jnp.sum(p * b, axis=0, keepdims=True) for p, b in zip(lifted, back)) * inverse
    for (keys, _, _), p, b in zip(parts, lifted, back):
        p = p * inverse
        dv_ref[keys, :] += mm(p.astype(BF16), do, NN)
        dk_ref[keys, :] += mm((p * (b - dot)).astype(BF16), q, NN)


FRONT_HOPS = 1
FRONT_ORDER = (
    "kv q1 o1 kv", "q1 q2 o1 o2", "kv q1 q2 q3", "kv o1 o2 o3", "g kv* s q2", "q3 s o2 o3", "s g q2 q3",
    "s o2 o3 s", "q3 s g s", "o3 s q1* o1*", "q2* o2* q3* o3*", "s* g*",
)


def front_kernel(
    links, docs, tokens, gain, w_kv, cosine, sine, q_two, g_two, wq_hbm, wo_hbm, og_hbm,
    normed, wq_out, wo_out, kv_out, kt_ref, dk_ref, dv_ref, *refs,
):
    og_outs, (kv, ss, rs, ls) = refs[:-4], refs[-4:]
    chips, bits, n_dp = links.chips, links.bits, links.n_dp
    own, depth = tokens.shape
    seq = own * links.n_tensor
    width = wq_hbm.shape[1]
    me = lax.axis_index("tensor")
    me_dp = lax.axis_index("dp")
    chip, core = me // 2, lax.rem(me, 2)
    ahead, behind = links.neighbours(chip)
    right = {"tensor": ahead * 2 + core}
    left = {"tensor": behind * 2 + core}
    sibling = {"tensor": me ^ 1}
    barrier = pltpu.get_barrier_semaphore()
    peers = [right, left, sibling] + [{"dp": me_dp ^ bit} for bit in bits]
    for peer in peers:
        pl.semaphore_signal(barrier, inc=1, device_id=peer, device_id_type=pl.DeviceIdType.MESH)

    copies = []

    def send(src, dst, peer):
        number = len(copies)
        copy = mesh_copy(src, dst, ss.at[number], rs.at[number], peer)
        copy.start()
        copies.append(copy)
        return copy

    def q_piece(ref, k, j, way, size=1):
        rows = depth // n_dp // 2
        at = pl.ds(pl.multiple_of((2 * j + way) * rows, rows), size * rows)
        return ref.at[at, :] if k is None else ref.at[at, pl.ds(k * width, width)]

    def o_piece(ref, k, j, way, size=1):
        rows, half = width // n_dp, depth // 2
        at = pl.ds(pl.multiple_of((k or 0) * width + j * rows, rows), rows)
        return ref.at[at, pl.ds(way * half, size * half)]

    pl.semaphore_wait(barrier, len(peers))
    locals_ = [
        pltpu.make_async_copy(wq_hbm, wq_out.at[:, pl.ds(0, width)], ls.at[0]),
        pltpu.make_async_copy(wo_hbm, wo_out.at[pl.ds(0, width), :], ls.at[1]),
    ]
    for copy in locals_:
        copy.start()
    hops = {}
    for name, piece, src, dst in (("q", q_piece, wq_hbm, wq_out), ("o", o_piece, wo_hbm, wo_out)):
        hops[name, 1] = send(piece(src, None, me_dp, 0, 2), piece(dst, 1, me_dp, 0, 2), right)

    x = tokens[...].astype(F32)
    own_rows = pl.ds(0, own)
    normed[own_rows] = (x * lax.rsqrt(jnp.mean(x * x, axis=1, keepdims=True) + EPSILON) * gain[...]).astype(BF16)
    normed_swap = send(normed.at[own_rows], normed.at[pl.ds(own, own)], sibling)
    lin = mm(normed[own_rows], w_kv[...], NN)
    key = lin[:, :HD] * cosine[...] + pltpu.roll(lin[:, :HD], HD // 2, 1) * sine[...]

    def chip_up(k):
        found = chip * 0
        for i, c in enumerate(links.order):
            found = jnp.where(chip == c, links.order[(i - k) % chips], found)
        return found

    def kv_at(k):
        return kv.at[pl.ds(pl.multiple_of((chip_up(k) * 2 + core) * own, own), own)]

    kv_at(0)[...] = jnp.concatenate([key, lin[:, HD:]], axis=1).astype(BF16)
    late = jnp.where(docs[0] > 0, MASKED, 0.0)
    dk_ref[...] = jnp.zeros_like(dk_ref)
    dv_ref[...] = jnp.zeros_like(dv_ref)

    def kv_chain():
        swaps = []
        for k in range(chips):
            copy = send(kv_at(k), kv_at(k), right) if k + 1 < chips else None
            swaps.append(send(kv_at(k), kv_at(k), sibling))
            yield
            if copy is not None:
                copy.wait_recv()
        for copy in swaps:
            copy.wait_recv()
        store = pltpu.make_async_copy(kv, kv_out, ls.at[2])
        store.start()
        locals_.append(store)
        kt_ref[...] = kv[:, :HD].T

    def block_chain(name, piece, dst, k):
        hops[name, k].wait_recv()
        if k + 1 < chips:
            hops[name, k + 1] = send(piece(dst, k, me_dp, 0, 2), piece(dst, k + 1, me_dp, 0, 2), right)
        held = [[0], [0]]
        for step in range(len(bits)):
            sent = []
            for rank in range(len(held[0])):
                for way, order in enumerate((bits, bits[::-1])):
                    bit, rel = order[step], held[way][rank]
                    where = piece(dst, k, me_dp ^ rel, way)
                    sent.append((send(where, where, {"dp": me_dp ^ bit}), way, rel ^ bit))
            yield
            for copy, way, rel in sent:
                copy.wait_recv()
                held[way].append(rel)

    def grad_chain():
        source = og_hbm
        swaps = [send(og_hbm, og_outs[0], sibling)]
        for i in range(1, len(og_outs), 2):
            hop = send(source, og_outs[i], right)
            yield
            hop.wait_recv()
            source = og_outs[i]
            swaps.append(send(source, og_outs[i + 1], sibling))
        yield
        for copy in swaps:
            copy.wait_recv()

    rows = min(512, SEQ_SHORT)
    heads = q_two.shape[1] // HD

    def second_chain():
        for block in reversed(range(seq // rows)):
            for head in range(heads):
                at = (pl.ds(block * rows, rows), pl.ds(head * HD, HD))
                second_unit(block, rows, q_two[at], g_two[at], kv, dk_ref, dv_ref, late)
                yield

    chains = {"kv": kv_chain(), "s": second_chain(), "g": grad_chain()}
    for k in range(1, chips):
        chains["q%d" % k] = block_chain("q", q_piece, wq_out, k)
        chains["o%d" % k] = block_chain("o", o_piece, wo_out, k)
    take_turns(chains, FRONT_ORDER)
    normed_swap.wait_recv()
    for copy in copies:
        copy.wait_send()
    for copy in locals_:
        copy.wait()


def take_turns(chains, order):
    def turn(name):
        if name in chains and next(chains[name], chains) is chains:
            del chains[name]

    for name in " ".join(order).split():
        turn(name.rstrip("*"))
        while name.endswith("*") and name.rstrip("*") in chains:
            turn(name.rstrip("*"))
    while chains:
        for name in list(chains):
            turn(name)


def front(links, docs, tokens, gain, w_kv, cosine, sine, q_two, g_two, w_query, w_out, out_grad):
    chips = links.chips
    own, depth = tokens.shape
    seq = own * links.n_tensor
    width = w_query.shape[1]
    anywhere = pl.BlockSpec(memory_space=pl.ANY)
    here = pl.BlockSpec(memory_space=pltpu.VMEM)
    dma = pltpu.SemaphoreType.DMA
    shape = jax.ShapeDtypeStruct
    count = 2 * chips * (2 * links.n_dp) + 4 * chips + 8
    hops = min(FRONT_HOPS, chips - 1)
    return pl.pallas_call(
        functools.partial(front_kernel, links),
        in_specs=[pl.BlockSpec(memory_space=pltpu.SMEM)] + [here] * 7 + [anywhere] * 3,
        out_specs=[here] + [anywhere] * 3 + [here] * 3 + [anywhere] * (1 + 2 * hops),
        out_shape=[
            shape((2 * own, depth), BF16), shape((depth, chips * width), BF16), shape((chips * width, depth), BF16),
            shape((seq, 2 * HD), BF16), shape((HD, seq), BF16), shape((seq, HD), F32), shape((seq, HD), F32),
        ]
        + [shape((own, depth), BF16)] * (1 + 2 * hops),
        scratch_shapes=[pltpu.VMEM((seq, 2 * HD), BF16), dma((count,)), dma((count,)), dma((3,))],
        compiler_params=pltpu.CompilerParams(
            collective_id=3, has_side_effects=True, vmem_limit_bytes=VMEM_LIMIT
        ),
        cost_estimate=pl.CostEstimate(flops=10**10, bytes_accessed=64 * 2**20, transcendentals=0),
        name="front",
    )(docs, tokens, gain, w_kv, cosine, sine, q_two, g_two, w_query, w_out, out_grad)


def mlp_kernel(
    links, h_hbm, wg_hbm, wu_hbm, wd_hbm, *refs,
):
    g_hbm, refs = refs[: links.n_tensor], refs[links.n_tensor :]
    (
    ghn_ref, mlp_hbm, grads_hbm, h_all, g_all, wg, wu, wd, act_t, gg_t, gu_t, mlp_in, stage, pair_out, pair_in, ring_out, ring_in,
    load_sem, ring_s, ring_r, swap_s, swap_r, pair_s, pair_r, rs_s, rs_r, mlp_s, mlp_r,
    stage_sem, store_sem,
    ) = refs
    chips = links.chips
    own, depth = h_hbm.shape
    seq = chips * 2 * own
    me = lax.axis_index("tensor")
    chip, core = me // 2, lax.rem(me, 2)
    ahead, behind = links.neighbours(chip)
    right = {"tensor": ahead * 2 + core}
    left = {"tensor": behind * 2 + core}
    sibling = {"tensor": chip * 2 + 1 - core}

    loads = [
        pltpu.make_async_copy(h_hbm, h_all.at[0, 0], load_sem.at[0]),
        pltpu.make_async_copy(wg_hbm, wg, load_sem.at[1]),
        pltpu.make_async_copy(wu_hbm, wu, load_sem.at[2]),
        pltpu.make_async_copy(wd_hbm, wd, load_sem.at[3]),
    ] + [
        pltpu.make_async_copy(ref, g_all.at[i // 2, i % 2], load_sem.at[4 + i]) for i, ref in enumerate(g_hbm)
    ]
    for load in loads:
        load.start()
    barrier = pltpu.get_barrier_semaphore()
    for peer in (right, left, sibling):
        pl.semaphore_signal(barrier, inc=1, device_id=peer, device_id_type=pl.DeviceIdType.MESH)
    pl.semaphore_wait(barrier, 3)

    def remote(src, dst, send, recv, peer):
        return pltpu.make_async_remote_copy(
            src_ref=src, dst_ref=dst, send_sem=send, recv_sem=recv, device_id=peer,
            device_id_type=pl.DeviceIdType.MESH,
        )

    def ring(k):
        return remote(h_all.at[k, 0], h_all.at[k + 1, 0], ring_s.at[k], ring_r.at[k], right)

    def swap(k):
        return remote(h_all.at[k, 0], h_all.at[k, 1], swap_s.at[k], swap_r.at[k], sibling)

    def pair(k):
        slot = lax.rem(k, 2)
        return remote(pair_out.at[slot], pair_in.at[slot], pair_s.at[slot], pair_r.at[slot], sibling)

    def scatter(k):
        slot = lax.rem(k, 2)
        return remote(ring_out.at[slot], ring_in.at[k], rs_s.at[k], rs_r.at[k], right)

    def mlp_pair(k):
        slot = lax.rem(k, 2)
        return remote(stage.at[1], mlp_in.at[slot], mlp_s.at[slot], mlp_r.at[slot], sibling)

    def store(k):
        return pltpu.make_async_copy(stage.at[0], mlp_hbm.at[k], stage_sem.at[0])

    loads[0].wait()
    ring(0).start()
    swap(0).start()
    for load in loads[1:]:
        load.wait()

    def hidden_units(k, half):
        h, g = h_all[k, half], g_all[k, half]
        gate = mm(h, wg[...], NT)
        upward = mm(h, wu[...], NT)
        grad_act = mm(g, wd[...], NT)
        sigma = jax.nn.sigmoid(gate)
        swish = gate * sigma
        act = (swish * upward).astype(BF16)
        gg = (grad_act * upward * sigma * (1.0 + gate * (1.0 - sigma))).astype(BF16)
        gu = (grad_act * swish).astype(BF16)
        return act, gg, gu

    def keep_units(k, half, act, gg, gu):
        columns = pl.ds(pl.multiple_of((2 * k + half) * own, own), own)
        act_t[:, columns] = act.T
        gg_t[:, columns] = gg.T
        gu_t[:, columns] = gu.T

    def chunk(k, _):
        @pl.when(k >= 1)
        def _():
            ring(k - 1).wait_recv()

            @pl.when(k < chips - 1)
            def _():
                ring(k).start()

            swap(k).start()

        act0, gg0, gu0 = hidden_units(k, 0)
        swap(k).wait_recv()
        act1, gg1, gu1 = hidden_units(k, 1)

        @pl.when(k >= 2)
        def _():
            pair(k - 2).wait_send()

        pair_out[lax.rem(k, 2)] = (mm(gg1, wg[...], NN) + mm(gu1, wu[...], NN)).astype(BF16)
        pair(k).start()
        part = mm(gg0, wg[...], NN) + mm(gu0, wu[...], NN)
        pair(k).wait_recv()
        total = part + pair_in[lax.rem(k, 2)].astype(F32)

        @pl.when(k == 0)
        def _():
            ghn_ref[...] = total

        @pl.when(k == 1)
        def _():
            ring_out[1] = total.astype(BF16)
            scatter(k).start()

        @pl.when(k >= 2)
        def _():
            scatter(k - 1).wait_recv()

            @pl.when(k >= 3)
            def _():
                scatter(k - 2).wait_send()

            ring_out[lax.rem(k, 2)] = (total + ring_in[k - 1].astype(F32)).astype(BF16)
            scatter(k).start()

        @pl.when(k >= 1)
        def _():
            mlp_pair(k - 1).wait_send()

        stage[1] = mm(act1, wd[...], NN).astype(BF16)
        mlp_pair(k).start()
        keep_units(k, 0, act0, gg0, gu0)
        keep_units(k, 1, act1, gg1, gu1)
        mine = mm(act0, wd[...], NN)
        mlp_pair(k).wait_recv()

        @pl.when(k >= 1)
        def _():
            store(k - 1).wait()

        stage[0] = (mine + mlp_in[lax.rem(k, 2)].astype(F32)).astype(BF16)
        store(k).start()
        return 0

    lax.fori_loop(0, chips, chunk, 0)

    tile = 512

    def columns_of(j, _):
        at = pl.ds(pl.multiple_of(j * tile, tile), tile)
        h = h_all[:, :, :, at].reshape(seq, tile)
        g = g_all[:, :, :, at].reshape(seq, tile)
        wg[:, at] = mm(gg_t[...], h, NN).astype(BF16)
        wu[:, at] = mm(gu_t[...], h, NN).astype(BF16)
        wd[:, at] = mm(act_t[...], g, NN).astype(BF16)
        return 0

    lax.fori_loop(0, depth // tile, columns_of, 0)
    units, (pieces, _, piece) = wg.shape[0], grads_hbm.shape
    stores = [
        pltpu.make_async_copy(
            w.at[:, pl.ds(j * piece, piece)], grads_hbm.at[j, pl.ds(i * units, units)], store_sem.at[i, j]
        )
        for i, w in enumerate((wg, wu, wd))
        for j in range(pieces)
    ]
    for copy in stores:
        copy.start()
    scatter(chips - 1).wait_recv()
    ghn_ref[...] += ring_in[chips - 1].astype(F32)

    for copy in stores:
        copy.wait()
    store(chips - 1).wait()
    mlp_pair(chips - 1).wait_send()
    for k in (chips - 2, chips - 1):
        pair(k).wait_send()
        scatter(k).wait_send()
    for k in range(chips):
        swap(k).wait_send()
    for k in range(chips - 1):
        ring(k).wait_send()


def feed_forward(links, hidden_own, grad_chunks, gate_t, up_t, down):
    own, depth = hidden_own.shape
    chips, units = links.chips, down.shape[0]
    seq = chips * 2 * own
    pieces = 2 * links.n_dp
    anywhere = pl.BlockSpec(memory_space=pl.ANY)
    dma = pltpu.SemaphoreType.DMA
    return pl.pallas_call(
        functools.partial(mlp_kernel, links),
        in_specs=[anywhere] * (4 + links.n_tensor),
        out_specs=[pl.BlockSpec(memory_space=pltpu.VMEM)] + [anywhere] * 2,
        out_shape=[
            jax.ShapeDtypeStruct((own, depth), F32),
            jax.ShapeDtypeStruct((chips, own, depth), BF16),
            jax.ShapeDtypeStruct((pieces, 3 * units, depth // pieces), BF16),
        ],
        scratch_shapes=[
            pltpu.VMEM((chips, 2, own, depth), BF16),
            pltpu.VMEM((chips, 2, own, depth), BF16),
            pltpu.VMEM((units, depth), BF16),
            pltpu.VMEM((units, depth), BF16),
            pltpu.VMEM((units, depth), BF16),
            pltpu.VMEM((units, seq), BF16),
            pltpu.VMEM((units, seq), BF16),
            pltpu.VMEM((units, seq), BF16),
            pltpu.VMEM((2, own, depth), BF16),
            pltpu.VMEM((2, own, depth), BF16),
            pltpu.VMEM((2, own, depth), BF16),
            pltpu.VMEM((2, own, depth), BF16),
            pltpu.VMEM((2, own, depth), BF16),
            pltpu.VMEM((chips, own, depth), BF16),
            dma((4 + links.n_tensor,)),
            dma((chips,)), dma((chips,)), dma((chips,)), dma((chips,)), dma((2,)), dma((2,)),
            dma((chips,)), dma((chips,)), dma((2,)), dma((2,)), dma((1,)), dma((3, pieces)),
        ],
        compiler_params=pltpu.CompilerParams(
            collective_id=1, has_side_effects=True, vmem_limit_bytes=60 * 2**20
        ),
        cost_estimate=pl.CostEstimate(
            flops=18 * seq * depth * units, bytes_accessed=64 * 2**20, transcendentals=seq * units
        ),
        name="feed_forward",
    )(hidden_own, gate_t, up_t, down, *grad_chunks)


def mesh_copy(src, dst, send, recv, peer):
    return pltpu.make_async_remote_copy(
        src_ref=src, dst_ref=dst, send_sem=send, recv_sem=recv, device_id=peer,
        device_id_type=pl.DeviceIdType.MESH,
    )


def add_into(dst, src, rows):
    band = max(b for b in range(16, 353, 16) if rows % b == 0)

    def step(i, _):
        at = pl.ds(pl.multiple_of(i * band, band), band)
        dst[at, :] = (dst[at, :].astype(F32) + src[at, :].astype(F32)).astype(BF16)
        return 0

    lax.fori_loop(0, rows // band, step, 0)


class DpSum:
    def __init__(self, links, send, me, buf, got, free, first=0, rows=None):
        self.first, self.rows = first, rows or buf.shape[1]
        self.links, self.send, self.me, self.buf, self.got, self.free = links, send, me, buf, got, free
        self.n = links.n_dp
        self.ways = [links.bits, links.bits[::-1]]
        self.pending = []

    def at(self, way, rel):
        return way * self.n + (self.me ^ rel)

    def view(self, way, rel):
        return self.buf.at[self.at(way, rel), pl.ds(0, self.rows)]

    def kept(self, way, step):
        done = sum(self.ways[way][: step + 1])
        return [r for r in range(self.n) if r & done == 0]

    def first_slot(self, step):
        return sum(self.n >> (i + 1) for i in range(self.first, step))

    def peer(self, bit):
        return {"dp": self.me ^ bit}

    def start_halving(self, step):
        self.pending = []
        for rank in range(self.n >> (step + 1)):
            for way in (0, 1):
                bit = self.ways[way][step]
                rel = self.kept(way, step)[rank]
                slot = self.first_slot(step) + rank
                copy = self.send(self.buf.at[self.at(way, rel ^ bit)], self.got.at[way, slot], self.peer(bit), False)
                self.pending.append((copy, way, rel, slot))
        self.step = step

    def finish_halving(self):
        for copy, way, rel, slot in self.pending:
            copy.wait_recv()
            add_into(self.buf.at[self.at(way, rel)], self.got.at[way, slot], self.buf.shape[1])
        for copy, _, _, _ in self.pending:
            copy.wait_send()
        for way in (0, 1):
            pl.semaphore_signal(
                self.free.at[way, self.step], inc=1, device_id=self.peer(self.ways[way][self.step]),
                device_id_type=pl.DeviceIdType.MESH,
            )

    def start_doubling(self, step):
        self.pending = []
        if step >= self.first:
            for way in (0, 1):
                pl.semaphore_wait(self.free.at[way, step], 1)
        for rank in range(self.n >> (step + 1)):
            for way in (0, 1):
                bit = self.ways[way][step]
                rel = self.kept(way, step)[rank]
                where = self.view(way, rel)
                self.pending.append((self.send(where, where, self.peer(bit)), way, rel ^ bit))

    def finish_doubling(self):
        for copy, _, _ in self.pending:
            copy.wait_recv()
        return [(way, rel) for _, way, rel in self.pending]

    def chain(self, done, middle=()):
        rounds = len(self.links.bits)
        for step in range(self.first, rounds):
            self.start_halving(step)
            yield
            self.finish_halving()
        yield from middle
        for step in reversed(range(rounds)):
            self.start_doubling(step)
            if step == rounds - 1:
                done(0, 0)
                done(1, 0)
            yield
            for way, rel in self.finish_doubling():
                done(way, rel)


def first_halving(links, parts, me):
    n = links.n_dp
    out, names = [], []
    for way, bits in enumerate((links.bits, links.bits[::-1])):
        for rel in range(n):
            if rel & bits[0] == 0:
                mine = lax.dynamic_index_in_dim(parts, way * n + (me ^ rel), 0, keepdims=False)
                other = lax.dynamic_index_in_dim(parts, way * n + (me ^ rel ^ bits[0]), 0, keepdims=False)
                out.append((mine.astype(F32) + links.across(other, bits[0]).astype(F32)).astype(BF16))
                names.append((way, rel))
    return out, names


def tail_kernel(
    links, names, *refs,
):
    w_hbm, refs = refs[: len(names)], refs[len(names) :]
    (
        o_hbm, q_hbm, m_hbm, kv_keep, kv_send, gn_keep, gn_send, tokens, normed, w_kv, cosine, sine, gain_part,
        ws_hbm, ow_hbm, qw_hbm, kvw_hbm, got_hbm, gn_ref, gains_ref,
        o_buf, o_in, o_ring, q_buf, q_in, w_buf, w_in, c_buf, c_in, b_buf, b_in,
        kv_got, kv_ring, kv_in, gn_got, kvw_half, kvw_got, kvw_in, kvw_all, gains_in,
        ss, rs, o_sem, q_sem, w_sem, out_sem, w_free, o_free, b_free,
    ) = refs
    chips, bits = links.chips, links.bits
    n_dp = links.n_dp
    width = q_buf.shape[1]
    piece = w_buf.shape[2]
    me = lax.axis_index("tensor")
    me_dp = lax.axis_index("dp")
    chip, core = me // 2, lax.rem(me, 2)
    ahead, behind = links.neighbours(chip)
    right = {"tensor": ahead * 2 + core}
    left = {"tensor": behind * 2 + core}
    sibling = {"tensor": me ^ 1}
    column = [None] + [{"tensor": me ^ (2 * k)} for k in range(1, chips)]
    group = [{"tensor": me ^ k} for k in range(1, links.n_tensor)]
    replicas = [{"dp": me_dp ^ k} for k in range(1, n_dp)]

    w_loads = [
        pltpu.make_async_copy(ref, w_buf.at[way * n_dp + (me_dp ^ rel)], w_sem.at[i])
        for i, (ref, (way, rel)) in enumerate(zip(w_hbm, names))
    ]
    loads = {}
    for k in list(range(1, chips)) + [0]:
        loads["q", k] = pltpu.make_async_copy(q_hbm.at[k], q_buf.at[k], q_sem.at[k])
    o_loads = [
        pltpu.make_async_copy(o_hbm.at[:, pl.ds(j * piece, piece)], o_buf.at[j], o_sem.at[j]) for j in range(2 * n_dp)
    ]
    for load in o_loads + list(loads.values()) + w_loads:
        load.start()
    barrier = pltpu.get_barrier_semaphore()
    peers = [right, left] + group + replicas
    for peer in peers:
        pl.semaphore_signal(barrier, inc=1, device_id=peer, device_id_type=pl.DeviceIdType.MESH)
    pl.semaphore_wait(barrier, len(peers))

    copies, opened, locals_ = [], [], []

    def send(src, dst, peer, later=True):
        number = len(copies)
        copy = mesh_copy(src, dst, ss.at[number], rs.at[number], peer)
        copy.start()
        copies.append(copy)
        if later:
            opened.append(copy)
        return copy

    def put(src, dst):
        copy = pltpu.make_async_copy(src, dst, out_sem.at[len(locals_)])
        copy.start()
        locals_.append(copy)

    def ring_chain(name, buf, got):
        copy = None
        for k in list(range(1, chips)) + [0]:
            loads[name, k].wait()
            if copy is not None:
                copy.wait_recv()
                add_into(buf.at[k], got.at[(k - 1) % chips - 1], buf.shape[1])
            if k:
                copy = send(buf.at[k], got.at[k - 1], right)
            yield

    kv_swap = send(kv_send, kv_got, sibling)
    gn_swap = send(gn_send, gn_got, sibling)
    held = {}

    def kv_chain():
        kv_swap.wait_recv()
        sent = []
        for k in range(1, chips):
            kv_ring[k - 1] = (kv_keep[k] + kv_got[k].astype(F32)).astype(BF16)
            sent.append(send(kv_ring.at[k - 1], kv_in.at[k - 1], column[k]))
        yield
        total = kv_keep[0] + kv_got[0].astype(F32)
        for k, copy in enumerate(sent):
            copy.wait_recv()
            total = total + kv_in[k].astype(F32)
        key_grad = total[:, :HD]
        key_grad = key_grad * cosine[...] - pltpu.roll(key_grad, HD // 2, 1) * sine[...]
        kv_lin = jnp.concatenate([key_grad, total[:, HD:]], axis=1).astype(BF16)
        kv_lin_t = kv_lin.T
        for half in (0, 1):
            kvw_half[half] = mm(kv_lin_t[half * HD : (half + 1) * HD], normed[...], NN).astype(BF16)
        held["swap"] = send(kvw_half.at[1 - core], kvw_got, sibling)
        yield
        gn_swap.wait_recv()
        grad = gn_keep[...] + gn_got[...].astype(F32) + mm(kv_lin, w_kv[...], NT)
        gn_ref[...] = grad
        x = tokens[...].astype(F32)
        factor = lax.rsqrt(jnp.mean(x * x, axis=1, keepdims=True) + EPSILON)
        part = jnp.sum(grad * (x * factor), axis=0, keepdims=True)
        lanes = gains_ref.shape[1]
        gains_ref[...] = jnp.concatenate(
            [v[:, i * lanes : (i + 1) * lanes] for v in (part, gain_part[...]) for i in range(4)], axis=0
        )

    def gains_chain():
        done = 0
        for stage in (group, replicas):
            sent = [send(gains_ref, gains_in.at[done + i], peer, False) for i, peer in enumerate(stage)]
            yield
            total = gains_ref[...]
            for i, copy in enumerate(sent):
                copy.wait_recv()
                copy.wait_send()
                total = total + gains_in[done + i]
            gains_ref[...] = total
            done += len(stage)

    band = HD // chips

    def rows_of(k):
        return pl.ds(pl.multiple_of((chip ^ k) * band, band), band)

    def kvw_chain():
        held["swap"].wait_recv()
        add_into(kvw_half.at[core], kvw_got, HD)
        sent = [send(kvw_half.at[core, rows_of(k)], kvw_in.at[k - 1], column[k]) for k in range(1, chips)]
        yield
        total = kvw_half[core, rows_of(0)].astype(F32)
        for k, copy in enumerate(sent):
            copy.wait_recv()
            total = total + kvw_in[k].astype(F32)
        c_buf[...] = total.astype(BF16)

    sum_w = DpSum(links, send, me_dp, w_buf, w_in, w_free, 1)
    sum_o = DpSum(links, send, me_dp, o_buf, o_in, o_free, 0, width)
    sum_b = DpSum(links, send, me_dp, b_buf, b_in, b_free)

    def columns(ref, number):
        return ref.at[:, pl.ds(pl.multiple_of(number * piece, piece), piece)]

    def w_chain():
        for load in w_loads:
            load.wait()
        yield from sum_w.chain(lambda way, rel: put(w_buf.at[sum_w.at(way, rel)], columns(ws_hbm, sum_w.at(way, rel))))

    def o_ring_chain():
        sent = []
        for k in list(range(1, chips)) + [0]:
            rows = pl.ds(k * width, width)
            for way, copy in enumerate(sent):
                copy.wait_recv()
                add_into(o_buf.at[sum_o.at(way, 0), rows], o_ring.at[(k - 1) % chips - 1, way], width)
            if k:
                sent = [
                    send(o_buf.at[sum_o.at(way, 0), rows], o_ring.at[k - 1, way], right) for way in (0, 1)
                ]
                yield

    def o_chain():
        for load in o_loads:
            load.wait()
        yield from sum_o.chain(
            lambda way, rel: put(sum_o.view(way, rel), columns(ow_hbm, sum_o.at(way, rel))), o_ring_chain()
        )

    def c_chain():
        sent = [send(c_buf, c_in.at[i], peer) for i, peer in enumerate(replicas)]
        yield
        total = c_buf[...].astype(F32)
        for i, copy in enumerate(sent):
            copy.wait_recv()
            total = total + c_in[i].astype(F32)
        kvw_all[0, core] = total.astype(BF16)
        sent = [send(kvw_all.at[0, core], kvw_all.at[k, core], column[k]) for k in range(1, chips)]
        yield
        for copy in sent:
            copy.wait_recv()
        copy = send(kvw_all.at[:, core], kvw_all.at[:, core], sibling)
        yield
        copy.wait_recv()
        for k in range(chips):
            for half in (0, 1):
                to = pl.ds(pl.multiple_of(half * HD + (chip ^ k) * band, band), band)
                put(kvw_all.at[k, half], kvw_hbm.at[to])

    def b_chain():
        for j in range(2 * n_dp):
            b_buf[j] = q_buf[0, :, pl.ds(j * piece, piece)]
        yield from sum_b.chain(lambda way, rel: put(b_buf.at[sum_b.at(way, rel)], columns(qw_hbm, sum_b.at(way, rel))))

    def m_chain():
        copy = send(m_hbm, got_hbm, right)
        yield
        copy.wait_recv()

    chains = {
        "w": w_chain(), "o": o_chain(), "q": ring_chain("q", q_buf, q_in), "kv": kv_chain(),
        "g": gains_chain(), "kvw": kvw_chain(), "m": m_chain(), "c": c_chain(), "b": b_chain(),
    }

    take_turns(chains, TAIL_ORDER)
    for copy in opened:
        copy.wait_send()
    for copy in locals_:
        copy.wait()


TAIL_ORDER = (
    "o w kv q", "kv* kvw g kvw*", "c g* o c", "w q o c*", "o q w o", "q* b o m", "b o* b* m*", "w*",
)


def tail(
    links, o_parts, q_parts, m_part, w_pieces, names, kv_keep, kv_send, gn_keep, gn_send, tokens, normed, w_kv, cosine,
    sine, gain_part,
):
    chips, width, depth = q_parts.shape
    own = tokens.shape[0]
    rows, piece = w_pieces[0].shape
    band = HD // chips
    n = links.n_dp
    pieces = 2 * n
    anywhere = pl.BlockSpec(memory_space=pl.ANY)
    here = pl.BlockSpec(memory_space=pltpu.VMEM)
    dma = pltpu.SemaphoreType.DMA
    shape = jax.ShapeDtypeStruct
    count = 20 * chips + 20 * n + 16
    return pl.pallas_call(
        functools.partial(tail_kernel, links, names),
        in_specs=[anywhere] * (3 + len(names)) + [here] * 10,
        out_specs=[anywhere] * 5 + [here] * 2,
        out_shape=[
            shape((rows, depth), BF16), shape((width, depth), BF16),
            shape((width, depth), BF16), shape((2 * HD, depth), BF16), shape((own, depth), BF16),
            shape((own, depth), F32), shape((8, depth // 4), F32),
        ],
        scratch_shapes=[
            pltpu.VMEM((pieces, chips * width, piece), BF16), pltpu.VMEM((2, n - 1, chips * width, piece), BF16),
            pltpu.VMEM((chips - 1, 2, width, piece), BF16),
            pltpu.VMEM((chips, width, depth), BF16), pltpu.VMEM((chips - 1, width, depth), BF16),
            pltpu.VMEM((pieces, rows, piece), BF16), pltpu.VMEM((2, max(1, n // 2 - 1), rows, piece), BF16),
            pltpu.VMEM((band, depth), BF16), pltpu.VMEM((n - 1, band, depth), BF16),
            pltpu.VMEM((pieces, width, piece), BF16), pltpu.VMEM((2, n - 1, width, piece), BF16),
            pltpu.VMEM((chips, own, 2 * HD), BF16),
            pltpu.VMEM((chips - 1, own, 2 * HD), BF16), pltpu.VMEM((chips - 1, own, 2 * HD), BF16),
            pltpu.VMEM((own, depth), BF16),
            pltpu.VMEM((2, HD, depth), BF16), pltpu.VMEM((HD, depth), BF16),
            pltpu.VMEM((chips - 1, band, depth), BF16),
            pltpu.VMEM((chips, 2, band, depth), BF16),
            pltpu.VMEM((links.n_tensor + n, 8, depth // 4), F32),
            dma((count,)), dma((count,)), dma((pieces,)), dma((chips,)), dma((len(names),)),
            dma((3 * pieces + 2 * chips,)),
        ]
        + [pltpu.SemaphoreType.REGULAR((2, len(links.bits)))] * 3,
        compiler_params=pltpu.CompilerParams(
            collective_id=2, has_side_effects=True, vmem_limit_bytes=60 * 2**20
        ),
        cost_estimate=pl.CostEstimate(flops=10**9, bytes_accessed=64 * 2**20, transcendentals=0),
        name="tail",
    )(
        *w_pieces, o_parts, q_parts, m_part, kv_keep, kv_send, gn_keep, gn_send, tokens, normed, w_kv, cosine, sine,
        gain_part,
    )


def rms_factor(values):
    return lax.rsqrt(jnp.mean(values * values, axis=-1, keepdims=True) + EPSILON)


def local(
    n_tensor, n_dp,
    tokens, out_grad, query_two, grad_two, doc_split, attn_gain, mlp_gain, w_query, w_kv, w_out, w_gate, w_up, w_down,
):
    links = Links(n_tensor, n_dp)
    chips = links.chips
    own = tokens.shape[0]
    rows = 2 * own
    seq = own * n_tensor
    width = w_query.shape[1]
    me_dp = lax.axis_index("dp")
    me_t = lax.axis_index("tensor")
    chip, core = me_t // 2, me_t % 2
    two_docs = doc_split[0]
    sp = jnp.stack([chip, two_docs, core]).astype(jnp.int32)
    place = jnp.array(links.place, jnp.int32)
    order = jnp.array(links.order, jnp.int32)

    spot = jnp.arange(rows, dtype=jnp.int32) + core * own
    spot = chip * rows + jnp.where(spot >= rows, spot - rows, spot)
    position = jnp.where(two_docs > 0, spot % SEQ_SHORT, spot)
    frequency = 10000.0 ** (-jnp.arange(HD // 2, dtype=F32) * 2.0 / HD)
    phases = position.astype(F32)[:, None] * frequency[None, :]
    cos, sin = jnp.cos(phases), jnp.sin(phases)
    cosine = jnp.concatenate([cos, cos], axis=1)
    sine = jnp.concatenate([-sin, sin], axis=1)

    residual = tokens.astype(F32)
    attn_scale = rms_factor(residual)
    attn_pre = residual * attn_scale

    normed, wq, wo, kv_all, key_rows_t, dk2, dv2, *grad_chunks = front(
        links, doc_split, tokens, attn_gain[None], w_kv, cosine[:own], sine[:own], query_two, grad_two, w_query, w_out,
        out_grad,
    )
    normed_own = normed[:own]
    grad_chunks = [out_grad] + grad_chunks
    while len(grad_chunks) < n_tensor:
        further = links.ring(grad_chunks[-2])
        grad_chunks += [further, links.swap(further)]

    q_lin = mm(normed, wq, NN)
    queries, context, lse = attend(sp, q_lin, cosine, sine, kv_all)
    branch = pair_sum(links, mm(context, wo, NN))
    hidden = residual + branch
    mlp_scale = rms_factor(hidden)
    mlp_pre = hidden * mlp_scale
    hidden_own = (mlp_pre * mlp_gain).astype(BF16)

    grad_hn, mlp_terms, ffn_parts = feed_forward(links, hidden_own, grad_chunks, w_gate.T, w_up.T, w_down)
    ffn_pieces, ffn_names = first_halving(links, ffn_parts, me_dp)
    mlp_sent = mlp_terms[1]
    for k in range(2, chips):
        mlp_sent = (mlp_terms[k].astype(F32) + links.ring(mlp_sent).astype(F32)).astype(BF16)

    mlp_gain_part = jnp.sum(grad_hn * mlp_pre, axis=0)
    scaled_mlp = grad_hn * mlp_gain
    grad_hidden = out_grad.astype(F32) + mlp_scale * (
        scaled_mlp - mlp_pre * jnp.mean(scaled_mlp * mlp_pre, axis=-1, keepdims=True)
    )

    grad_branch = both(links, grad_hidden.astype(BF16))
    grad_context = mm(grad_branch, wo, NT).astype(BF16)
    query_grad, dk, dv = attend_back(
        sp, queries, grad_context, context, lse, cosine, sine, kv_all, key_rows_t, dk2, dv2
    )
    out_parts = mm(context, grad_branch, TN).astype(BF16)
    query_parts = mm(query_grad, normed, TN).astype(BF16).reshape(chips, width, -1)

    kv_part = jnp.concatenate([dk * SCALE, dv], axis=1).reshape(chips, 2, own, 2 * HD)
    kv_part = jnp.stack(
        [
            lax.dynamic_index_in_dim(kv_part, chip ^ k, 0, keepdims=False)
            for k in range(chips)
        ]
    )
    kv_keep = lax.dynamic_index_in_dim(kv_part, core, 1, keepdims=False)
    kv_send = lax.dynamic_index_in_dim(kv_part, 1 - core, 1, keepdims=False).astype(BF16)
    gn_part = mm(query_grad, wq, NT)
    gain_part = mlp_gain_part[None]
    ffn_w, out_w, query_w, kv_w, mlp_got, grad_normed, gains = tail(
        links, out_parts, query_parts, mlp_sent, ffn_pieces, ffn_names, kv_keep, kv_send, gn_part[:own],
        gn_part[own:].astype(BF16), tokens, normed_own, w_kv, cosine[:own], sine[:own], gain_part,
    )
    units = w_down.shape[0]

    gate_w_grad = ffn_w[:units].astype(F32).T
    up_w_grad = ffn_w[units : 2 * units].astype(F32).T
    down_w_grad = ffn_w[2 * units :].astype(F32)
    out_w_grad = out_w.astype(F32)
    query_w_grad = query_w.astype(F32).T
    kv_w_grad = kv_w.astype(F32).T
    attn_gain_grad, mlp_gain_grad = gains[:4].reshape(-1), gains[4:].reshape(-1)
    block_output = (hidden + (mlp_terms[0].astype(F32) + mlp_got.astype(F32))).astype(BF16)
    scaled_attn = grad_normed * attn_gain
    tokens_grad = (
        grad_hidden
        + attn_scale * (scaled_attn - attn_pre * jnp.mean(scaled_attn * attn_pre, axis=-1, keepdims=True))
    ).astype(BF16)
    return (
        block_output,
        tokens_grad,
        attn_gain_grad,
        mlp_gain_grad,
        query_w_grad,
        kv_w_grad,
        out_w_grad,
        gate_w_grad,
        up_w_grad,
        down_w_grad,
    )


def solution(mesh):
    both_axes = P(("dp", "tensor"), None)
    return jax.shard_map(
        functools.partial(local, mesh.shape["tensor"], mesh.shape["dp"]),
        mesh=mesh,
        in_specs=(
            both_axes,
            both_axes,
            P("dp", "tensor"),
            P("dp", "tensor"),
            P("dp"),
            P(),
            P(),
            P(None, "tensor"),
            P(),
            P("tensor", None),
            P(None, "tensor"),
            P(None, "tensor"),
            P("tensor", None),
        ),
        out_specs=(
            both_axes,
            both_axes,
            P(),
            P(),
            P(None, "tensor"),
            P(),
            P("tensor", None),
            P(None, "tensor"),
            P(None, "tensor"),
            P("tensor", None),
        ),
        check_vma=False,
    )
```

```python
import functools

import jax
import jax.numpy as jnp
from jax import lax
from jax.experimental import pallas as pl
from jax.experimental.pallas import tpu as pltpu
from jax.sharding import PartitionSpec as P

HD = 128
SEQ_SHORT = 1024
EPSILON = 1e-05
MASKED = -1e30
SCALE = HD ** (-0.5)
SCALE2 = SCALE * 1.4426950408889634
F32 = jnp.float32
BF16 = jnp.bfloat16
VMEM_LIMIT = 56 * 2**20


def mm(left, right, dims):
    return lax.dot_general(left, right, (dims, ((), ())), preferred_element_type=F32)


NN = ((1,), (0,))
NT = ((1,), (1,))
TN = ((0,), (0,))


class Links:
    def __init__(self, n_tensor, n_dp):
        self.n_tensor, self.n_dp = n_tensor, n_dp
        self.chips = n_tensor // 2
        odd = list(range(1, self.chips, 2))
        even = list(range(2, self.chips, 2))
        self.order = [0] + odd + even[::-1]
        nxt = {c: self.order[(i + 1) % self.chips] for i, c in enumerate(self.order)}
        self.place = [self.order.index(c) for c in range(self.chips)]
        self.ring_pairs = [(2 * c + k, 2 * nxt[c] + k) for c in range(self.chips) for k in (0, 1)]
        self.swap_pairs = [(i, i ^ 1) for i in range(n_tensor)]
        self.bits = [1 << b for b in range(n_dp.bit_length() - 1)]

    def ring(self, x):
        return lax.ppermute(x, "tensor", self.ring_pairs)

    def swap(self, x):
        return lax.ppermute(x, "tensor", self.swap_pairs)

    def across(self, x, bit):
        return lax.ppermute(x, "dp", [(i, i ^ bit) for i in range(self.n_dp)])

    def neighbours(self, chip):
        ahead, behind = chip * 0, chip * 0
        for i, c in enumerate(self.order):
            ahead = jnp.where(chip == c, self.order[(i + 1) % self.chips], ahead)
            behind = jnp.where(chip == c, self.order[i - 1], behind)
        return ahead, behind


def both(links, own):
    return jnp.concatenate([own, links.swap(own)], axis=0)


def pair_sum(links, part):
    rows = part.shape[0] // 2
    return part[:rows].astype(F32) + links.swap(part[rows:].astype(BF16)).astype(F32)


def diagonal(shape, row_axis, shift):
    size = shape[row_axis]
    row = lax.broadcasted_iota(jnp.int32, shape, row_axis) + shift
    row = jnp.where(row >= size, row - size, row)
    return lax.broadcasted_iota(jnp.int32, shape, 1 - row_axis) <= row


def span(block, two_docs, rows):
    per_doc = SEQ_SHORT // rows
    inner = jnp.where(two_docs > 0, lax.rem(block, per_doc), block)
    return inner + 1, pl.multiple_of((block - inner) * rows, rows)


def fwd_kernel(blocks, sp_ref, q_ref, c_ref, s_ref, k_ref, v_ref, *refs):
    qo_ref, ctx_ref, lse_ref = refs[-3:]
    rows = q_ref.shape[0]
    chip, two_docs, core = sp_ref[0], sp_ref[1], sp_ref[2]
    x = q_ref[...]
    q = (x * c_ref[...] + pltpu.roll(x, HD // 2, 1) * s_ref[...]).astype(BF16)
    qo_ref[...] = q
    count, low = span(chip, two_docs, rows)
    mask = diagonal((rows, rows), 0, core * (rows // 2))
    for n in range(1, blocks + 1):

        @pl.when(count == n)
        def _(n=n):
            near = (n - 1) * rows
            diag = pl.ds(low + near, rows)
            s_diag = jnp.where(mask, mm(q, k_ref[diag, :], NT), MASKED)
            top = jnp.max(s_diag, axis=1, keepdims=True)
            if n > 1:
                main = pl.ds(low, near)
                s_main = mm(q, k_ref[main, :], NT)
                top = jnp.maximum(top, jnp.max(s_main, axis=1, keepdims=True))
            p_diag = jnp.exp2(s_diag - top)
            total = jnp.sum(p_diag, axis=1, keepdims=True)
            out = mm(p_diag.astype(BF16), v_ref[diag, :], NN)
            if n > 1:
                p_main = jnp.exp2(s_main - top)
                total = total + jnp.sum(p_main, axis=1, keepdims=True)
                out = out + mm(p_main.astype(BF16), v_ref[main, :], NN)
            ctx_ref[...] = (out / total).astype(BF16)
            lse = jnp.broadcast_to(top + jnp.log2(total), (rows, HD))
            lse_ref[0] = lse.T[:8]


def bwd_kernel(
    blocks, sp_ref, q_ref, do_ref, ctx_ref, lse_ref, c_ref, s_ref, k_ref, kt_ref, v_ref, dk0_ref, dv0_ref,
    dq_ref, dk_ref, dv_ref,
):
    rows = q_ref.shape[0]
    chip, two_docs, core = sp_ref[0], sp_ref[1], sp_ref[2]

    @pl.when(pl.program_id(0) == 0)
    def _():
        dk_ref[...] = dk0_ref[...]
        dv_ref[...] = dv0_ref[...]

    q, do = q_ref[...], do_ref[...]
    dot = jnp.sum(do.astype(F32) * ctx_ref[...].astype(F32), axis=1, keepdims=True)
    dot = jnp.broadcast_to(dot, (rows, HD)).T[:1]
    lse = lse_ref[0, :1]
    count, low = span(chip, two_docs, rows)
    mask = diagonal((rows, rows), 1, core * (rows // 2))
    for n in range(1, blocks + 1):

        @pl.when(count == n)
        def _(n=n):
            near = (n - 1) * rows
            dqt = jnp.zeros((HD, rows), F32)
            for keys, masked in ((pl.ds(low, near), False), (pl.ds(low + near, rows), True)):
                if not masked and n == 1:
                    continue
                p = jnp.exp2(mm(k_ref[keys, :], q, NT) - lse)
                if masked:
                    p = jnp.where(mask, p, 0.0)
                ds = (p * (mm(v_ref[keys, :], do, NT) - dot)).astype(BF16)
                dv_ref[keys, :] += mm(p.astype(BF16), do, NN)
                dk_ref[keys, :] += mm(ds, q, NN)
                dqt = dqt + mm(kt_ref[:, keys], ds, NN)
            g = dqt.T
            dq_ref[...] = (g * c_ref[...] - pltpu.roll(g, HD // 2, 1) * s_ref[...]).astype(BF16)


def whole(shape):
    return pl.BlockSpec(shape, lambda *_: (0,) * len(shape))


def second_half(seq):
    return pl.BlockSpec((seq, HD), lambda *_: (0, 1))


def attend(sp, q_lin, cosine, sine, kv_all, first, count, before=()):
    rows, width = q_lin.shape
    seq = kv_all.shape[0]
    heads = width // HD
    column = pl.BlockSpec((rows, HD), lambda h, *_: (0, h + first))
    return pl.pallas_call(
        functools.partial(fwd_kernel, seq // rows),
        grid_spec=pltpu.PrefetchScalarGridSpec(
            num_scalar_prefetch=1,
            grid=(count,),
            in_specs=[column, whole((rows, HD)), whole((rows, HD)), whole((seq, HD)), second_half(seq)]
            + [pl.BlockSpec(memory_space=pl.ANY)] * len(before),
            out_specs=[column, column, pl.BlockSpec((1, 8, rows), lambda h, *_: (h + first, 0, 0))],
        ),
        out_shape=[
            jax.ShapeDtypeStruct((rows, width), BF16),
            jax.ShapeDtypeStruct((rows, width), BF16),
            jax.ShapeDtypeStruct((heads, 8, rows), F32),
        ],
        input_output_aliases={6 + i: i for i in range(len(before))},
        compiler_params=pltpu.CompilerParams(vmem_limit_bytes=VMEM_LIMIT),
        cost_estimate=pl.CostEstimate(
            flops=8 * count * rows * seq * HD, bytes_accessed=16 * rows * width, transcendentals=count * rows * seq
        ),
        name="attend",
    )(sp, q_lin, cosine, sine, kv_all, kv_all, *before)


def attend_back(sp, queries, grad_context, context, lse, cosine, sine, kv_all, key_rows_t, dk0, dv0):
    rows, width = queries.shape
    seq = kv_all.shape[0]
    heads = width // HD
    column = pl.BlockSpec((rows, HD), lambda h, *_: (0, h))
    return pl.pallas_call(
        functools.partial(bwd_kernel, seq // rows),
        grid_spec=pltpu.PrefetchScalarGridSpec(
            num_scalar_prefetch=1,
            grid=(heads,),
            in_specs=[
                column, column, column, pl.BlockSpec((1, 8, rows), lambda h, *_: (h, 0, 0)),
                whole((rows, HD)), whole((rows, HD)), whole((seq, HD)), whole((HD, seq)), second_half(seq),
                whole((seq, HD)), whole((seq, HD)),
            ],
            out_specs=[column, whole((seq, HD)), whole((seq, HD))],
        ),
        out_shape=[
            jax.ShapeDtypeStruct((rows, width), BF16),
            jax.ShapeDtypeStruct((seq, HD), F32),
            jax.ShapeDtypeStruct((seq, HD), F32),
        ],
        compiler_params=pltpu.CompilerParams(vmem_limit_bytes=VMEM_LIMIT),
        cost_estimate=pl.CostEstimate(
            flops=20 * heads * rows * seq * HD, bytes_accessed=16 * rows * width, transcendentals=heads * rows * seq
        ),
        name="attend_back",
    )(sp, queries, grad_context, context, lse, cosine, sine, kv_all, key_rows_t, kv_all, dk0, dv0)


def second_unit(block, rows, q, do, kv, dk_ref, dv_ref, late):
    mask = diagonal((rows, rows), 1, 0)
    first = block * rows
    parts = [(pl.ds(first, rows), True, False)]
    middle = SEQ_SHORT * (first // SEQ_SHORT)
    if first > middle:
        parts.append((pl.ds(middle, first - middle), False, False))
    if middle:
        parts.append((pl.ds(0, middle), False, True))
    scores = []
    for keys, masked, far in parts:
        score = mm(kv[keys, :HD], q, NT) * SCALE2
        scores.append(jnp.where(mask, score, MASKED) if masked else score + late if far else score)
    top = functools.reduce(jnp.maximum, [jnp.max(score, axis=0, keepdims=True) for score in scores])
    lifted = [jnp.exp2(score - top) for score in scores]
    inverse = 1.0 / sum(jnp.sum(p, axis=0, keepdims=True) for p in lifted)
    back = [mm(kv[keys, HD:], do, NT) for keys, _, _ in parts]
    dot = sum(jnp.sum(p * b, axis=0, keepdims=True) for p, b in zip(lifted, back)) * inverse
    for (keys, _, _), p, b in zip(parts, lifted, back):
        p = p * inverse
        dv_ref[keys, :] += mm(p.astype(BF16), do, NN)
        dk_ref[keys, :] += mm((p * (b - dot)).astype(BF16), q, NN)


FRONT_HOPS = 1
FRONT_ORDER = (
    "kv q1 o1 kv", "q1 q2 o1 o2", "kv q1 q2 q3", "kv o1 o2 o3", "g kv* s q2", "q3 s o2 o3", "s g q2 q3",
    "s o2 o3 s", "q3 s g s", "o3 s q1* o1*", "q2* o2* q3* o3*", "s* g*",
)


def front_kernel(
    links, docs, tokens, gain, w_kv, cosine, sine, q_two, g_two, wq_hbm, wo_hbm, og_hbm,
    normed, wq_out, wo_out, kv_out, kt_ref, dk_ref, dv_ref, *refs,
):
    og_outs, (kv, ss, rs, ls) = refs[:-4], refs[-4:]
    chips, bits, n_dp = links.chips, links.bits, links.n_dp
    own, depth = tokens.shape
    seq = own * links.n_tensor
    width = wq_hbm.shape[1]
    me = lax.axis_index("tensor")
    me_dp = lax.axis_index("dp")
    chip, core = me // 2, lax.rem(me, 2)
    ahead, behind = links.neighbours(chip)
    right = {"tensor": ahead * 2 + core}
    left = {"tensor": behind * 2 + core}
    sibling = {"tensor": me ^ 1}
    barrier = pltpu.get_barrier_semaphore()
    peers = [right, left, sibling] + [{"dp": me_dp ^ bit} for bit in bits]
    for peer in peers:
        pl.semaphore_signal(barrier, inc=1, device_id=peer, device_id_type=pl.DeviceIdType.MESH)

    copies = []

    def send(src, dst, peer):
        number = len(copies)
        copy = mesh_copy(src, dst, ss.at[number], rs.at[number], peer)
        copy.start()
        copies.append(copy)
        return copy

    def q_piece(ref, k, j, way, size=1):
        rows = depth // n_dp // 2
        at = pl.ds(pl.multiple_of((2 * j + way) * rows, rows), size * rows)
        return ref.at[at, :] if k is None else ref.at[at, pl.ds(k * width, width)]

    def o_piece(ref, k, j, way, size=1):
        rows, half = width // n_dp, depth // 2
        at = pl.ds(pl.multiple_of((k or 0) * width + j * rows, rows), rows)
        return ref.at[at, pl.ds(way * half, size * half)]

    pl.semaphore_wait(barrier, len(peers))
    locals_ = [
        pltpu.make_async_copy(wq_hbm, wq_out.at[:, pl.ds(0, width)], ls.at[0]),
        pltpu.make_async_copy(wo_hbm, wo_out.at[pl.ds(0, width), :], ls.at[1]),
    ]
    for copy in locals_:
        copy.start()
    hops = {}
    for name, piece, src, dst in (("q", q_piece, wq_hbm, wq_out), ("o", o_piece, wo_hbm, wo_out)):
        hops[name, 1] = send(piece(src, None, me_dp, 0, 2), piece(dst, 1, me_dp, 0, 2), right)

    x = tokens[...].astype(F32)
    own_rows = pl.ds(0, own)
    normed[own_rows] = (x * lax.rsqrt(jnp.mean(x * x, axis=1, keepdims=True) + EPSILON) * gain[...]).astype(BF16)
    normed_swap = send(normed.at[own_rows], normed.at[pl.ds(own, own)], sibling)
    lin = mm(normed[own_rows], w_kv[...], NN)
    key = lin[:, :HD] * cosine[...] + pltpu.roll(lin[:, :HD], HD // 2, 1) * sine[...]

    def chip_up(k):
        found = chip * 0
        for i, c in enumerate(links.order):
            found = jnp.where(chip == c, links.order[(i - k) % chips], found)
        return found

    def kv_at(k):
        return kv.at[pl.ds(pl.multiple_of((chip_up(k) * 2 + core) * own, own), own)]

    kv_at(0)[...] = jnp.concatenate([key, lin[:, HD:]], axis=1).astype(BF16)
    late = jnp.where(docs[0] > 0, MASKED, 0.0)
    dk_ref[...] = jnp.zeros_like(dk_ref)
    dv_ref[...] = jnp.zeros_like(dv_ref)

    def kv_chain():
        swaps = []
        for k in range(chips):
            copy = send(kv_at(k), kv_at(k), right) if k + 1 < chips else None
            swaps.append(send(kv_at(k), kv_at(k), sibling))
            yield
            if copy is not None:
                copy.wait_recv()
        for copy in swaps:
            copy.wait_recv()
        store = pltpu.make_async_copy(kv, kv_out, ls.at[2])
        store.start()
        locals_.append(store)
        kt_ref[...] = kv[:, :HD].T

    def block_chain(name, piece, dst, k):
        hops[name, k].wait_recv()
        if k + 1 < chips:
            hops[name, k + 1] = send(piece(dst, k, me_dp, 0, 2), piece(dst, k + 1, me_dp, 0, 2), right)
        held = [[0], [0]]
        for step in range(len(bits)):
            sent = []
            for rank in range(len(held[0])):
                for way, order in enumerate((bits, bits[::-1])):
                    bit, rel = order[step], held[way][rank]
                    where = piece(dst, k, me_dp ^ rel, way)
                    sent.append((send(where, where, {"dp": me_dp ^ bit}), way, rel ^ bit))
            yield
            for copy, way, rel in sent:
                copy.wait_recv()
                held[way].append(rel)

    def grad_chain():
        source = og_hbm
        swaps = [send(og_hbm, og_outs[0], sibling)]
        for i in range(1, len(og_outs), 2):
            hop = send(source, og_outs[i], right)
            yield
            hop.wait_recv()
            source = og_outs[i]
            swaps.append(send(source, og_outs[i + 1], sibling))
        yield
        for copy in swaps:
            copy.wait_recv()

    rows = min(512, SEQ_SHORT)
    heads = q_two.shape[1] // HD

    def second_chain():
        for block in reversed(range(seq // rows)):
            for head in range(heads):
                at = (pl.ds(block * rows, rows), pl.ds(head * HD, HD))
                second_unit(block, rows, q_two[at], g_two[at], kv, dk_ref, dv_ref, late)
                yield
        dk_ref[...] *= SCALE2

    chains = {"kv": kv_chain(), "s": second_chain(), "g": grad_chain()}
    for k in range(1, chips):
        chains["q%d" % k] = block_chain("q", q_piece, wq_out, k)
        chains["o%d" % k] = block_chain("o", o_piece, wo_out, k)
    take_turns(chains, FRONT_ORDER)
    normed_swap.wait_recv()
    for copy in copies:
        copy.wait_send()
    for copy in locals_:
        copy.wait()


def take_turns(chains, order):
    def turn(name):
        if name in chains and next(chains[name], chains) is chains:
            del chains[name]

    for name in " ".join(order).split():
        turn(name.rstrip("*"))
        while name.endswith("*") and name.rstrip("*") in chains:
            turn(name.rstrip("*"))
    while chains:
        for name in list(chains):
            turn(name)


def front(links, docs, tokens, gain, w_kv, cosine, sine, q_two, g_two, w_query, w_out, out_grad):
    chips = links.chips
    own, depth = tokens.shape
    seq = own * links.n_tensor
    width = w_query.shape[1]
    anywhere = pl.BlockSpec(memory_space=pl.ANY)
    here = pl.BlockSpec(memory_space=pltpu.VMEM)
    dma = pltpu.SemaphoreType.DMA
    shape = jax.ShapeDtypeStruct
    count = 2 * chips * (2 * links.n_dp) + 4 * chips + 8
    hops = min(FRONT_HOPS, chips - 1)
    return pl.pallas_call(
        functools.partial(front_kernel, links),
        in_specs=[pl.BlockSpec(memory_space=pltpu.SMEM)] + [here] * 7 + [anywhere] * 3,
        out_specs=[here] + [anywhere] * 3 + [here] * 3 + [anywhere] * (1 + 2 * hops),
        out_shape=[
            shape((2 * own, depth), BF16), shape((depth, chips * width), BF16), shape((chips * width, depth), BF16),
            shape((seq, 2 * HD), BF16), shape((HD, seq), BF16), shape((seq, HD), F32), shape((seq, HD), F32),
        ]
        + [shape((own, depth), BF16)] * (1 + 2 * hops),
        scratch_shapes=[pltpu.VMEM((seq, 2 * HD), BF16), dma((count,)), dma((count,)), dma((3,))],
        compiler_params=pltpu.CompilerParams(
            collective_id=3, has_side_effects=True, vmem_limit_bytes=VMEM_LIMIT
        ),
        cost_estimate=pl.CostEstimate(flops=10**10, bytes_accessed=64 * 2**20, transcendentals=0),
        name="front",
    )(docs, tokens, gain, w_kv, cosine, sine, q_two, g_two, w_query, w_out, out_grad)


def mlp_kernel(
    links, h_hbm, wg_hbm, wu_hbm, wd_hbm, *refs,
):
    paired = 1 + min(FRONT_HOPS, links.chips - 1)
    given = [(k, half) for k in range(links.chips) for half in ((0, 1) if k < paired else (0,))]
    g_hbm, refs = refs[: len(given)], refs[len(given) :]
    (
    ghn_ref, mlp_hbm, grads_hbm, h_all, g_all, wg, wu, wd, act_t, gg_t, gu_t, mlp_in, stage, pair_out, pair_in, ring_out, ring_in,
    load_sem, ring_s, ring_r, swap_s, swap_r, pair_s, pair_r, rs_s, rs_r, mlp_s, mlp_r,
    stage_sem, store_sem, g_s, g_r,
    ) = refs
    chips = links.chips
    own, depth = h_hbm.shape
    seq = chips * 2 * own
    me = lax.axis_index("tensor")
    chip, core = me // 2, lax.rem(me, 2)
    ahead, behind = links.neighbours(chip)
    right = {"tensor": ahead * 2 + core}
    left = {"tensor": behind * 2 + core}
    sibling = {"tensor": chip * 2 + 1 - core}

    loads = [
        pltpu.make_async_copy(h_hbm, h_all.at[0, 0], load_sem.at[0]),
        pltpu.make_async_copy(wg_hbm, wg, load_sem.at[1]),
        pltpu.make_async_copy(wu_hbm, wu, load_sem.at[2]),
        pltpu.make_async_copy(wd_hbm, wd, load_sem.at[3]),
    ] + [
        pltpu.make_async_copy(ref, g_all.at[at], load_sem.at[4 + i]) for i, (ref, at) in enumerate(zip(g_hbm, given))
    ]
    for load in loads:
        load.start()
    barrier = pltpu.get_barrier_semaphore()
    for peer in (right, left, sibling):
        pl.semaphore_signal(barrier, inc=1, device_id=peer, device_id_type=pl.DeviceIdType.MESH)
    pl.semaphore_wait(barrier, 3)

    def remote(src, dst, send, recv, peer):
        return pltpu.make_async_remote_copy(
            src_ref=src, dst_ref=dst, send_sem=send, recv_sem=recv, device_id=peer,
            device_id_type=pl.DeviceIdType.MESH,
        )

    def ring(k):
        return remote(h_all.at[k, 0], h_all.at[k + 1, 0], ring_s.at[k], ring_r.at[k], right)

    def swap(k):
        return remote(h_all.at[k, 0], h_all.at[k, 1], swap_s.at[k], swap_r.at[k], sibling)

    def g_swap(k):
        return remote(g_all.at[k, 0], g_all.at[k, 1], g_s.at[k], g_r.at[k], sibling)

    def pair(k):
        slot = lax.rem(k, 2)
        return remote(pair_out.at[slot], pair_in.at[slot], pair_s.at[slot], pair_r.at[slot], sibling)

    def scatter(k):
        slot = lax.rem(k, 2)
        return remote(ring_out.at[slot], ring_in.at[k], rs_s.at[k], rs_r.at[k], right)

    def mlp_pair(k):
        slot = lax.rem(k, 2)
        return remote(stage.at[1], mlp_in.at[slot], mlp_s.at[slot], mlp_r.at[slot], sibling)

    def store(k):
        return pltpu.make_async_copy(stage.at[0], mlp_hbm.at[k], stage_sem.at[0])

    loads[0].wait()
    ring(0).start()
    swap(0).start()
    for load in loads[1:]:
        load.wait()
    for k in range(paired, chips):
        g_swap(k).start()

    def hidden_units(k, half):
        h, g = h_all[k, half], g_all[k, half]
        gate = mm(h, wg[...], NT)
        upward = mm(h, wu[...], NT)
        grad_act = mm(g, wd[...], NT)
        sigma = jax.nn.sigmoid(gate)
        swish = gate * sigma
        act = (swish * upward).astype(BF16)
        gg = (grad_act * upward * sigma * (1.0 + gate * (1.0 - sigma))).astype(BF16)
        gu = (grad_act * swish).astype(BF16)
        return act, gg, gu

    def keep_units(k, half, act, gg, gu):
        columns = pl.ds(pl.multiple_of((2 * k + half) * own, own), own)
        act_t[:, columns] = act.T
        gg_t[:, columns] = gg.T
        gu_t[:, columns] = gu.T

    def chunk(k, _):
        @pl.when(k >= 1)
        def _():
            ring(k - 1).wait_recv()

            @pl.when(k < chips - 1)
            def _():
                ring(k).start()

            swap(k).start()

        act0, gg0, gu0 = hidden_units(k, 0)
        swap(k).wait_recv()

        @pl.when(k >= paired)
        def _():
            g_swap(k).wait_recv()

        act1, gg1, gu1 = hidden_units(k, 1)

        @pl.when(k >= 2)
        def _():
            pair(k - 2).wait_send()

        pair_out[lax.rem(k, 2)] = (mm(gg1, wg[...], NN) + mm(gu1, wu[...], NN)).astype(BF16)
        pair(k).start()
        part = mm(gg0, wg[...], NN) + mm(gu0, wu[...], NN)
        pair(k).wait_recv()
        total = part + pair_in[lax.rem(k, 2)].astype(F32)

        @pl.when(k == 0)
        def _():
            ghn_ref[...] = total

        @pl.when(k == 1)
        def _():
            ring_out[1] = total.astype(BF16)
            scatter(k).start()

        @pl.when(k >= 2)
        def _():
            scatter(k - 1).wait_recv()

            @pl.when(k >= 3)
            def _():
                scatter(k - 2).wait_send()

            ring_out[lax.rem(k, 2)] = (total + ring_in[k - 1].astype(F32)).astype(BF16)
            scatter(k).start()

        @pl.when(k >= 1)
        def _():
            mlp_pair(k - 1).wait_send()

        stage[1] = mm(act1, wd[...], NN).astype(BF16)
        mlp_pair(k).start()
        keep_units(k, 0, act0, gg0, gu0)
        keep_units(k, 1, act1, gg1, gu1)
        mine = mm(act0, wd[...], NN)
        mlp_pair(k).wait_recv()

        @pl.when(k >= 1)
        def _():
            store(k - 1).wait()

        stage[0] = (mine + mlp_in[lax.rem(k, 2)].astype(F32)).astype(BF16)
        store(k).start()
        return 0

    lax.fori_loop(0, chips, chunk, 0)

    tile = 512

    def columns_of(j, _):
        at = pl.ds(pl.multiple_of(j * tile, tile), tile)
        h = h_all[:, :, :, at].reshape(seq, tile)
        g = g_all[:, :, :, at].reshape(seq, tile)
        wg[:, at] = mm(gg_t[...], h, NN).astype(BF16)
        wu[:, at] = mm(gu_t[...], h, NN).astype(BF16)
        wd[:, at] = mm(act_t[...], g, NN).astype(BF16)
        return 0

    lax.fori_loop(0, depth // tile, columns_of, 0)
    units, (pieces, _, piece) = wg.shape[0], grads_hbm.shape
    stores = [
        pltpu.make_async_copy(
            w.at[:, pl.ds(j * piece, piece)], grads_hbm.at[j, pl.ds(i * units, units)], store_sem.at[i, j]
        )
        for i, w in enumerate((wg, wu, wd))
        for j in range(pieces)
    ]
    for copy in stores:
        copy.start()
    scatter(chips - 1).wait_recv()
    ghn_ref[...] += ring_in[chips - 1].astype(F32)

    for copy in stores:
        copy.wait()
    store(chips - 1).wait()
    mlp_pair(chips - 1).wait_send()
    for k in (chips - 2, chips - 1):
        pair(k).wait_send()
        scatter(k).wait_send()
    for k in range(chips):
        swap(k).wait_send()
    for k in range(paired, chips):
        g_swap(k).wait_send()
    for k in range(chips - 1):
        ring(k).wait_send()


def feed_forward(links, hidden_own, grad_chunks, gate_t, up_t, down):
    own, depth = hidden_own.shape
    chips, units = links.chips, down.shape[0]
    seq = chips * 2 * own
    pieces = 2 * links.n_dp
    anywhere = pl.BlockSpec(memory_space=pl.ANY)
    dma = pltpu.SemaphoreType.DMA
    return pl.pallas_call(
        functools.partial(mlp_kernel, links),
        in_specs=[anywhere] * (4 + len(grad_chunks)),
        out_specs=[pl.BlockSpec(memory_space=pltpu.VMEM)] + [anywhere] * 2,
        out_shape=[
            jax.ShapeDtypeStruct((own, depth), F32),
            jax.ShapeDtypeStruct((chips, own, depth), BF16),
            jax.ShapeDtypeStruct((pieces, 3 * units, depth // pieces), BF16),
        ],
        scratch_shapes=[
            pltpu.VMEM((chips, 2, own, depth), BF16),
            pltpu.VMEM((chips, 2, own, depth), BF16),
            pltpu.VMEM((units, depth), BF16),
            pltpu.VMEM((units, depth), BF16),
            pltpu.VMEM((units, depth), BF16),
            pltpu.VMEM((units, seq), BF16),
            pltpu.VMEM((units, seq), BF16),
            pltpu.VMEM((units, seq), BF16),
            pltpu.VMEM((2, own, depth), BF16),
            pltpu.VMEM((2, own, depth), BF16),
            pltpu.VMEM((2, own, depth), BF16),
            pltpu.VMEM((2, own, depth), BF16),
            pltpu.VMEM((2, own, depth), BF16),
            pltpu.VMEM((chips, own, depth), BF16),
            dma((4 + len(grad_chunks),)),
            dma((chips,)), dma((chips,)), dma((chips,)), dma((chips,)), dma((2,)), dma((2,)),
            dma((chips,)), dma((chips,)), dma((2,)), dma((2,)), dma((1,)), dma((3, pieces)), dma((chips,)), dma((chips,)),
        ],
        compiler_params=pltpu.CompilerParams(
            collective_id=1, has_side_effects=True, vmem_limit_bytes=60 * 2**20
        ),
        cost_estimate=pl.CostEstimate(
            flops=18 * seq * depth * units, bytes_accessed=64 * 2**20, transcendentals=seq * units
        ),
        name="feed_forward",
    )(hidden_own, gate_t, up_t, down, *grad_chunks)


def mesh_copy(src, dst, send, recv, peer):
    return pltpu.make_async_remote_copy(
        src_ref=src, dst_ref=dst, send_sem=send, recv_sem=recv, device_id=peer,
        device_id_type=pl.DeviceIdType.MESH,
    )


def add_into(dst, src, rows):
    band = max(b for b in range(16, 353, 16) if rows % b == 0)

    def step(i, _):
        at = pl.ds(pl.multiple_of(i * band, band), band)
        dst[at, :] = (dst[at, :].astype(F32) + src[at, :].astype(F32)).astype(BF16)
        return 0

    lax.fori_loop(0, rows // band, step, 0)


class DpSum:
    def __init__(self, links, send, me, buf, got, free, first=0, rows=None):
        self.first, self.rows = first, rows or buf.shape[1]
        self.links, self.send, self.me, self.buf, self.got, self.free = links, send, me, buf, got, free
        self.n = links.n_dp
        self.ways = [links.bits, links.bits[::-1]]
        self.pending = []

    def at(self, way, rel):
        return way * self.n + (self.me ^ rel)

    def view(self, way, rel):
        return self.buf.at[self.at(way, rel), pl.ds(0, self.rows)]

    def kept(self, way, step):
        done = sum(self.ways[way][: step + 1])
        return [r for r in range(self.n) if r & done == 0]

    def first_slot(self, step):
        return sum(self.n >> (i + 1) for i in range(self.first, step))

    def peer(self, bit):
        return {"dp": self.me ^ bit}

    def start_halving(self, step):
        self.pending = []
        for rank in range(self.n >> (step + 1)):
            for way in (0, 1):
                bit = self.ways[way][step]
                rel = self.kept(way, step)[rank]
                slot = self.first_slot(step) + rank
                copy = self.send(self.buf.at[self.at(way, rel ^ bit)], self.got.at[way, slot], self.peer(bit), False)
                self.pending.append((copy, way, rel, slot))
        self.step = step

    def finish_halving(self):
        for copy, way, rel, slot in self.pending:
            copy.wait_recv()
            add_into(self.buf.at[self.at(way, rel)], self.got.at[way, slot], self.buf.shape[1])
        for copy, _, _, _ in self.pending:
            copy.wait_send()
        for way in (0, 1):
            pl.semaphore_signal(
                self.free.at[way, self.step], inc=1, device_id=self.peer(self.ways[way][self.step]),
                device_id_type=pl.DeviceIdType.MESH,
            )

    def start_doubling(self, step):
        self.pending = []
        if step >= self.first:
            for way in (0, 1):
                pl.semaphore_wait(self.free.at[way, step], 1)
        for rank in range(self.n >> (step + 1)):
            for way in (0, 1):
                bit = self.ways[way][step]
                rel = self.kept(way, step)[rank]
                where = self.view(way, rel)
                self.pending.append((self.send(where, where, self.peer(bit)), way, rel ^ bit))

    def finish_doubling(self):
        for copy, _, _ in self.pending:
            copy.wait_recv()
        return [(way, rel) for _, way, rel in self.pending]

    def chain(self, done, middle=()):
        rounds = len(self.links.bits)
        for step in range(self.first, rounds):
            self.start_halving(step)
            yield
            self.finish_halving()
        yield from middle
        for step in reversed(range(rounds)):
            self.start_doubling(step)
            if step == rounds - 1:
                done(0, 0)
                done(1, 0)
            yield
            for way, rel in self.finish_doubling():
                done(way, rel)


def first_halving(links, parts, me):
    n = links.n_dp
    stay, came, names = [], [], []
    for way, bits in enumerate((links.bits, links.bits[::-1])):
        for rel in range(n):
            if rel & bits[0] == 0:
                stay.append(lax.dynamic_index_in_dim(parts, way * n + (me ^ rel), 0, keepdims=False))
                other = lax.dynamic_index_in_dim(parts, way * n + (me ^ rel ^ bits[0]), 0, keepdims=False)
                came.append(links.across(other, bits[0]))
                names.append((way, rel))
    return stay, came, names


def tail_kernel(
    links, names, *refs,
):
    w_hbm, refs = refs[: len(names)], refs[len(names) :]
    (
        o_hbm, q_hbm, m_hbm, kv_keep, kv_send, gn_keep, gn_send, tokens, normed, w_kv, cosine, sine, gain_part,
        gain, grad_hidden, hidden,
        ws_hbm, ow_hbm, qw_hbm, kvw_hbm, block_ref, grad_ref, gains_ref,
        o_buf, o_in, o_ring, q_buf, q_in, w_buf, w_in, c_buf, c_in, b_buf, b_in, b_turned, got,
        kv_got, kv_ring, kv_in, gn_got, kvw_half, kvw_got, kvw_in, kvw_all, gains_in,
        ss, rs, o_sem, q_sem, w_sem, out_sem, w_free, o_free, b_free,
    ) = refs
    chips, bits = links.chips, links.bits
    n_dp = links.n_dp
    width = q_buf.shape[1]
    piece = w_buf.shape[2]
    me = lax.axis_index("tensor")
    me_dp = lax.axis_index("dp")
    chip, core = me // 2, lax.rem(me, 2)
    ahead, behind = links.neighbours(chip)
    right = {"tensor": ahead * 2 + core}
    left = {"tensor": behind * 2 + core}
    sibling = {"tensor": me ^ 1}
    column = [None] + [{"tensor": me ^ (2 * k)} for k in range(1, chips)]
    group = [{"tensor": me ^ k} for k in range(1, links.n_tensor)]
    replicas = [{"dp": me_dp ^ k} for k in range(1, n_dp)]

    w_loads = [
        pltpu.make_async_copy(ref, w_buf.at[way * n_dp + (me_dp ^ rel)], w_sem.at[i])
        for i, (ref, (way, rel)) in enumerate(zip(w_hbm, names))
    ]
    loads = {}
    for k in list(range(1, chips)) + [0]:
        loads["q", k] = pltpu.make_async_copy(q_hbm.at[k], q_buf.at[k], q_sem.at[k])
    o_loads = [
        pltpu.make_async_copy(o_hbm.at[:, pl.ds(j * piece, piece)], o_buf.at[j], o_sem.at[j]) for j in range(2 * n_dp)
    ]
    for load in o_loads + list(loads.values()) + w_loads:
        load.start()
    barrier = pltpu.get_barrier_semaphore()
    peers = [right, left] + group + replicas
    for peer in peers:
        pl.semaphore_signal(barrier, inc=1, device_id=peer, device_id_type=pl.DeviceIdType.MESH)
    pl.semaphore_wait(barrier, len(peers))

    copies, opened, locals_ = [], [], []

    def send(src, dst, peer, later=True):
        number = len(copies)
        copy = mesh_copy(src, dst, ss.at[number], rs.at[number], peer)
        copy.start()
        copies.append(copy)
        if later:
            opened.append(copy)
        return copy

    def put(src, dst):
        copy = pltpu.make_async_copy(src, dst, out_sem.at[len(locals_)])
        copy.start()
        locals_.append(copy)

    def ring_chain(name, buf, got):
        copy = None
        for k in list(range(1, chips)) + [0]:
            loads[name, k].wait()
            if copy is not None:
                copy.wait_recv()
                add_into(buf.at[k], got.at[(k - 1) % chips - 1], buf.shape[1])
            if k:
                copy = send(buf.at[k], got.at[k - 1], right)
            yield

    kv_swap = send(kv_send, kv_got, sibling)
    gn_swap = send(gn_send, gn_got, sibling)
    held = {}

    def kv_chain():
        kv_swap.wait_recv()
        sent = []
        for k in range(1, chips):
            kv_ring[k - 1] = (kv_keep[k] + kv_got[k].astype(F32)).astype(BF16)
            sent.append(send(kv_ring.at[k - 1], kv_in.at[k - 1], column[k]))
        yield
        total = kv_keep[0] + kv_got[0].astype(F32)
        for k, copy in enumerate(sent):
            copy.wait_recv()
            total = total + kv_in[k].astype(F32)
        key_grad = total[:, :HD]
        key_grad = key_grad * cosine[...] - pltpu.roll(key_grad, HD // 2, 1) * sine[...]
        kv_lin = jnp.concatenate([key_grad, total[:, HD:]], axis=1).astype(BF16)
        kv_lin_t = kv_lin.T
        for half in (0, 1):
            kvw_half[half] = mm(kv_lin_t[half * HD : (half + 1) * HD], normed[...], NN).astype(BF16)
        held["swap"] = send(kvw_half.at[1 - core], kvw_got, sibling)
        yield
        gn_swap.wait_recv()
        grad = gn_keep[...] + gn_got[...].astype(F32) + mm(kv_lin, w_kv[...], NT)
        x = tokens[...].astype(F32)
        factor = lax.rsqrt(jnp.mean(x * x, axis=1, keepdims=True) + EPSILON)
        x = x * factor
        part = jnp.sum(grad * x, axis=0, keepdims=True)
        scaled = grad * gain[...]
        back = scaled - x * jnp.mean(scaled * x, axis=1, keepdims=True)
        grad_ref[...] = (grad_hidden[...] + factor * back).astype(BF16)
        lanes = gains_ref.shape[1]
        gains_ref[...] = jnp.concatenate(
            [v[:, i * lanes : (i + 1) * lanes] for v in (part, gain_part[...]) for i in range(4)], axis=0
        )

    def gains_chain():
        done = 0
        for stage in (group, replicas):
            sent = [send(gains_ref, gains_in.at[done + i], peer, False) for i, peer in enumerate(stage)]
            yield
            total = gains_ref[...]
            for i, copy in enumerate(sent):
                copy.wait_recv()
                copy.wait_send()
                total = total + gains_in[done + i]
            gains_ref[...] = total
            done += len(stage)

    band = HD // chips

    def rows_of(k):
        return pl.ds(pl.multiple_of((chip ^ k) * band, band), band)

    def kvw_chain():
        held["swap"].wait_recv()
        add_into(kvw_half.at[core], kvw_got, HD)
        sent = [send(kvw_half.at[core, rows_of(k)], kvw_in.at[k - 1], column[k]) for k in range(1, chips)]
        yield
        total = kvw_half[core, rows_of(0)].astype(F32)
        for k, copy in enumerate(sent):
            copy.wait_recv()
            total = total + kvw_in[k].astype(F32)
        c_buf[...] = total.astype(BF16)

    sum_w = DpSum(links, send, me_dp, w_buf, w_in, w_free, 1)
    sum_o = DpSum(links, send, me_dp, o_buf, o_in, o_free, 0, width)
    sum_b = DpSum(links, send, me_dp, b_buf, b_in, b_free)

    def columns(ref, number):
        return ref.at[:, pl.ds(pl.multiple_of(number * piece, piece), piece)]

    def w_chain():
        for load in w_loads:
            load.wait()
        yield from sum_w.chain(lambda way, rel: put(w_buf.at[sum_w.at(way, rel)], columns(ws_hbm, sum_w.at(way, rel))))

    def o_ring_chain():
        sent = []
        for k in list(range(1, chips)) + [0]:
            rows = pl.ds(k * width, width)
            for way, copy in enumerate(sent):
                copy.wait_recv()
                add_into(o_buf.at[sum_o.at(way, 0), rows], o_ring.at[(k - 1) % chips - 1, way], width)
            if k:
                sent = [
                    send(o_buf.at[sum_o.at(way, 0), rows], o_ring.at[k - 1, way], right) for way in (0, 1)
                ]
                yield

    def o_chain():
        for load in o_loads:
            load.wait()
        yield from sum_o.chain(
            lambda way, rel: put(sum_o.view(way, rel), columns(ow_hbm, sum_o.at(way, rel))), o_ring_chain()
        )

    def c_chain():
        sent = [send(c_buf, c_in.at[i], peer) for i, peer in enumerate(replicas)]
        yield
        total = c_buf[...].astype(F32)
        for i, copy in enumerate(sent):
            copy.wait_recv()
            total = total + c_in[i].astype(F32)
        kvw_all[0, core] = total.astype(BF16)
        sent = [send(kvw_all.at[0, core], kvw_all.at[k, core], column[k]) for k in range(1, chips)]
        yield
        for copy in sent:
            copy.wait_recv()
        copy = send(kvw_all.at[:, core], kvw_all.at[:, core], sibling)
        yield
        copy.wait_recv()
        for k in range(chips):
            for half in (0, 1):
                to = pl.ds(pl.multiple_of(half * HD + (chip ^ k) * band, band), band)
                put(kvw_all.at[k, half], kvw_hbm.at[to])

    def b_chain():
        for j in range(2 * n_dp):
            b_buf[j] = q_buf[0, :, pl.ds(j * piece, piece)]

        def turn_over(way, rel):
            at = sum_b.at(way, rel)
            b_turned[at] = b_buf[at].T
            put(b_turned.at[at], qw_hbm.at[pl.ds(pl.multiple_of(at * piece, piece), piece)])

        yield from sum_b.chain(turn_over)

    def m_chain():
        copy = send(m_hbm, got, right)
        yield
        copy.wait_recv()
        block_ref[...] = (hidden[...] + got[...].astype(F32)).astype(BF16)

    chains = {
        "w": w_chain(), "o": o_chain(), "q": ring_chain("q", q_buf, q_in), "kv": kv_chain(),
        "g": gains_chain(), "kvw": kvw_chain(), "m": m_chain(), "c": c_chain(), "b": b_chain(),
    }

    take_turns(chains, TAIL_ORDER)
    for copy in opened:
        copy.wait_send()
    for copy in locals_:
        copy.wait()


TAIL_ORDER = (
    "o kv w kv", "kvw kv g kvw", "q c g* o", "c w o o", "c* o q w", "q* m b b", "o o b o*", "b* w* m*",
)


def tail(
    links, o_parts, q_parts, m_part, w_pieces, names, kv_keep, kv_send, gn_keep, gn_send, tokens, normed, w_kv, cosine,
    sine, gain_part, gain, grad_hidden, hidden,
):
    chips, width, depth = q_parts.shape
    own = tokens.shape[0]
    rows, piece = w_pieces[0].shape
    band = HD // chips
    n = links.n_dp
    pieces = 2 * n
    anywhere = pl.BlockSpec(memory_space=pl.ANY)
    here = pl.BlockSpec(memory_space=pltpu.VMEM)
    dma = pltpu.SemaphoreType.DMA
    shape = jax.ShapeDtypeStruct
    count = 20 * chips + 20 * n + 16
    return pl.pallas_call(
        functools.partial(tail_kernel, links, names),
        in_specs=[anywhere] * (3 + len(names)) + [here] * 13,
        out_specs=[anywhere] * 4 + [here] * 3,
        out_shape=[
            shape((rows, depth), BF16), shape((width, depth), BF16),
            shape((depth, width), BF16), shape((2 * HD, depth), BF16), shape((own, depth), BF16),
            shape((own, depth), BF16), shape((8, depth // 4), F32),
        ],
        scratch_shapes=[
            pltpu.VMEM((pieces, chips * width, piece), BF16), pltpu.VMEM((2, n - 1, chips * width, piece), BF16),
            pltpu.VMEM((chips - 1, 2, width, piece), BF16),
            pltpu.VMEM((chips, width, depth), BF16), pltpu.VMEM((chips - 1, width, depth), BF16),
            pltpu.VMEM((pieces, rows, piece), BF16), pltpu.VMEM((2, max(1, n // 2 - 1), rows, piece), BF16),
            pltpu.VMEM((band, depth), BF16), pltpu.VMEM((n - 1, band, depth), BF16),
            pltpu.VMEM((pieces, width, piece), BF16), pltpu.VMEM((2, n - 1, width, piece), BF16),
            pltpu.VMEM((pieces, piece, width), BF16), pltpu.VMEM((own, depth), BF16),
            pltpu.VMEM((chips, own, 2 * HD), BF16),
            pltpu.VMEM((chips - 1, own, 2 * HD), BF16), pltpu.VMEM((chips - 1, own, 2 * HD), BF16),
            pltpu.VMEM((own, depth), BF16),
            pltpu.VMEM((2, HD, depth), BF16), pltpu.VMEM((HD, depth), BF16),
            pltpu.VMEM((chips - 1, band, depth), BF16),
            pltpu.VMEM((chips, 2, band, depth), BF16),
            pltpu.VMEM((links.n_tensor + n, 8, depth // 4), F32),
            dma((count,)), dma((count,)), dma((pieces,)), dma((chips,)), dma((len(names),)),
            dma((3 * pieces + 2 * chips,)),
        ]
        + [pltpu.SemaphoreType.REGULAR((2, len(links.bits)))] * 3,
        compiler_params=pltpu.CompilerParams(
            collective_id=2, has_side_effects=True, vmem_limit_bytes=60 * 2**20
        ),
        cost_estimate=pl.CostEstimate(flops=10**9, bytes_accessed=64 * 2**20, transcendentals=0),
        name="tail",
    )(
        *w_pieces, o_parts, q_parts, m_part, kv_keep, kv_send, gn_keep, gn_send, tokens, normed, w_kv, cosine, sine,
        gain_part, gain, grad_hidden, hidden,
    )


def rms_factor(values):
    return lax.rsqrt(jnp.mean(values * values, axis=-1, keepdims=True) + EPSILON)


def local(
    n_tensor, n_dp,
    tokens, out_grad, query_two, grad_two, doc_split, attn_gain, mlp_gain, w_query, w_kv, w_out, w_gate, w_up, w_down,
):
    links = Links(n_tensor, n_dp)
    chips = links.chips
    own = tokens.shape[0]
    rows = 2 * own
    seq = own * n_tensor
    width = w_query.shape[1]
    me_dp = lax.axis_index("dp")
    me_t = lax.axis_index("tensor")
    chip, core = me_t // 2, me_t % 2
    two_docs = doc_split[0]
    sp = jnp.stack([chip, two_docs, core]).astype(jnp.int32)
    place = jnp.array(links.place, jnp.int32)
    order = jnp.array(links.order, jnp.int32)

    spot = jnp.arange(rows, dtype=jnp.int32) + core * own
    spot = chip * rows + jnp.where(spot >= rows, spot - rows, spot)
    position = jnp.where(two_docs > 0, spot % SEQ_SHORT, spot)
    frequency = 10000.0 ** (-jnp.arange(HD // 2, dtype=F32) * 2.0 / HD)
    phases = position.astype(F32)[:, None] * frequency[None, :]
    cos, sin = jnp.cos(phases), jnp.sin(phases)
    cosine = jnp.concatenate([cos, cos], axis=1)
    sine = jnp.concatenate([-sin, sin], axis=1)

    residual = tokens.astype(F32)

    normed, wq, wo, kv_all, key_rows_t, dk2, dv2, *grad_chunks = front(
        links, doc_split, tokens, attn_gain[None], w_kv, cosine[:own], sine[:own], query_two, grad_two, w_query, w_out,
        out_grad,
    )
    normed_own = normed[:own]
    grad_chunks = [out_grad] + grad_chunks

    q_lin = mm(normed, wq, NN)
    some = q_lin.shape[1] // HD // 2
    tables = (cosine * SCALE2, sine * SCALE2)
    results = attend(sp, q_lin, *tables, kv_all, 0, some)
    results, further = lax.optimization_barrier((results, links.ring(grad_chunks[-2])))
    later_chunks = [further]
    for _ in range(3 + FRONT_HOPS, chips + 1):
        later_chunks.append(links.ring(later_chunks[-1]))
    queries, context, lse = attend(sp, q_lin, *tables, kv_all, some, q_lin.shape[1] // HD - some, results)
    branch, later_chunks = lax.optimization_barrier((mm(context, wo, NN), later_chunks))
    branch = pair_sum(links, branch)
    hidden = residual + branch
    mlp_scale = rms_factor(hidden)
    mlp_pre = hidden * mlp_scale
    hidden_own = (mlp_pre * mlp_gain).astype(BF16)

    grad_hn, mlp_terms, ffn_parts = feed_forward(links, hidden_own, grad_chunks + later_chunks, w_gate.T, w_up.T, w_down)
    mlp_came = links.ring(mlp_terms[1])
    ffn_stay, ffn_came, ffn_names = first_halving(links, ffn_parts, me_dp)

    mlp_gain_part = jnp.sum(grad_hn * mlp_pre, axis=0)
    scaled_mlp = grad_hn * mlp_gain
    grad_hidden = out_grad.astype(F32) + mlp_scale * (
        scaled_mlp - mlp_pre * jnp.mean(scaled_mlp * mlp_pre, axis=-1, keepdims=True)
    )

    grad_branch = both(links, grad_hidden.astype(BF16))
    grad_context = mm(grad_branch, wo, NT).astype(BF16)
    query_grad, dk, dv = attend_back(
        sp, queries, grad_context, context, lse, cosine * SCALE, sine * SCALE, kv_all, key_rows_t, dk2, dv2
    )
    for k in range(2, chips - 1):
        query_grad, mlp_came = lax.optimization_barrier((query_grad, mlp_came))
        mlp_sent = (mlp_terms[k].astype(F32) + mlp_came.astype(F32)).astype(BF16)
        query_grad, mlp_sent = lax.optimization_barrier((query_grad, mlp_sent))
        mlp_came = links.ring(mlp_sent)
    out_parts = mm(context, grad_branch, TN).astype(BF16)
    query_parts = mm(query_grad, normed, TN).astype(BF16).reshape(chips, width, -1)

    kv_part = jnp.concatenate([dk * (SCALE / SCALE2), dv], axis=1).reshape(chips, 2, own, 2 * HD)
    kv_part = jnp.stack(
        [
            lax.dynamic_index_in_dim(kv_part, chip ^ k, 0, keepdims=False)
            for k in range(chips)
        ]
    )
    kv_keep = lax.dynamic_index_in_dim(kv_part, core, 1, keepdims=False)
    kv_send = lax.dynamic_index_in_dim(kv_part, 1 - core, 1, keepdims=False).astype(BF16)
    gn_part = mm(query_grad, wq, NT)
    query_parts, ffn_came, mlp_came = lax.optimization_barrier((query_parts, ffn_came, mlp_came))
    mlp_sent = (mlp_terms[chips - 1].astype(F32) + mlp_came.astype(F32)).astype(BF16)
    ffn_pieces = [(a.astype(F32) + b.astype(F32)).astype(BF16) for a, b in zip(ffn_stay, ffn_came)]
    gain_part = mlp_gain_part[None]
    ffn_w, out_w, query_w, kv_w, block_output, tokens_grad, gains = tail(
        links, out_parts, query_parts, mlp_sent, ffn_pieces, ffn_names, kv_keep, kv_send, gn_part[:own],
        gn_part[own:].astype(BF16), tokens, normed_own, w_kv, cosine[:own], sine[:own], gain_part,
        attn_gain[None], grad_hidden, hidden + mlp_terms[0].astype(F32),
    )
    units = w_down.shape[0]

    gate_w_grad = ffn_w[:units].astype(F32).T
    up_w_grad = ffn_w[units : 2 * units].astype(F32).T
    down_w_grad = ffn_w[2 * units :].astype(F32)
    out_w_grad = out_w.astype(F32)
    query_w_grad = query_w.astype(F32)
    kv_w_grad = kv_w.astype(F32).T
    attn_gain_grad, mlp_gain_grad = gains[:4].reshape(-1), gains[4:].reshape(-1)

    return (
        block_output,
        tokens_grad,
        attn_gain_grad,
        mlp_gain_grad,
        query_w_grad,
        kv_w_grad,
        out_w_grad,
        gate_w_grad,
        up_w_grad,
        down_w_grad,
    )


def solution(mesh):
    both_axes = P(("dp", "tensor"), None)
    return jax.shard_map(
        functools.partial(local, mesh.shape["tensor"], mesh.shape["dp"]),
        mesh=mesh,
        in_specs=(
            both_axes,
            both_axes,
            P("dp", "tensor"),
            P("dp", "tensor"),
            P("dp"),
            P(),
            P(),
            P(None, "tensor"),
            P(),
            P("tensor", None),
            P(None, "tensor"),
            P(None, "tensor"),
            P("tensor", None),
        ),
        out_specs=(
            both_axes,
            both_axes,
            P(),
            P(),
            P(None, "tensor"),
            P(),
            P("tensor", None),
            P(None, "tensor"),
            P(None, "tensor"),
            P("tensor", None),
        ),
        check_vma=False,
    )
```

```python
import functools

import jax
import jax.numpy as jnp
from jax import lax
from jax.experimental import pallas as pl
from jax.experimental.pallas import tpu as pltpu
from jax.sharding import PartitionSpec as P

HD = 128
SEQ_SHORT = 1024
EPSILON = 1e-05
MASKED = -1e30
SCALE = HD ** (-0.5)
SCALE2 = SCALE * 1.4426950408889634
F32 = jnp.float32
BF16 = jnp.bfloat16
VMEM_LIMIT = 56 * 2**20


def mm(left, right, dims):
    return lax.dot_general(left, right, (dims, ((), ())), preferred_element_type=F32)


NN = ((1,), (0,))
NT = ((1,), (1,))
TN = ((0,), (0,))


class Links:
    def __init__(self, n_tensor, n_dp):
        self.n_tensor, self.n_dp = n_tensor, n_dp
        self.chips = n_tensor // 2
        odd = list(range(1, self.chips, 2))
        even = list(range(2, self.chips, 2))
        self.order = [0] + odd + even[::-1]
        nxt = {c: self.order[(i + 1) % self.chips] for i, c in enumerate(self.order)}
        self.place = [self.order.index(c) for c in range(self.chips)]
        self.ring_pairs = [(2 * c + k, 2 * nxt[c] + k) for c in range(self.chips) for k in (0, 1)]
        self.swap_pairs = [(i, i ^ 1) for i in range(n_tensor)]
        self.bits = [1 << b for b in range(n_dp.bit_length() - 1)]

    def ring(self, x):
        return lax.ppermute(x, "tensor", self.ring_pairs)

    def swap(self, x):
        return lax.ppermute(x, "tensor", self.swap_pairs)

    def across(self, x, bit):
        return lax.ppermute(x, "dp", [(i, i ^ bit) for i in range(self.n_dp)])

    def neighbours(self, chip):
        ahead, behind = chip * 0, chip * 0
        for i, c in enumerate(self.order):
            ahead = jnp.where(chip == c, self.order[(i + 1) % self.chips], ahead)
            behind = jnp.where(chip == c, self.order[i - 1], behind)
        return ahead, behind


def both(links, own):
    return jnp.concatenate([own, links.swap(own)], axis=0)


def pair_sum(links, part):
    rows = part.shape[0] // 2
    return part[:rows].astype(F32) + links.swap(part[rows:].astype(BF16)).astype(F32)


def diagonal(shape, row_axis, shift):
    size = shape[row_axis]
    row = lax.broadcasted_iota(jnp.int32, shape, row_axis) + shift
    row = jnp.where(row >= size, row - size, row)
    return lax.broadcasted_iota(jnp.int32, shape, 1 - row_axis) <= row


def span(block, two_docs, rows):
    per_doc = SEQ_SHORT // rows
    inner = jnp.where(two_docs > 0, lax.rem(block, per_doc), block)
    return inner + 1, pl.multiple_of((block - inner) * rows, rows)


def fwd_kernel(blocks, sp_ref, q_ref, c_ref, s_ref, k_ref, v_ref, *refs):
    qo_ref, ctx_ref, lse_ref = refs[-3:]
    rows = q_ref.shape[0]
    chip, two_docs, core = sp_ref[0], sp_ref[1], sp_ref[2]
    x = q_ref[...]
    q = (x * c_ref[...] + pltpu.roll(x, HD // 2, 1) * s_ref[...]).astype(BF16)
    qo_ref[...] = q
    count, low = span(chip, two_docs, rows)
    mask = diagonal((rows, rows), 0, core * (rows // 2))
    for n in range(1, blocks + 1):

        @pl.when(count == n)
        def _(n=n):
            near = (n - 1) * rows
            diag = pl.ds(low + near, rows)
            s_diag = jnp.where(mask, mm(q, k_ref[diag, :], NT), MASKED)
            top = jnp.max(s_diag, axis=1, keepdims=True)
            if n > 1:
                main = pl.ds(low, near)
                s_main = mm(q, k_ref[main, :], NT)
                top = jnp.maximum(top, jnp.max(s_main, axis=1, keepdims=True))
            p_diag = jnp.exp2(s_diag - top)
            total = jnp.sum(p_diag, axis=1, keepdims=True)
            out = mm(p_diag.astype(BF16), v_ref[diag, :], NN)
            if n > 1:
                p_main = jnp.exp2(s_main - top)
                total = total + jnp.sum(p_main, axis=1, keepdims=True)
                out = out + mm(p_main.astype(BF16), v_ref[main, :], NN)
            ctx_ref[...] = (out / total).astype(BF16)
            lse = jnp.broadcast_to(top + jnp.log2(total), (rows, HD))
            lse_ref[0] = lse.T[:8]


def bwd_kernel(
    blocks, sp_ref, q_ref, do_ref, ctx_ref, lse_ref, c_ref, s_ref, k_ref, kt_ref, v_ref, dk0_ref, dv0_ref,
    dq_ref, dk_ref, dv_ref,
):
    rows = q_ref.shape[0]
    chip, two_docs, core = sp_ref[0], sp_ref[1], sp_ref[2]

    @pl.when(pl.program_id(0) == 0)
    def _():
        dk_ref[...] = dk0_ref[...]
        dv_ref[...] = dv0_ref[...]

    q, do = q_ref[...], do_ref[...]
    dot = jnp.sum(do.astype(F32) * ctx_ref[...].astype(F32), axis=1, keepdims=True)
    dot = jnp.broadcast_to(dot, (rows, HD)).T[:1]
    lse = lse_ref[0, :1]
    count, low = span(chip, two_docs, rows)
    mask = diagonal((rows, rows), 1, core * (rows // 2))
    for n in range(1, blocks + 1):

        @pl.when(count == n)
        def _(n=n):
            near = (n - 1) * rows
            dqt = jnp.zeros((HD, rows), F32)
            for keys, masked in ((pl.ds(low, near), False), (pl.ds(low + near, rows), True)):
                if not masked and n == 1:
                    continue
                p = jnp.exp2(mm(k_ref[keys, :], q, NT) - lse)
                if masked:
                    p = jnp.where(mask, p, 0.0)
                ds = (p * (mm(v_ref[keys, :], do, NT) - dot)).astype(BF16)
                dv_ref[keys, :] += mm(p.astype(BF16), do, NN)
                dk_ref[keys, :] += mm(ds, q, NN)
                dqt = dqt + mm(kt_ref[:, keys], ds, NN)
            g = dqt.T
            dq_ref[...] = (g * c_ref[...] - pltpu.roll(g, HD // 2, 1) * s_ref[...]).astype(BF16)


def whole(shape):
    return pl.BlockSpec(shape, lambda *_: (0,) * len(shape))


def second_half(seq):
    return pl.BlockSpec((seq, HD), lambda *_: (0, 1))


def attend(sp, q_lin, cosine, sine, kv_all, first, count, before=()):
    rows, width = q_lin.shape
    seq = kv_all.shape[0]
    heads = width // HD
    column = pl.BlockSpec((rows, HD), lambda h, *_: (0, h + first))
    return pl.pallas_call(
        functools.partial(fwd_kernel, seq // rows),
        grid_spec=pltpu.PrefetchScalarGridSpec(
            num_scalar_prefetch=1,
            grid=(count,),
            in_specs=[column, whole((rows, HD)), whole((rows, HD)), whole((seq, HD)), second_half(seq)]
            + [pl.BlockSpec(memory_space=pl.ANY)] * len(before),
            out_specs=[column, column, pl.BlockSpec((1, 8, rows), lambda h, *_: (h + first, 0, 0))],
        ),
        out_shape=[
            jax.ShapeDtypeStruct((rows, width), BF16),
            jax.ShapeDtypeStruct((rows, width), BF16),
            jax.ShapeDtypeStruct((heads, 8, rows), F32),
        ],
        input_output_aliases={6 + i: i for i in range(len(before))},
        compiler_params=pltpu.CompilerParams(vmem_limit_bytes=VMEM_LIMIT),
        cost_estimate=pl.CostEstimate(
            flops=8 * count * rows * seq * HD, bytes_accessed=16 * rows * width, transcendentals=count * rows * seq
        ),
        name="attend",
    )(sp, q_lin, cosine, sine, kv_all, kv_all, *before)


def attend_back(sp, queries, grad_context, context, lse, cosine, sine, kv_all, key_rows_t, dk0, dv0):
    rows, width = queries.shape
    seq = kv_all.shape[0]
    heads = width // HD
    column = pl.BlockSpec((rows, HD), lambda h, *_: (0, h))
    return pl.pallas_call(
        functools.partial(bwd_kernel, seq // rows),
        grid_spec=pltpu.PrefetchScalarGridSpec(
            num_scalar_prefetch=1,
            grid=(heads,),
            in_specs=[
                column, column, column, pl.BlockSpec((1, 8, rows), lambda h, *_: (h, 0, 0)),
                whole((rows, HD)), whole((rows, HD)), whole((seq, HD)), whole((HD, seq)), second_half(seq),
                whole((seq, HD)), whole((seq, HD)),
            ],
            out_specs=[column, whole((seq, HD)), whole((seq, HD))],
        ),
        out_shape=[
            jax.ShapeDtypeStruct((rows, width), BF16),
            jax.ShapeDtypeStruct((seq, HD), F32),
            jax.ShapeDtypeStruct((seq, HD), F32),
        ],
        compiler_params=pltpu.CompilerParams(vmem_limit_bytes=VMEM_LIMIT),
        cost_estimate=pl.CostEstimate(
            flops=20 * heads * rows * seq * HD, bytes_accessed=16 * rows * width, transcendentals=heads * rows * seq
        ),
        name="attend_back",
    )(sp, queries, grad_context, context, lse, cosine, sine, kv_all, key_rows_t, kv_all, dk0, dv0)


def second_unit(block, rows, q, do, kv, dk_ref, dv_ref, late):
    mask = diagonal((rows, rows), 1, 0)
    first = block * rows
    parts = [(pl.ds(first, rows), True, False)]
    middle = SEQ_SHORT * (first // SEQ_SHORT)
    if first > middle:
        parts.append((pl.ds(middle, first - middle), False, False))
    if middle:
        parts.append((pl.ds(0, middle), False, True))
    scores = []
    for keys, masked, far in parts:
        score = mm(kv[keys, :HD], q, NT) * SCALE2
        scores.append(jnp.where(mask, score, MASKED) if masked else score + late if far else score)
    top = functools.reduce(jnp.maximum, [jnp.max(score, axis=0, keepdims=True) for score in scores])
    lifted = [jnp.exp2(score - top) for score in scores]
    inverse = 1.0 / sum(jnp.sum(p, axis=0, keepdims=True) for p in lifted)
    back = [mm(kv[keys, HD:], do, NT) for keys, _, _ in parts]
    dot = sum(jnp.sum(p * b, axis=0, keepdims=True) for p, b in zip(lifted, back)) * inverse
    for (keys, _, _), p, b in zip(parts, lifted, back):
        p = p * inverse
        dv_ref[keys, :] += mm(p.astype(BF16), do, NN)
        dk_ref[keys, :] += mm((p * (b - dot)).astype(BF16), q, NN)


FRONT_HOPS = 1
FRONT_ORDER = (
    "kv q1 o1 kv", "q1 q2 o1 o2", "kv q1 q2 q3", "kv o1 o2 o3", "g kv* s q2", "q3 s o2 o3", "s g q2 q3",
    "s o2 o3 s", "q3 s g s", "o3 s q1* o1*", "q2* o2* q3* o3*", "s* g*",
)


def front_kernel(
    links, docs, tokens, gain, w_kv, cosine, sine, q_two, g_two, wq_hbm, wo_hbm, og_hbm,
    normed, wq_out, wo_out, kv_out, kt_ref, dk_ref, dv_ref, *refs,
):
    og_outs, (kv, ss, rs, ls) = refs[:-4], refs[-4:]
    chips, bits, n_dp = links.chips, links.bits, links.n_dp
    own, depth = tokens.shape
    seq = own * links.n_tensor
    width = wq_hbm.shape[1]
    me = lax.axis_index("tensor")
    me_dp = lax.axis_index("dp")
    chip, core = me // 2, lax.rem(me, 2)
    ahead, behind = links.neighbours(chip)
    right = {"tensor": ahead * 2 + core}
    left = {"tensor": behind * 2 + core}
    sibling = {"tensor": me ^ 1}
    barrier = pltpu.get_barrier_semaphore()
    peers = [right, left, sibling] + [{"dp": me_dp ^ bit} for bit in bits]
    for peer in peers:
        pl.semaphore_signal(barrier, inc=1, device_id=peer, device_id_type=pl.DeviceIdType.MESH)

    copies = []

    def send(src, dst, peer):
        number = len(copies)
        copy = mesh_copy(src, dst, ss.at[number], rs.at[number], peer)
        copy.start()
        copies.append(copy)
        return copy

    def q_piece(ref, k, j, way, size=1):
        rows = depth // n_dp // 2
        at = pl.ds(pl.multiple_of((2 * j + way) * rows, rows), size * rows)
        return ref.at[at, :] if k is None else ref.at[at, pl.ds(k * width, width)]

    def o_piece(ref, k, j, way, size=1):
        rows, half = width // n_dp, depth // 2
        at = pl.ds(pl.multiple_of((k or 0) * width + j * rows, rows), rows)
        return ref.at[at, pl.ds(way * half, size * half)]

    pl.semaphore_wait(barrier, len(peers))
    locals_ = [
        pltpu.make_async_copy(wq_hbm, wq_out.at[:, pl.ds(0, width)], ls.at[0]),
        pltpu.make_async_copy(wo_hbm, wo_out.at[pl.ds(0, width), :], ls.at[1]),
    ]
    for copy in locals_:
        copy.start()
    hops = {}
    for name, piece, src, dst in (("q", q_piece, wq_hbm, wq_out), ("o", o_piece, wo_hbm, wo_out)):
        hops[name, 1] = send(piece(src, None, me_dp, 0, 2), piece(dst, 1, me_dp, 0, 2), right)

    x = tokens[...].astype(F32)
    own_rows = pl.ds(0, own)
    normed[own_rows] = (x * lax.rsqrt(jnp.mean(x * x, axis=1, keepdims=True) + EPSILON) * gain[...]).astype(BF16)
    normed_swap = send(normed.at[own_rows], normed.at[pl.ds(own, own)], sibling)
    lin = mm(normed[own_rows], w_kv[...], NN)
    key = lin[:, :HD] * cosine[...] + pltpu.roll(lin[:, :HD], HD // 2, 1) * sine[...]

    def chip_up(k):
        found = chip * 0
        for i, c in enumerate(links.order):
            found = jnp.where(chip == c, links.order[(i - k) % chips], found)
        return found

    def kv_at(k):
        return kv.at[pl.ds(pl.multiple_of((chip_up(k) * 2 + core) * own, own), own)]

    kv_at(0)[...] = jnp.concatenate([key, lin[:, HD:]], axis=1).astype(BF16)
    late = jnp.where(docs[0] > 0, MASKED, 0.0)
    dk_ref[...] = jnp.zeros_like(dk_ref)
    dv_ref[...] = jnp.zeros_like(dv_ref)

    def kv_chain():
        swaps = []
        for k in range(chips):
            copy = send(kv_at(k), kv_at(k), right) if k + 1 < chips else None
            swaps.append(send(kv_at(k), kv_at(k), sibling))
            yield
            if copy is not None:
                copy.wait_recv()
        for copy in swaps:
            copy.wait_recv()
        store = pltpu.make_async_copy(kv, kv_out, ls.at[2])
        store.start()
        locals_.append(store)
        kt_ref[...] = kv[:, :HD].T

    def block_chain(name, piece, dst, k):
        hops[name, k].wait_recv()
        if k + 1 < chips:
            hops[name, k + 1] = send(piece(dst, k, me_dp, 0, 2), piece(dst, k + 1, me_dp, 0, 2), right)
        held = [[0], [0]]
        for step in range(len(bits)):
            sent = []
            for rank in range(len(held[0])):
                for way, order in enumerate((bits, bits[::-1])):
                    bit, rel = order[step], held[way][rank]
                    where = piece(dst, k, me_dp ^ rel, way)
                    sent.append((send(where, where, {"dp": me_dp ^ bit}), way, rel ^ bit))
            yield
            for copy, way, rel in sent:
                copy.wait_recv()
                held[way].append(rel)

    def grad_chain():
        source = og_hbm
        swaps = [send(og_hbm, og_outs[0], sibling)]
        for i in range(1, len(og_outs), 2):
            hop = send(source, og_outs[i], right)
            yield
            hop.wait_recv()
            source = og_outs[i]
            swaps.append(send(source, og_outs[i + 1], sibling))
        yield
        for copy in swaps:
            copy.wait_recv()

    rows = min(512, SEQ_SHORT)
    heads = q_two.shape[1] // HD

    def second_chain():
        for block in reversed(range(seq // rows)):
            for head in range(heads):
                at = (pl.ds(block * rows, rows), pl.ds(head * HD, HD))
                second_unit(block, rows, q_two[at], g_two[at], kv, dk_ref, dv_ref, late)
                yield
        dk_ref[...] *= SCALE2

    chains = {"kv": kv_chain(), "s": second_chain(), "g": grad_chain()}
    for k in range(1, chips):
        chains["q%d" % k] = block_chain("q", q_piece, wq_out, k)
        chains["o%d" % k] = block_chain("o", o_piece, wo_out, k)
    take_turns(chains, FRONT_ORDER)
    normed_swap.wait_recv()
    for copy in copies:
        copy.wait_send()
    for copy in locals_:
        copy.wait()


def take_turns(chains, order):
    def turn(name):
        if name in chains and next(chains[name], chains) is chains:
            del chains[name]

    for name in " ".join(order).split():
        turn(name.rstrip("*"))
        while name.endswith("*") and name.rstrip("*") in chains:
            turn(name.rstrip("*"))
    while chains:
        for name in list(chains):
            turn(name)


def front(links, docs, tokens, gain, w_kv, cosine, sine, q_two, g_two, w_query, w_out, out_grad):
    chips = links.chips
    own, depth = tokens.shape
    seq = own * links.n_tensor
    width = w_query.shape[1]
    anywhere = pl.BlockSpec(memory_space=pl.ANY)
    here = pl.BlockSpec(memory_space=pltpu.VMEM)
    dma = pltpu.SemaphoreType.DMA
    shape = jax.ShapeDtypeStruct
    count = 2 * chips * (2 * links.n_dp) + 4 * chips + 8
    hops = min(FRONT_HOPS, chips - 1)
    return pl.pallas_call(
        functools.partial(front_kernel, links),
        in_specs=[pl.BlockSpec(memory_space=pltpu.SMEM)] + [here] * 7 + [anywhere] * 3,
        out_specs=[here] + [anywhere] * 3 + [here] * 3 + [anywhere] * (1 + 2 * hops),
        out_shape=[
            shape((2 * own, depth), BF16), shape((depth, chips * width), BF16), shape((chips * width, depth), BF16),
            shape((seq, 2 * HD), BF16), shape((HD, seq), BF16), shape((seq, HD), F32), shape((seq, HD), F32),
        ]
        + [shape((own, depth), BF16)] * (1 + 2 * hops),
        scratch_shapes=[pltpu.VMEM((seq, 2 * HD), BF16), dma((count,)), dma((count,)), dma((3,))],
        compiler_params=pltpu.CompilerParams(
            collective_id=3, has_side_effects=True, vmem_limit_bytes=VMEM_LIMIT
        ),
        cost_estimate=pl.CostEstimate(flops=10**10, bytes_accessed=64 * 2**20, transcendentals=0),
        name="front",
    )(docs, tokens, gain, w_kv, cosine, sine, q_two, g_two, w_query, w_out, out_grad)


def mlp_kernel(
    links, h_hbm, wg_hbm, wu_hbm, wd_hbm, *refs,
):
    paired = 1 + min(FRONT_HOPS, links.chips - 1)
    given = [(k, half) for k in range(links.chips) for half in ((0, 1) if k < paired else (0,))]
    g_hbm, refs = refs[: len(given)], refs[len(given) :]
    (
    ghn_ref, mlp_hbm, grads_hbm, h_all, g_all, wg, wu, wd, act_t, gg_t, gu_t, mlp_in, stage, pair_out, pair_in, ring_out, ring_in,
    load_sem, ring_s, ring_r, swap_s, swap_r, pair_s, pair_r, rs_s, rs_r, mlp_s, mlp_r,
    stage_sem, store_sem, g_s, g_r,
    ) = refs
    chips = links.chips
    own, depth = h_hbm.shape
    seq = chips * 2 * own
    me = lax.axis_index("tensor")
    chip, core = me // 2, lax.rem(me, 2)
    ahead, behind = links.neighbours(chip)
    right = {"tensor": ahead * 2 + core}
    left = {"tensor": behind * 2 + core}
    sibling = {"tensor": chip * 2 + 1 - core}

    loads = [
        pltpu.make_async_copy(h_hbm, h_all.at[0, 0], load_sem.at[0]),
        pltpu.make_async_copy(wg_hbm, wg, load_sem.at[1]),
        pltpu.make_async_copy(wu_hbm, wu, load_sem.at[2]),
        pltpu.make_async_copy(wd_hbm, wd, load_sem.at[3]),
    ] + [
        pltpu.make_async_copy(ref, g_all.at[at], load_sem.at[4 + i]) for i, (ref, at) in enumerate(zip(g_hbm, given))
    ]
    for load in loads:
        load.start()
    barrier = pltpu.get_barrier_semaphore()
    for peer in (right, left, sibling):
        pl.semaphore_signal(barrier, inc=1, device_id=peer, device_id_type=pl.DeviceIdType.MESH)
    pl.semaphore_wait(barrier, 3)

    def remote(src, dst, send, recv, peer):
        return pltpu.make_async_remote_copy(
            src_ref=src, dst_ref=dst, send_sem=send, recv_sem=recv, device_id=peer,
            device_id_type=pl.DeviceIdType.MESH,
        )

    def ring(k):
        return remote(h_all.at[k, 0], h_all.at[k + 1, 0], ring_s.at[k], ring_r.at[k], right)

    def swap(k):
        return remote(h_all.at[k, 0], h_all.at[k, 1], swap_s.at[k], swap_r.at[k], sibling)

    def g_swap(k):
        return remote(g_all.at[k, 0], g_all.at[k, 1], g_s.at[k], g_r.at[k], sibling)

    def pair(k):
        slot = lax.rem(k, 2)
        return remote(pair_out.at[slot], pair_in.at[slot], pair_s.at[slot], pair_r.at[slot], sibling)

    def scatter(k):
        slot = lax.rem(k, 2)
        return remote(ring_out.at[slot], ring_in.at[k], rs_s.at[k], rs_r.at[k], right)

    def mlp_pair(k):
        slot = lax.rem(k, 2)
        return remote(stage.at[1], mlp_in.at[slot], mlp_s.at[slot], mlp_r.at[slot], sibling)

    def store(k):
        return pltpu.make_async_copy(stage.at[0], mlp_hbm.at[k], stage_sem.at[0])

    loads[0].wait()
    ring(0).start()
    swap(0).start()
    for load in loads[1:]:
        load.wait()
    for k in range(paired, chips):
        g_swap(k).start()

    def hidden_units(k, half):
        h, g = h_all[k, half], g_all[k, half]
        gate = mm(h, wg[...], NT)
        upward = mm(h, wu[...], NT)
        grad_act = mm(g, wd[...], NT)
        sigma = jax.nn.sigmoid(gate)
        swish = gate * sigma
        act = (swish * upward).astype(BF16)
        gg = (grad_act * upward * sigma * (1.0 + gate * (1.0 - sigma))).astype(BF16)
        gu = (grad_act * swish).astype(BF16)
        return act, gg, gu

    def keep_units(k, half, act, gg, gu):
        columns = pl.ds(pl.multiple_of((2 * k + half) * own, own), own)
        act_t[:, columns] = act.T
        gg_t[:, columns] = gg.T
        gu_t[:, columns] = gu.T

    def chunk(k, _):
        @pl.when(k >= 1)
        def _():
            ring(k - 1).wait_recv()

            @pl.when(k < chips - 1)
            def _():
                ring(k).start()

            swap(k).start()

        act0, gg0, gu0 = hidden_units(k, 0)
        swap(k).wait_recv()

        @pl.when(k >= paired)
        def _():
            g_swap(k).wait_recv()

        act1, gg1, gu1 = hidden_units(k, 1)

        @pl.when(k >= 2)
        def _():
            pair(k - 2).wait_send()

        pair_out[lax.rem(k, 2)] = (mm(gg1, wg[...], NN) + mm(gu1, wu[...], NN)).astype(BF16)
        pair(k).start()
        part = mm(gg0, wg[...], NN) + mm(gu0, wu[...], NN)
        pair(k).wait_recv()
        total = part + pair_in[lax.rem(k, 2)].astype(F32)

        @pl.when(k == 0)
        def _():
            ghn_ref[...] = total

        @pl.when(k == 1)
        def _():
            ring_out[1] = total.astype(BF16)
            scatter(k).start()

        @pl.when(k >= 2)
        def _():
            scatter(k - 1).wait_recv()

            @pl.when(k >= 3)
            def _():
                scatter(k - 2).wait_send()

            ring_out[lax.rem(k, 2)] = (total + ring_in[k - 1].astype(F32)).astype(BF16)
            scatter(k).start()

        @pl.when(k >= 1)
        def _():
            mlp_pair(k - 1).wait_send()

        stage[1] = mm(act1, wd[...], NN).astype(BF16)
        mlp_pair(k).start()
        keep_units(k, 0, act0, gg0, gu0)
        keep_units(k, 1, act1, gg1, gu1)
        mine = mm(act0, wd[...], NN)
        mlp_pair(k).wait_recv()

        @pl.when(k >= 1)
        def _():
            store(k - 1).wait()

        stage[0] = (mine + mlp_in[lax.rem(k, 2)].astype(F32)).astype(BF16)
        store(k).start()
        return 0

    lax.fori_loop(0, chips, chunk, 0)

    tile = 512

    def columns_of(j, _):
        at = pl.ds(pl.multiple_of(j * tile, tile), tile)
        h = h_all[:, :, :, at].reshape(seq, tile)
        g = g_all[:, :, :, at].reshape(seq, tile)
        wg[:, at] = mm(gg_t[...], h, NN).astype(BF16)
        wu[:, at] = mm(gu_t[...], h, NN).astype(BF16)
        wd[:, at] = mm(act_t[...], g, NN).astype(BF16)
        return 0

    lax.fori_loop(0, depth // tile, columns_of, 0)
    units, (pieces, _, piece) = wg.shape[0], grads_hbm.shape
    stores = [
        pltpu.make_async_copy(
            w.at[:, pl.ds(j * piece, piece)], grads_hbm.at[j, pl.ds(i * units, units)], store_sem.at[i, j]
        )
        for i, w in enumerate((wg, wu, wd))
        for j in range(pieces)
    ]
    for copy in stores:
        copy.start()
    scatter(chips - 1).wait_recv()
    ghn_ref[...] += ring_in[chips - 1].astype(F32)

    for copy in stores:
        copy.wait()
    store(chips - 1).wait()
    mlp_pair(chips - 1).wait_send()
    for k in (chips - 2, chips - 1):
        pair(k).wait_send()
        scatter(k).wait_send()
    for k in range(chips):
        swap(k).wait_send()
    for k in range(paired, chips):
        g_swap(k).wait_send()
    for k in range(chips - 1):
        ring(k).wait_send()


def feed_forward(links, hidden_own, grad_chunks, gate_t, up_t, down):
    own, depth = hidden_own.shape
    chips, units = links.chips, down.shape[0]
    seq = chips * 2 * own
    pieces = 2 * links.n_dp
    anywhere = pl.BlockSpec(memory_space=pl.ANY)
    dma = pltpu.SemaphoreType.DMA
    return pl.pallas_call(
        functools.partial(mlp_kernel, links),
        in_specs=[anywhere] * (4 + len(grad_chunks)),
        out_specs=[pl.BlockSpec(memory_space=pltpu.VMEM)] + [anywhere] * 2,
        out_shape=[
            jax.ShapeDtypeStruct((own, depth), F32),
            jax.ShapeDtypeStruct((chips, own, depth), BF16),
            jax.ShapeDtypeStruct((pieces, 3 * units, depth // pieces), BF16),
        ],
        scratch_shapes=[
            pltpu.VMEM((chips, 2, own, depth), BF16),
            pltpu.VMEM((chips, 2, own, depth), BF16),
            pltpu.VMEM((units, depth), BF16),
            pltpu.VMEM((units, depth), BF16),
            pltpu.VMEM((units, depth), BF16),
            pltpu.VMEM((units, seq), BF16),
            pltpu.VMEM((units, seq), BF16),
            pltpu.VMEM((units, seq), BF16),
            pltpu.VMEM((2, own, depth), BF16),
            pltpu.VMEM((2, own, depth), BF16),
            pltpu.VMEM((2, own, depth), BF16),
            pltpu.VMEM((2, own, depth), BF16),
            pltpu.VMEM((2, own, depth), BF16),
            pltpu.VMEM((chips, own, depth), BF16),
            dma((4 + len(grad_chunks),)),
            dma((chips,)), dma((chips,)), dma((chips,)), dma((chips,)), dma((2,)), dma((2,)),
            dma((chips,)), dma((chips,)), dma((2,)), dma((2,)), dma((1,)), dma((3, pieces)), dma((chips,)), dma((chips,)),
        ],
        compiler_params=pltpu.CompilerParams(
            collective_id=1, has_side_effects=True, vmem_limit_bytes=60 * 2**20
        ),
        cost_estimate=pl.CostEstimate(
            flops=18 * seq * depth * units, bytes_accessed=64 * 2**20, transcendentals=seq * units
        ),
        name="feed_forward",
    )(hidden_own, gate_t, up_t, down, *grad_chunks)


def mesh_copy(src, dst, send, recv, peer):
    return pltpu.make_async_remote_copy(
        src_ref=src, dst_ref=dst, send_sem=send, recv_sem=recv, device_id=peer,
        device_id_type=pl.DeviceIdType.MESH,
    )


def add_into(dst, src, rows):
    band = max(b for b in range(16, 353, 16) if rows % b == 0)

    def step(i, _):
        at = pl.ds(pl.multiple_of(i * band, band), band)
        dst[at, :] = (dst[at, :].astype(F32) + src[at, :].astype(F32)).astype(BF16)
        return 0

    lax.fori_loop(0, rows // band, step, 0)


class DpSum:
    def __init__(self, links, send, me, buf, got, free, first=0, rows=None):
        self.first, self.rows = first, rows or buf.shape[1]
        self.links, self.send, self.me, self.buf, self.got, self.free = links, send, me, buf, got, free
        self.n = links.n_dp
        self.ways = [links.bits, links.bits[::-1]]
        self.pending = []

    def at(self, way, rel):
        return way * self.n + (self.me ^ rel)

    def view(self, way, rel):
        return self.buf.at[self.at(way, rel), pl.ds(0, self.rows)]

    def kept(self, way, step):
        done = sum(self.ways[way][: step + 1])
        return [r for r in range(self.n) if r & done == 0]

    def first_slot(self, step):
        return sum(self.n >> (i + 1) for i in range(self.first, step))

    def peer(self, bit):
        return {"dp": self.me ^ bit}

    def start_halving(self, step):
        self.pending = []
        for rank in range(self.n >> (step + 1)):
            for way in (0, 1):
                bit = self.ways[way][step]
                rel = self.kept(way, step)[rank]
                slot = self.first_slot(step) + rank
                copy = self.send(self.buf.at[self.at(way, rel ^ bit)], self.got.at[way, slot], self.peer(bit), False)
                self.pending.append((copy, way, rel, slot))
        self.step = step

    def finish_halving(self):
        for copy, way, rel, slot in self.pending:
            copy.wait_recv()
            add_into(self.buf.at[self.at(way, rel)], self.got.at[way, slot], self.buf.shape[1])
        for copy, _, _, _ in self.pending:
            copy.wait_send()
        for way in (0, 1):
            pl.semaphore_signal(
                self.free.at[way, self.step], inc=1, device_id=self.peer(self.ways[way][self.step]),
                device_id_type=pl.DeviceIdType.MESH,
            )

    def start_doubling(self, step):
        self.pending = []
        if step >= self.first:
            for way in (0, 1):
                pl.semaphore_wait(self.free.at[way, step], 1)
        for rank in range(self.n >> (step + 1)):
            for way in (0, 1):
                bit = self.ways[way][step]
                rel = self.kept(way, step)[rank]
                where = self.view(way, rel)
                self.pending.append((self.send(where, where, self.peer(bit)), way, rel ^ bit))

    def finish_doubling(self):
        for copy, _, _ in self.pending:
            copy.wait_recv()
        return [(way, rel) for _, way, rel in self.pending]

    def chain(self, done, middle=()):
        rounds = len(self.links.bits)
        for step in range(self.first, rounds):
            self.start_halving(step)
            yield
            self.finish_halving()
        yield from middle
        for step in reversed(range(rounds)):
            self.start_doubling(step)
            if step == rounds - 1:
                done(0, 0)
                done(1, 0)
            yield
            for way, rel in self.finish_doubling():
                done(way, rel)


def first_halving(links, parts, me):
    n = links.n_dp
    stay, came, names = [], [], []
    for way, bits in enumerate((links.bits, links.bits[::-1])):
        for rel in range(n):
            if rel & bits[0] == 0:
                stay.append(lax.dynamic_index_in_dim(parts, way * n + (me ^ rel), 0, keepdims=False))
                other = lax.dynamic_index_in_dim(parts, way * n + (me ^ rel ^ bits[0]), 0, keepdims=False)
                came.append(links.across(other, bits[0]))
                names.append((way, rel))
    return stay, came, names


def tail_kernel(
    links, names, *refs,
):
    w_hbm, refs = refs[: len(names)], refs[len(names) :]
    (
        o_hbm, q_hbm, m_hbm, kv_keep, kv_send, gn_keep, gn_send, tokens, normed, w_kv, cosine, sine, gain_part,
        gain, grad_hidden, hidden, terms,
        ws_hbm, ow_hbm, qw_hbm, kvw_hbm, block_ref, grad_ref, gains_ref,
        o_buf, o_in, o_ring, q_buf, q_in, w_buf, w_in, c_buf, c_in, b_buf, b_in, b_turned, got, mine, m_sem,
        kv_got, kv_ring, kv_in, gn_got, kvw_half, kvw_got, kvw_in, kvw_all, gains_in,
        ss, rs, o_sem, q_sem, w_sem, out_sem, w_free, o_free, b_free,
    ) = refs
    chips, bits = links.chips, links.bits
    n_dp = links.n_dp
    width = q_buf.shape[1]
    piece = w_buf.shape[2]
    me = lax.axis_index("tensor")
    me_dp = lax.axis_index("dp")
    chip, core = me // 2, lax.rem(me, 2)
    ahead, behind = links.neighbours(chip)
    right = {"tensor": ahead * 2 + core}
    left = {"tensor": behind * 2 + core}
    sibling = {"tensor": me ^ 1}
    column = [None] + [{"tensor": me ^ (2 * k)} for k in range(1, chips)]
    group = [{"tensor": me ^ k} for k in range(1, links.n_tensor)]
    replicas = [{"dp": me_dp ^ k} for k in range(1, n_dp)]

    w_loads = [
        pltpu.make_async_copy(ref, w_buf.at[way * n_dp + (me_dp ^ rel)], w_sem.at[i])
        for i, (ref, (way, rel)) in enumerate(zip(w_hbm, names))
    ]
    loads = {}
    for k in list(range(1, chips)) + [0]:
        loads["q", k] = pltpu.make_async_copy(q_hbm.at[k], q_buf.at[k], q_sem.at[k])
    o_loads = [
        pltpu.make_async_copy(o_hbm.at[:, pl.ds(j * piece, piece)], o_buf.at[j], o_sem.at[j]) for j in range(2 * n_dp)
    ]
    for load in o_loads + list(loads.values()) + w_loads:
        load.start()
    barrier = pltpu.get_barrier_semaphore()
    peers = [right, left] + group + replicas
    for peer in peers:
        pl.semaphore_signal(barrier, inc=1, device_id=peer, device_id_type=pl.DeviceIdType.MESH)
    pl.semaphore_wait(barrier, len(peers))

    copies, opened, locals_ = [], [], []

    def send(src, dst, peer, later=True):
        number = len(copies)
        copy = mesh_copy(src, dst, ss.at[number], rs.at[number], peer)
        copy.start()
        copies.append(copy)
        if later:
            opened.append(copy)
        return copy

    def put(src, dst):
        copy = pltpu.make_async_copy(src, dst, out_sem.at[len(locals_)])
        copy.start()
        locals_.append(copy)

    def ring_chain(name, buf, got):
        copy = None
        for k in list(range(1, chips)) + [0]:
            loads[name, k].wait()
            if copy is not None:
                copy.wait_recv()
                add_into(buf.at[k], got.at[(k - 1) % chips - 1], buf.shape[1])
            if k:
                copy = send(buf.at[k], got.at[k - 1], right)
            yield

    kv_swap = send(kv_send, kv_got, sibling)
    gn_swap = send(gn_send, gn_got, sibling)
    held = {}

    def kv_chain():
        kv_swap.wait_recv()
        sent = []
        for k in range(1, chips):
            kv_ring[k - 1] = (kv_keep[k] + kv_got[k].astype(F32)).astype(BF16)
            sent.append(send(kv_ring.at[k - 1], kv_in.at[k - 1], column[k]))
        yield
        total = kv_keep[0] + kv_got[0].astype(F32)
        for k, copy in enumerate(sent):
            copy.wait_recv()
            total = total + kv_in[k].astype(F32)
        key_grad = total[:, :HD]
        key_grad = key_grad * cosine[...] - pltpu.roll(key_grad, HD // 2, 1) * sine[...]
        kv_lin = jnp.concatenate([key_grad, total[:, HD:]], axis=1).astype(BF16)
        kv_lin_t = kv_lin.T
        for half in (0, 1):
            kvw_half[half] = mm(kv_lin_t[half * HD : (half + 1) * HD], normed[...], NN).astype(BF16)
        held["swap"] = send(kvw_half.at[1 - core], kvw_got, sibling)
        yield
        gn_swap.wait_recv()
        grad = gn_keep[...] + gn_got[...].astype(F32) + mm(kv_lin, w_kv[...], NT)
        x = tokens[...].astype(F32)
        factor = lax.rsqrt(jnp.mean(x * x, axis=1, keepdims=True) + EPSILON)
        x = x * factor
        part = jnp.sum(grad * x, axis=0, keepdims=True)
        scaled = grad * gain[...]
        back = scaled - x * jnp.mean(scaled * x, axis=1, keepdims=True)
        grad_ref[...] = (grad_hidden[...] + factor * back).astype(BF16)
        lanes = gains_ref.shape[1]
        gains_ref[...] = jnp.concatenate(
            [v[:, i * lanes : (i + 1) * lanes] for v in (part, gain_part[...]) for i in range(4)], axis=0
        )

    def gains_chain():
        done = 0
        for stage in (group, replicas):
            sent = [send(gains_ref, gains_in.at[done + i], peer, False) for i, peer in enumerate(stage)]
            yield
            total = gains_ref[...]
            for i, copy in enumerate(sent):
                copy.wait_recv()
                copy.wait_send()
                total = total + gains_in[done + i]
            gains_ref[...] = total
            done += len(stage)

    band = HD // chips

    def rows_of(k):
        return pl.ds(pl.multiple_of((chip ^ k) * band, band), band)

    def kvw_chain():
        held["swap"].wait_recv()
        add_into(kvw_half.at[core], kvw_got, HD)
        sent = [send(kvw_half.at[core, rows_of(k)], kvw_in.at[k - 1], column[k]) for k in range(1, chips)]
        yield
        total = kvw_half[core, rows_of(0)].astype(F32)
        for k, copy in enumerate(sent):
            copy.wait_recv()
            total = total + kvw_in[k].astype(F32)
        c_buf[...] = total.astype(BF16)

    sum_w = DpSum(links, send, me_dp, w_buf, w_in, w_free, 1)
    sum_o = DpSum(links, send, me_dp, o_buf, o_in, o_free, 0, width)
    sum_b = DpSum(links, send, me_dp, b_buf, b_in, b_free)

    def columns(ref, number):
        return ref.at[:, pl.ds(pl.multiple_of(number * piece, piece), piece)]

    def w_chain():
        for load in w_loads:
            load.wait()
        yield from sum_w.chain(lambda way, rel: put(w_buf.at[sum_w.at(way, rel)], columns(ws_hbm, sum_w.at(way, rel))))

    def o_ring_chain():
        sent = []
        for k in list(range(1, chips)) + [0]:
            rows = pl.ds(k * width, width)
            for way, copy in enumerate(sent):
                copy.wait_recv()
                add_into(o_buf.at[sum_o.at(way, 0), rows], o_ring.at[(k - 1) % chips - 1, way], width)
            if k:
                sent = [
                    send(o_buf.at[sum_o.at(way, 0), rows], o_ring.at[k - 1, way], right) for way in (0, 1)
                ]
                yield

    def o_chain():
        for load in o_loads:
            load.wait()
        yield from sum_o.chain(
            lambda way, rel: put(sum_o.view(way, rel), columns(ow_hbm, sum_o.at(way, rel))), o_ring_chain()
        )

    def c_chain():
        sent = [send(c_buf, c_in.at[i], peer) for i, peer in enumerate(replicas)]
        yield
        total = c_buf[...].astype(F32)
        for i, copy in enumerate(sent):
            copy.wait_recv()
            total = total + c_in[i].astype(F32)
        kvw_all[0, core] = total.astype(BF16)
        sent = [send(kvw_all.at[0, core], kvw_all.at[k, core], column[k]) for k in range(1, chips)]
        yield
        for copy in sent:
            copy.wait_recv()
        copy = send(kvw_all.at[:, core], kvw_all.at[:, core], sibling)
        yield
        copy.wait_recv()
        for k in range(chips):
            for half in (0, 1):
                to = pl.ds(pl.multiple_of(half * HD + (chip ^ k) * band, band), band)
                put(kvw_all.at[k, half], kvw_hbm.at[to])

    def b_chain():
        for j in range(2 * n_dp):
            b_buf[j] = q_buf[0, :, pl.ds(j * piece, piece)]

        def turn_over(way, rel):
            at = sum_b.at(way, rel)
            b_turned[at] = b_buf[at].T
            put(b_turned.at[at], qw_hbm.at[pl.ds(pl.multiple_of(at * piece, piece), piece)])

        yield from sum_b.chain(turn_over)

    def m_chain():
        copy = send(m_hbm, got, right)
        load = pltpu.make_async_copy(terms.at[0], mine, m_sem.at[0])
        load.start()
        yield
        load.wait()
        copy.wait_recv()
        block_ref[...] = (hidden[...] + mine[...].astype(F32) + got[...].astype(F32)).astype(BF16)

    chains = {
        "w": w_chain(), "o": o_chain(), "q": ring_chain("q", q_buf, q_in), "kv": kv_chain(),
        "g": gains_chain(), "kvw": kvw_chain(), "m": m_chain(), "c": c_chain(), "b": b_chain(),
    }

    take_turns(chains, TAIL_ORDER)
    for copy in opened:
        copy.wait_send()
    for copy in locals_:
        copy.wait()


TAIL_ORDER = (
    "o kv w kv", "kvw kvw q c", "o c w o", "c o q kv", "g o w q", "g q m g", "b o b c", "o b o b", "b w m",
)


def tail(
    links, o_parts, q_parts, m_part, w_pieces, names, kv_keep, kv_send, gn_keep, gn_send, tokens, normed, w_kv, cosine,
    sine, gain_part, gain, grad_hidden, hidden, terms,
):
    chips, width, depth = q_parts.shape
    own = tokens.shape[0]
    rows, piece = w_pieces[0].shape
    band = HD // chips
    n = links.n_dp
    pieces = 2 * n
    anywhere = pl.BlockSpec(memory_space=pl.ANY)
    here = pl.BlockSpec(memory_space=pltpu.VMEM)
    dma = pltpu.SemaphoreType.DMA
    shape = jax.ShapeDtypeStruct
    count = 20 * chips + 20 * n + 16
    return pl.pallas_call(
        functools.partial(tail_kernel, links, names),
        in_specs=[anywhere] * (3 + len(names)) + [here] * 13 + [anywhere],
        out_specs=[anywhere] * 4 + [here] * 3,
        out_shape=[
            shape((rows, depth), BF16), shape((width, depth), BF16),
            shape((depth, width), BF16), shape((2 * HD, depth), BF16), shape((own, depth), BF16),
            shape((own, depth), BF16), shape((8, depth // 4), F32),
        ],
        scratch_shapes=[
            pltpu.VMEM((pieces, chips * width, piece), BF16), pltpu.VMEM((2, n - 1, chips * width, piece), BF16),
            pltpu.VMEM((chips - 1, 2, width, piece), BF16),
            pltpu.VMEM((chips, width, depth), BF16), pltpu.VMEM((chips - 1, width, depth), BF16),
            pltpu.VMEM((pieces, rows, piece), BF16), pltpu.VMEM((2, max(1, n // 2 - 1), rows, piece), BF16),
            pltpu.VMEM((band, depth), BF16), pltpu.VMEM((n - 1, band, depth), BF16),
            pltpu.VMEM((pieces, width, piece), BF16), pltpu.VMEM((2, n - 1, width, piece), BF16),
            pltpu.VMEM((pieces, piece, width), BF16), pltpu.VMEM((own, depth), BF16),
            pltpu.VMEM((own, depth), BF16), dma((1,)),
            pltpu.VMEM((chips, own, 2 * HD), BF16),
            pltpu.VMEM((chips - 1, own, 2 * HD), BF16), pltpu.VMEM((chips - 1, own, 2 * HD), BF16),
            pltpu.VMEM((own, depth), BF16),
            pltpu.VMEM((2, HD, depth), BF16), pltpu.VMEM((HD, depth), BF16),
            pltpu.VMEM((chips - 1, band, depth), BF16),
            pltpu.VMEM((chips, 2, band, depth), BF16),
            pltpu.VMEM((links.n_tensor + n, 8, depth // 4), F32),
            dma((count,)), dma((count,)), dma((pieces,)), dma((chips,)), dma((len(names),)),
            dma((3 * pieces + 2 * chips,)),
        ]
        + [pltpu.SemaphoreType.REGULAR((2, len(links.bits)))] * 3,
        compiler_params=pltpu.CompilerParams(
            collective_id=2, has_side_effects=True, vmem_limit_bytes=60 * 2**20
        ),
        cost_estimate=pl.CostEstimate(flops=10**9, bytes_accessed=64 * 2**20, transcendentals=0),
        name="tail",
    )(
        *w_pieces, o_parts, q_parts, m_part, kv_keep, kv_send, gn_keep, gn_send, tokens, normed, w_kv, cosine, sine,
        gain_part, gain, grad_hidden, hidden, terms,
    )


def rms_factor(values):
    return lax.rsqrt(jnp.mean(values * values, axis=-1, keepdims=True) + EPSILON)


def local(
    n_tensor, n_dp,
    tokens, out_grad, query_two, grad_two, doc_split, attn_gain, mlp_gain, w_query, w_kv, w_out, w_gate, w_up, w_down,
):
    links = Links(n_tensor, n_dp)
    chips = links.chips
    own = tokens.shape[0]
    rows = 2 * own
    seq = own * n_tensor
    width = w_query.shape[1]
    me_dp = lax.axis_index("dp")
    me_t = lax.axis_index("tensor")
    chip, core = me_t // 2, me_t % 2
    two_docs = doc_split[0]
    sp = jnp.stack([chip, two_docs, core]).astype(jnp.int32)
    place = jnp.array(links.place, jnp.int32)
    order = jnp.array(links.order, jnp.int32)

    spot = jnp.arange(rows, dtype=jnp.int32) + core * own
    spot = chip * rows + jnp.where(spot >= rows, spot - rows, spot)
    position = jnp.where(two_docs > 0, spot % SEQ_SHORT, spot)
    frequency = 10000.0 ** (-jnp.arange(HD // 2, dtype=F32) * 2.0 / HD)
    phases = position.astype(F32)[:, None] * frequency[None, :]
    cos, sin = jnp.cos(phases), jnp.sin(phases)
    cosine = jnp.concatenate([cos, cos], axis=1)
    sine = jnp.concatenate([-sin, sin], axis=1)

    residual = tokens.astype(F32)

    normed, wq, wo, kv_all, key_rows_t, dk2, dv2, *grad_chunks = front(
        links, doc_split, tokens, attn_gain[None], w_kv, cosine[:own], sine[:own], query_two, grad_two, w_query, w_out,
        out_grad,
    )
    normed_own = normed[:own]
    grad_chunks = [out_grad] + grad_chunks

    q_lin = mm(normed, wq, NN)
    some = q_lin.shape[1] // HD // 2
    tables = (cosine * SCALE2, sine * SCALE2)
    results = attend(sp, q_lin, *tables, kv_all, 0, some)
    results, further = lax.optimization_barrier((results, links.ring(grad_chunks[-2])))
    later_chunks = [further]
    for _ in range(3 + FRONT_HOPS, chips + 1):
        later_chunks.append(links.ring(later_chunks[-1]))
    queries, context, lse = attend(sp, q_lin, *tables, kv_all, some, q_lin.shape[1] // HD - some, results)
    branch, later_chunks = lax.optimization_barrier((mm(context, wo, NN), later_chunks))
    branch = pair_sum(links, branch)
    hidden = residual + branch
    mlp_scale = rms_factor(hidden)
    mlp_pre = hidden * mlp_scale
    hidden_own = (mlp_pre * mlp_gain).astype(BF16)

    grad_hn, mlp_terms, ffn_parts = feed_forward(links, hidden_own, grad_chunks + later_chunks, w_gate.T, w_up.T, w_down)
    mlp_came = links.ring(mlp_terms[1])
    ffn_stay, ffn_came, ffn_names = first_halving(links, ffn_parts, me_dp)

    mlp_gain_part = jnp.sum(grad_hn * mlp_pre, axis=0)
    scaled_mlp = grad_hn * mlp_gain
    grad_hidden = out_grad.astype(F32) + mlp_scale * (
        scaled_mlp - mlp_pre * jnp.mean(scaled_mlp * mlp_pre, axis=-1, keepdims=True)
    )

    grad_branch = both(links, grad_hidden.astype(BF16))
    grad_context = mm(grad_branch, wo, NT).astype(BF16)
    query_grad, dk, dv = attend_back(
        sp, queries, grad_context, context, lse, cosine * SCALE, sine * SCALE, kv_all, key_rows_t, dk2, dv2
    )
    for k in range(2, chips - 1):
        query_grad, mlp_came = lax.optimization_barrier((query_grad, mlp_came))
        mlp_sent = (mlp_terms[k].astype(F32) + mlp_came.astype(F32)).astype(BF16)
        mlp_came = links.ring(mlp_sent)
    out_parts = mm(context, grad_branch, TN).astype(BF16)
    query_parts = mm(query_grad, normed, TN).astype(BF16).reshape(chips, width, -1)

    kv_part = jnp.concatenate([dk * (SCALE / SCALE2), dv], axis=1).reshape(chips, 2, own, 2 * HD)
    kv_part = jnp.stack(
        [
            lax.dynamic_index_in_dim(kv_part, chip ^ k, 0, keepdims=False)
            for k in range(chips)
        ]
    )
    kv_keep = lax.dynamic_index_in_dim(kv_part, core, 1, keepdims=False)
    kv_send = lax.dynamic_index_in_dim(kv_part, 1 - core, 1, keepdims=False).astype(BF16)
    gn_part = mm(query_grad, wq, NT)
    mlp_sent = (mlp_terms[chips - 1].astype(F32) + mlp_came.astype(F32)).astype(BF16)
    ffn_pieces = [(a.astype(F32) + b.astype(F32)).astype(BF16) for a, b in zip(ffn_stay, ffn_came)]
    gain_part = mlp_gain_part[None]
    ffn_w, out_w, query_w, kv_w, block_output, tokens_grad, gains = tail(
        links, out_parts, query_parts, mlp_sent, ffn_pieces, ffn_names, kv_keep, kv_send, gn_part[:own],
        gn_part[own:].astype(BF16), tokens, normed_own, w_kv, cosine[:own], sine[:own], gain_part,
        attn_gain[None], grad_hidden, hidden, mlp_terms,
    )
    units = w_down.shape[0]

    gate_w_grad = ffn_w[:units].astype(F32).T
    up_w_grad = ffn_w[units : 2 * units].astype(F32).T
    down_w_grad = ffn_w[2 * units :].astype(F32)
    out_w_grad = out_w.astype(F32)
    query_w_grad = query_w.astype(F32)
    kv_w_grad = kv_w.astype(F32).T
    attn_gain_grad, mlp_gain_grad = gains[:4].reshape(-1), gains[4:].reshape(-1)

    return (
        block_output,
        tokens_grad,
        attn_gain_grad,
        mlp_gain_grad,
        query_w_grad,
        kv_w_grad,
        out_w_grad,
        gate_w_grad,
        up_w_grad,
        down_w_grad,
    )


def solution(mesh):
    both_axes = P(("dp", "tensor"), None)
    return jax.shard_map(
        functools.partial(local, mesh.shape["tensor"], mesh.shape["dp"]),
        mesh=mesh,
        in_specs=(
            both_axes,
            both_axes,
            P("dp", "tensor"),
            P("dp", "tensor"),
            P("dp"),
            P(),
            P(),
            P(None, "tensor"),
            P(),
            P("tensor", None),
            P(None, "tensor"),
            P(None, "tensor"),
            P("tensor", None),
        ),
        out_specs=(
            both_axes,
            both_axes,
            P(),
            P(),
            P(None, "tensor"),
            P(),
            P("tensor", None),
            P(None, "tensor"),
            P(None, "tensor"),
            P("tensor", None),
        ),
        check_vma=False,
    )
```

```python
import functools

import jax
import jax.numpy as jnp
from jax import lax
from jax.experimental import pallas as pl
from jax.experimental.pallas import tpu as pltpu
from jax.sharding import PartitionSpec as P

HD = 128
SEQ_SHORT = 1024
EPSILON = 1e-05
MASKED = -1e30
SCALE = HD ** (-0.5)
SCALE2 = SCALE * 1.4426950408889634
F32 = jnp.float32
BF16 = jnp.bfloat16
VMEM_LIMIT = 56 * 2**20


def mm(left, right, dims):
    return lax.dot_general(left, right, (dims, ((), ())), preferred_element_type=F32)


NN = ((1,), (0,))
NT = ((1,), (1,))
TN = ((0,), (0,))


class Links:
    def __init__(self, n_tensor, n_dp):
        self.n_tensor, self.n_dp = n_tensor, n_dp
        self.chips = n_tensor // 2
        odd = list(range(1, self.chips, 2))
        even = list(range(2, self.chips, 2))
        self.order = [0] + odd + even[::-1]
        nxt = {c: self.order[(i + 1) % self.chips] for i, c in enumerate(self.order)}
        self.place = [self.order.index(c) for c in range(self.chips)]
        self.ring_pairs = [(2 * c + k, 2 * nxt[c] + k) for c in range(self.chips) for k in (0, 1)]
        self.swap_pairs = [(i, i ^ 1) for i in range(n_tensor)]
        self.bits = [1 << b for b in range(n_dp.bit_length() - 1)]

    def ring(self, x):
        return lax.ppermute(x, "tensor", self.ring_pairs)

    def swap(self, x):
        return lax.ppermute(x, "tensor", self.swap_pairs)

    def across(self, x, bit):
        return lax.ppermute(x, "dp", [(i, i ^ bit) for i in range(self.n_dp)])

    def neighbours(self, chip):
        ahead, behind = chip * 0, chip * 0
        for i, c in enumerate(self.order):
            ahead = jnp.where(chip == c, self.order[(i + 1) % self.chips], ahead)
            behind = jnp.where(chip == c, self.order[i - 1], behind)
        return ahead, behind


def both(links, own):
    return jnp.concatenate([own, links.swap(own)], axis=0)


def pair_sum(links, part):
    rows = part.shape[0] // 2
    return part[:rows].astype(F32) + links.swap(part[rows:].astype(BF16)).astype(F32)


def diagonal(shape, row_axis, shift):
    size = shape[row_axis]
    row = lax.broadcasted_iota(jnp.int32, shape, row_axis) + shift
    row = jnp.where(row >= size, row - size, row)
    return lax.broadcasted_iota(jnp.int32, shape, 1 - row_axis) <= row


def span(block, two_docs, rows):
    per_doc = SEQ_SHORT // rows
    inner = jnp.where(two_docs > 0, lax.rem(block, per_doc), block)
    return inner + 1, pl.multiple_of((block - inner) * rows, rows)


HEADS = 2


def fwd_kernel(blocks, sp_ref, q_ref, c_ref, s_ref, k_ref, v_ref, *refs):
    qo_ref, ctx_ref, lse_ref = refs[-3:]
    rows = q_ref.shape[0]
    chip, two_docs, core = sp_ref[0], sp_ref[1], sp_ref[2]
    heads = [slice(h * HD, (h + 1) * HD) for h in range(HEADS)]
    for at in heads:
        x = q_ref[:, at]
        qo_ref[:, at] = (x * c_ref[...] + pltpu.roll(x, HD // 2, 1) * s_ref[...]).astype(BF16)
    count, low = span(chip, two_docs, rows)
    mask = diagonal((rows, rows), 0, core * (rows // 2))
    for n in range(1, blocks + 1):

        @pl.when(count == n)
        def _(n=n):
            near = (n - 1) * rows
            keys = [pl.ds(low + near, rows)] + ([pl.ds(low, near)] if n > 1 else [])
            scores = [[mm(qo_ref[:, at], k_ref[at_keys, :], NT) for at_keys in keys] for at in heads]
            for h, at in enumerate(heads):
                score = scores[h]
                score[0] = jnp.where(mask, score[0], MASKED)
                top = functools.reduce(jnp.maximum, [jnp.max(v, axis=1, keepdims=True) for v in score])
                lifted = [jnp.exp2(v - top) for v in score]
                total = sum(jnp.sum(p, axis=1, keepdims=True) for p in lifted)
                out = sum(mm(p.astype(BF16), v_ref[at_keys, :], NN) for p, at_keys in zip(lifted, keys))
                ctx_ref[:, at] = (out / total).astype(BF16)
                lse = jnp.broadcast_to(top + jnp.log2(total), (rows, HD))
                lse_ref[h] = lse.T[:8]


def bwd_kernel(
    blocks, sp_ref, q_ref, do_ref, ctx_ref, lse_ref, c_ref, s_ref, k_ref, kt_ref, v_ref, dk0_ref, dv0_ref,
    dq_ref, dk_ref, dv_ref,
):
    rows = q_ref.shape[0]
    chip, two_docs, core = sp_ref[0], sp_ref[1], sp_ref[2]

    @pl.when(pl.program_id(0) == 0)
    def _():
        dk_ref[...] = dk0_ref[...]
        dv_ref[...] = dv0_ref[...]

    heads = [slice(h * HD, (h + 1) * HD) for h in range(HEADS)]
    dots = []
    for at in heads:
        dot = jnp.sum(do_ref[:, at].astype(F32) * ctx_ref[:, at].astype(F32), axis=1, keepdims=True)
        dots.append(jnp.broadcast_to(dot, (rows, HD)).T[:1])
    count, low = span(chip, two_docs, rows)
    mask = diagonal((rows, rows), 1, core * (rows // 2))
    for n in range(1, blocks + 1):

        @pl.when(count == n)
        def _(n=n):
            near = (n - 1) * rows
            dqt = [jnp.zeros((HD, rows), F32) for _ in heads]
            for keys, masked in ((pl.ds(low, near), False), (pl.ds(low + near, rows), True)):
                if not masked and n == 1:
                    continue
                scores = [mm(k_ref[keys, :], q_ref[:, at], NT) for at in heads]
                backs = [mm(v_ref[keys, :], do_ref[:, at], NT) for at in heads]
                dv, dk = 0.0, 0.0
                for h, at in enumerate(heads):
                    p = jnp.exp2(scores[h] - lse_ref[h, :1])
                    if masked:
                        p = jnp.where(mask, p, 0.0)
                    ds = (p * (backs[h] - dots[h])).astype(BF16)
                    dv = dv + mm(p.astype(BF16), do_ref[:, at], NN)
                    dk = dk + mm(ds, q_ref[:, at], NN)
                    dqt[h] = dqt[h] + mm(kt_ref[:, keys], ds, NN)
                dv_ref[keys, :] += dv
                dk_ref[keys, :] += dk
            for h, at in enumerate(heads):
                g = dqt[h].T
                dq_ref[:, at] = (g * c_ref[...] - pltpu.roll(g, HD // 2, 1) * s_ref[...]).astype(BF16)


def whole(shape):
    return pl.BlockSpec(shape, lambda *_: (0,) * len(shape))


def second_half(seq):
    return pl.BlockSpec((seq, HD), lambda *_: (0, 1))


def attend(sp, q_lin, cosine, sine, kv_all, first, count, before=()):
    rows, width = q_lin.shape
    seq = kv_all.shape[0]
    heads = width // HD
    column = pl.BlockSpec((rows, HEADS * HD), lambda h, *_: (0, h + first // HEADS))
    return pl.pallas_call(
        functools.partial(fwd_kernel, seq // rows),
        grid_spec=pltpu.PrefetchScalarGridSpec(
            num_scalar_prefetch=1,
            grid=(count // HEADS,),
            in_specs=[column, whole((rows, HD)), whole((rows, HD)), whole((seq, HD)), second_half(seq)]
            + [pl.BlockSpec(memory_space=pl.ANY)] * len(before),
            out_specs=[column, column, pl.BlockSpec((HEADS, 8, rows), lambda h, *_: (h + first // HEADS, 0, 0))],
        ),
        out_shape=[
            jax.ShapeDtypeStruct((rows, width), BF16),
            jax.ShapeDtypeStruct((rows, width), BF16),
            jax.ShapeDtypeStruct((heads, 8, rows), F32),
        ],
        input_output_aliases={6 + i: i for i in range(len(before))},
        compiler_params=pltpu.CompilerParams(vmem_limit_bytes=VMEM_LIMIT),
        cost_estimate=pl.CostEstimate(
            flops=8 * count * rows * seq * HD, bytes_accessed=16 * rows * width, transcendentals=count * rows * seq
        ),
        name="attend",
    )(sp, q_lin, cosine, sine, kv_all, kv_all, *before)


def attend_back(sp, queries, grad_context, context, lse, cosine, sine, kv_all, key_rows_t, dk0, dv0):
    rows, width = queries.shape
    seq = kv_all.shape[0]
    heads = width // HD
    column = pl.BlockSpec((rows, HEADS * HD), lambda h, *_: (0, h))
    return pl.pallas_call(
        functools.partial(bwd_kernel, seq // rows),
        grid_spec=pltpu.PrefetchScalarGridSpec(
            num_scalar_prefetch=1,
            grid=(heads // HEADS,),
            in_specs=[
                column, column, column, pl.BlockSpec((HEADS, 8, rows), lambda h, *_: (h, 0, 0)),
                whole((rows, HD)), whole((rows, HD)), whole((seq, HD)), whole((HD, seq)), second_half(seq),
                whole((seq, HD)), whole((seq, HD)),
            ],
            out_specs=[column, whole((seq, HD)), whole((seq, HD))],
        ),
        out_shape=[
            jax.ShapeDtypeStruct((rows, width), BF16),
            jax.ShapeDtypeStruct((seq, HD), F32),
            jax.ShapeDtypeStruct((seq, HD), F32),
        ],
        compiler_params=pltpu.CompilerParams(vmem_limit_bytes=VMEM_LIMIT),
        cost_estimate=pl.CostEstimate(
            flops=20 * heads * rows * seq * HD, bytes_accessed=16 * rows * width, transcendentals=heads * rows * seq
        ),
        name="attend_back",
    )(sp, queries, grad_context, context, lse, cosine, sine, kv_all, key_rows_t, kv_all, dk0, dv0)


def second_unit(block, rows, q, do, kv, dk_ref, dv_ref, late):
    mask = diagonal((rows, rows), 1, 0)
    first = block * rows
    parts = [(pl.ds(first, rows), True, False)]
    middle = SEQ_SHORT * (first // SEQ_SHORT)
    if first > middle:
        parts.append((pl.ds(middle, first - middle), False, False))
    if middle:
        parts.append((pl.ds(0, middle), False, True))
    scores = []
    for keys, masked, far in parts:
        score = mm(kv[keys, :HD], q, NT) * SCALE2
        scores.append(jnp.where(mask, score, MASKED) if masked else score + late if far else score)
    top = functools.reduce(jnp.maximum, [jnp.max(score, axis=0, keepdims=True) for score in scores])
    lifted = [jnp.exp2(score - top) for score in scores]
    inverse = 1.0 / sum(jnp.sum(p, axis=0, keepdims=True) for p in lifted)
    back = [mm(kv[keys, HD:], do, NT) for keys, _, _ in parts]
    dot = sum(jnp.sum(p * b, axis=0, keepdims=True) for p, b in zip(lifted, back)) * inverse
    for (keys, _, _), p, b in zip(parts, lifted, back):
        p = p * inverse
        dv_ref[keys, :] += mm(p.astype(BF16), do, NN)
        dk_ref[keys, :] += mm((p * (b - dot)).astype(BF16), q, NN)


FRONT_HOPS = 1
FRONT_ORDER = (
    "kv q1 o1 kv", "q1 q2 o1 o2", "kv q1 q2 q3", "kv o1 o2 o3", "g kv* s q2", "q3 s o2 o3", "s g q2 q3",
    "s o2 o3 s", "q3 s g s", "o3 s q1* o1*", "q2* o2* q3* o3*", "s* g*",
)


def front_kernel(
    links, docs, tokens, gain, w_kv, cosine, sine, q_two, g_two, wq_hbm, wo_hbm, og_hbm,
    normed, wq_out, wo_out, kv_out, kt_ref, dk_ref, dv_ref, *refs,
):
    og_outs, (kv, ss, rs, ls) = refs[:-4], refs[-4:]
    chips, bits, n_dp = links.chips, links.bits, links.n_dp
    own, depth = tokens.shape
    seq = own * links.n_tensor
    width = wq_hbm.shape[1]
    me = lax.axis_index("tensor")
    me_dp = lax.axis_index("dp")
    chip, core = me // 2, lax.rem(me, 2)
    ahead, behind = links.neighbours(chip)
    right = {"tensor": ahead * 2 + core}
    left = {"tensor": behind * 2 + core}
    sibling = {"tensor": me ^ 1}
    barrier = pltpu.get_barrier_semaphore()
    peers = [right, left, sibling] + [{"dp": me_dp ^ bit} for bit in bits]
    for peer in peers:
        pl.semaphore_signal(barrier, inc=1, device_id=peer, device_id_type=pl.DeviceIdType.MESH)

    copies = []

    def send(src, dst, peer):
        number = len(copies)
        copy = mesh_copy(src, dst, ss.at[number], rs.at[number], peer)
        copy.start()
        copies.append(copy)
        return copy

    def q_piece(ref, k, j, way, size=1):
        rows = depth // n_dp // 2
        at = pl.ds(pl.multiple_of((2 * j + way) * rows, rows), size * rows)
        return ref.at[at, :] if k is None else ref.at[at, pl.ds(k * width, width)]

    def o_piece(ref, k, j, way, size=1):
        rows, half = width // n_dp, depth // 2
        at = pl.ds(pl.multiple_of((k or 0) * width + j * rows, rows), rows)
        return ref.at[at, pl.ds(way * half, size * half)]

    pl.semaphore_wait(barrier, len(peers))
    locals_ = [
        pltpu.make_async_copy(wq_hbm, wq_out.at[:, pl.ds(0, width)], ls.at[0]),
        pltpu.make_async_copy(wo_hbm, wo_out.at[pl.ds(0, width), :], ls.at[1]),
    ]
    for copy in locals_:
        copy.start()
    hops = {}
    for name, piece, src, dst in (("q", q_piece, wq_hbm, wq_out), ("o", o_piece, wo_hbm, wo_out)):
        hops[name, 1] = send(piece(src, None, me_dp, 0, 2), piece(dst, 1, me_dp, 0, 2), right)

    x = tokens[...].astype(F32)
    own_rows = pl.ds(0, own)
    normed[own_rows] = (x * lax.rsqrt(jnp.mean(x * x, axis=1, keepdims=True) + EPSILON) * gain[...]).astype(BF16)
    normed_swap = send(normed.at[own_rows], normed.at[pl.ds(own, own)], sibling)
    lin = mm(normed[own_rows], w_kv[...], NN)
    key = lin[:, :HD] * cosine[...] + pltpu.roll(lin[:, :HD], HD // 2, 1) * sine[...]

    def chip_up(k):
        found = chip * 0
        for i, c in enumerate(links.order):
            found = jnp.where(chip == c, links.order[(i - k) % chips], found)
        return found

    def kv_at(k):
        return kv.at[pl.ds(pl.multiple_of((chip_up(k) * 2 + core) * own, own), own)]

    kv_at(0)[...] = jnp.concatenate([key, lin[:, HD:]], axis=1).astype(BF16)
    late = jnp.where(docs[0] > 0, MASKED, 0.0)
    dk_ref[...] = jnp.zeros_like(dk_ref)
    dv_ref[...] = jnp.zeros_like(dv_ref)

    def kv_chain():
        swaps = []
        for k in range(chips):
            copy = send(kv_at(k), kv_at(k), right) if k + 1 < chips else None
            swaps.append(send(kv_at(k), kv_at(k), sibling))
            yield
            if copy is not None:
                copy.wait_recv()
        for copy in swaps:
            copy.wait_recv()
        store = pltpu.make_async_copy(kv, kv_out, ls.at[2])
        store.start()
        locals_.append(store)
        kt_ref[...] = kv[:, :HD].T

    def block_chain(name, piece, dst, k):
        hops[name, k].wait_recv()
        if k + 1 < chips:
            hops[name, k + 1] = send(piece(dst, k, me_dp, 0, 2), piece(dst, k + 1, me_dp, 0, 2), right)
        held = [[0], [0]]
        for step in range(len(bits)):
            sent = []
            for rank in range(len(held[0])):
                for way, order in enumerate((bits, bits[::-1])):
                    bit, rel = order[step], held[way][rank]
                    where = piece(dst, k, me_dp ^ rel, way)
                    sent.append((send(where, where, {"dp": me_dp ^ bit}), way, rel ^ bit))
            yield
            for copy, way, rel in sent:
                copy.wait_recv()
                held[way].append(rel)

    def grad_chain():
        source = og_hbm
        swaps = [send(og_hbm, og_outs[0], sibling)]
        for i in range(1, len(og_outs), 2):
            hop = send(source, og_outs[i], right)
            yield
            hop.wait_recv()
            source = og_outs[i]
            swaps.append(send(source, og_outs[i + 1], sibling))
        yield
        for copy in swaps:
            copy.wait_recv()

    rows = min(512, SEQ_SHORT)
    heads = q_two.shape[1] // HD

    def second_chain():
        for block in reversed(range(seq // rows)):
            for head in range(heads):
                at = (pl.ds(block * rows, rows), pl.ds(head * HD, HD))
                second_unit(block, rows, q_two[at], g_two[at], kv, dk_ref, dv_ref, late)
                yield
        dk_ref[...] *= SCALE2

    chains = {"kv": kv_chain(), "s": second_chain(), "g": grad_chain()}
    for k in range(1, chips):
        chains["q%d" % k] = block_chain("q", q_piece, wq_out, k)
        chains["o%d" % k] = block_chain("o", o_piece, wo_out, k)
    take_turns(chains, FRONT_ORDER)
    normed_swap.wait_recv()
    for copy in copies:
        copy.wait_send()
    for copy in locals_:
        copy.wait()


def take_turns(chains, order):
    def turn(name):
        if name in chains and next(chains[name], chains) is chains:
            del chains[name]

    for name in " ".join(order).split():
        turn(name.rstrip("*"))
        while name.endswith("*") and name.rstrip("*") in chains:
            turn(name.rstrip("*"))
    while chains:
        for name in list(chains):
            turn(name)


def front(links, docs, tokens, gain, w_kv, cosine, sine, q_two, g_two, w_query, w_out, out_grad):
    chips = links.chips
    own, depth = tokens.shape
    seq = own * links.n_tensor
    width = w_query.shape[1]
    anywhere = pl.BlockSpec(memory_space=pl.ANY)
    here = pl.BlockSpec(memory_space=pltpu.VMEM)
    dma = pltpu.SemaphoreType.DMA
    shape = jax.ShapeDtypeStruct
    count = 2 * chips * (2 * links.n_dp) + 4 * chips + 8
    hops = min(FRONT_HOPS, chips - 1)
    return pl.pallas_call(
        functools.partial(front_kernel, links),
        in_specs=[pl.BlockSpec(memory_space=pltpu.SMEM)] + [here] * 7 + [anywhere] * 3,
        out_specs=[here] + [anywhere] * 3 + [here] * 3 + [anywhere] * (1 + 2 * hops),
        out_shape=[
            shape((2 * own, depth), BF16), shape((depth, chips * width), BF16), shape((chips * width, depth), BF16),
            shape((seq, 2 * HD), BF16), shape((HD, seq), BF16), shape((seq, HD), F32), shape((seq, HD), F32),
        ]
        + [shape((own, depth), BF16)] * (1 + 2 * hops),
        scratch_shapes=[pltpu.VMEM((seq, 2 * HD), BF16), dma((count,)), dma((count,)), dma((3,))],
        compiler_params=pltpu.CompilerParams(
            collective_id=3, has_side_effects=True, vmem_limit_bytes=VMEM_LIMIT
        ),
        cost_estimate=pl.CostEstimate(flops=10**10, bytes_accessed=64 * 2**20, transcendentals=0),
        name="front",
    )(docs, tokens, gain, w_kv, cosine, sine, q_two, g_two, w_query, w_out, out_grad)


def mlp_kernel(
    links, h_hbm, wg_hbm, wu_hbm, wd_hbm, *refs,
):
    paired = 1 + min(FRONT_HOPS, links.chips - 1)
    given = [(k, half) for k in range(links.chips) for half in ((0, 1) if k < paired else (0,))]
    g_hbm, refs = refs[: len(given)], refs[len(given) :]
    (
    ghn_ref, mlp_hbm, grads_hbm, h_all, g_all, wg, wu, wd, act_t, gg_t, gu_t, mlp_in, stage, pair_out, pair_in, ring_out, ring_in,
    load_sem, ring_s, ring_r, swap_s, swap_r, pair_s, pair_r, rs_s, rs_r, mlp_s, mlp_r,
    stage_sem, store_sem, g_s, g_r,
    ) = refs
    chips = links.chips
    own, depth = h_hbm.shape
    seq = chips * 2 * own
    me = lax.axis_index("tensor")
    chip, core = me // 2, lax.rem(me, 2)
    ahead, behind = links.neighbours(chip)
    right = {"tensor": ahead * 2 + core}
    left = {"tensor": behind * 2 + core}
    sibling = {"tensor": chip * 2 + 1 - core}

    loads = [
        pltpu.make_async_copy(h_hbm, h_all.at[0, 0], load_sem.at[0]),
        pltpu.make_async_copy(wg_hbm, wg, load_sem.at[1]),
        pltpu.make_async_copy(wu_hbm, wu, load_sem.at[2]),
        pltpu.make_async_copy(wd_hbm, wd, load_sem.at[3]),
    ] + [
        pltpu.make_async_copy(ref, g_all.at[at], load_sem.at[4 + i]) for i, (ref, at) in enumerate(zip(g_hbm, given))
    ]
    for load in loads:
        load.start()
    barrier = pltpu.get_barrier_semaphore()
    for peer in (right, left, sibling):
        pl.semaphore_signal(barrier, inc=1, device_id=peer, device_id_type=pl.DeviceIdType.MESH)
    pl.semaphore_wait(barrier, 3)

    def remote(src, dst, send, recv, peer):
        return pltpu.make_async_remote_copy(
            src_ref=src, dst_ref=dst, send_sem=send, recv_sem=recv, device_id=peer,
            device_id_type=pl.DeviceIdType.MESH,
        )

    def ring(k):
        return remote(h_all.at[k, 0], h_all.at[k + 1, 0], ring_s.at[k], ring_r.at[k], right)

    def swap(k):
        return remote(h_all.at[k, 0], h_all.at[k, 1], swap_s.at[k], swap_r.at[k], sibling)

    def g_swap(k):
        return remote(g_all.at[k, 0], g_all.at[k, 1], g_s.at[k], g_r.at[k], sibling)

    def pair(k):
        slot = lax.rem(k, 2)
        return remote(pair_out.at[slot], pair_in.at[slot], pair_s.at[slot], pair_r.at[slot], sibling)

    def scatter(k):
        slot = lax.rem(k, 2)
        return remote(ring_out.at[slot], ring_in.at[k], rs_s.at[k], rs_r.at[k], right)

    def mlp_pair(k):
        slot = lax.rem(k, 2)
        return remote(stage.at[1], mlp_in.at[slot], mlp_s.at[slot], mlp_r.at[slot], sibling)

    def store(k):
        return pltpu.make_async_copy(stage.at[0], mlp_hbm.at[k], stage_sem.at[0])

    loads[0].wait()
    ring(0).start()
    swap(0).start()
    for load in loads[1:]:
        load.wait()
    for k in range(paired, chips):
        g_swap(k).start()

    def hidden_units(k, half):
        h, g = h_all[k, half], g_all[k, half]
        gate = mm(h, wg[...], NT)
        upward = mm(h, wu[...], NT)
        grad_act = mm(g, wd[...], NT)
        sigma = jax.nn.sigmoid(gate)
        swish = gate * sigma
        act = (swish * upward).astype(BF16)
        gg = (grad_act * upward * sigma * (1.0 + gate * (1.0 - sigma))).astype(BF16)
        gu = (grad_act * swish).astype(BF16)
        return act, gg, gu

    def keep_units(k, half, act, gg, gu):
        columns = pl.ds(pl.multiple_of((2 * k + half) * own, own), own)
        act_t[:, columns] = act.T
        gg_t[:, columns] = gg.T
        gu_t[:, columns] = gu.T

    def chunk(k, _):
        @pl.when(k >= 1)
        def _():
            ring(k - 1).wait_recv()

            @pl.when(k < chips - 1)
            def _():
                ring(k).start()

            swap(k).start()

        act0, gg0, gu0 = hidden_units(k, 0)
        swap(k).wait_recv()

        @pl.when(k >= paired)
        def _():
            g_swap(k).wait_recv()

        act1, gg1, gu1 = hidden_units(k, 1)

        @pl.when(k >= 2)
        def _():
            pair(k - 2).wait_send()

        pair_out[lax.rem(k, 2)] = (mm(gg1, wg[...], NN) + mm(gu1, wu[...], NN)).astype(BF16)
        pair(k).start()
        part = mm(gg0, wg[...], NN) + mm(gu0, wu[...], NN)
        pair(k).wait_recv()
        total = part + pair_in[lax.rem(k, 2)].astype(F32)

        @pl.when(k == 0)
        def _():
            ghn_ref[...] = total

        @pl.when(k == 1)
        def _():
            ring_out[1] = total.astype(BF16)
            scatter(k).start()

        @pl.when(k >= 2)
        def _():
            scatter(k - 1).wait_recv()

            @pl.when(k >= 3)
            def _():
                scatter(k - 2).wait_send()

            ring_out[lax.rem(k, 2)] = (total + ring_in[k - 1].astype(F32)).astype(BF16)
            scatter(k).start()

        @pl.when(k >= 1)
        def _():
            mlp_pair(k - 1).wait_send()

        stage[1] = mm(act1, wd[...], NN).astype(BF16)
        mlp_pair(k).start()
        keep_units(k, 0, act0, gg0, gu0)
        keep_units(k, 1, act1, gg1, gu1)
        mine = mm(act0, wd[...], NN)
        mlp_pair(k).wait_recv()

        @pl.when(k >= 1)
        def _():
            store(k - 1).wait()

        stage[0] = (mine + mlp_in[lax.rem(k, 2)].astype(F32)).astype(BF16)
        store(k).start()
        return 0

    lax.fori_loop(0, chips, chunk, 0)

    tile = 512

    def columns_of(j, _):
        at = pl.ds(pl.multiple_of(j * tile, tile), tile)
        h = h_all[:, :, :, at].reshape(seq, tile)
        g = g_all[:, :, :, at].reshape(seq, tile)
        wg[:, at] = mm(gg_t[...], h, NN).astype(BF16)
        wu[:, at] = mm(gu_t[...], h, NN).astype(BF16)
        wd[:, at] = mm(act_t[...], g, NN).astype(BF16)
        return 0

    lax.fori_loop(0, depth // tile, columns_of, 0)
    units, (pieces, _, piece) = wg.shape[0], grads_hbm.shape
    stores = [
        pltpu.make_async_copy(
            w.at[:, pl.ds(j * piece, piece)], grads_hbm.at[j, pl.ds(i * units, units)], store_sem.at[i, j]
        )
        for i, w in enumerate((wg, wu, wd))
        for j in range(pieces)
    ]
    for copy in stores:
        copy.start()
    scatter(chips - 1).wait_recv()
    ghn_ref[...] += ring_in[chips - 1].astype(F32)

    for copy in stores:
        copy.wait()
    store(chips - 1).wait()
    mlp_pair(chips - 1).wait_send()
    for k in (chips - 2, chips - 1):
        pair(k).wait_send()
        scatter(k).wait_send()
    for k in range(chips):
        swap(k).wait_send()
    for k in range(paired, chips):
        g_swap(k).wait_send()
    for k in range(chips - 1):
        ring(k).wait_send()


def feed_forward(links, hidden_own, grad_chunks, gate_t, up_t, down):
    own, depth = hidden_own.shape
    chips, units = links.chips, down.shape[0]
    seq = chips * 2 * own
    pieces = 2 * links.n_dp
    anywhere = pl.BlockSpec(memory_space=pl.ANY)
    dma = pltpu.SemaphoreType.DMA
    return pl.pallas_call(
        functools.partial(mlp_kernel, links),
        in_specs=[anywhere] * (4 + len(grad_chunks)),
        out_specs=[pl.BlockSpec(memory_space=pltpu.VMEM)] + [anywhere] * 2,
        out_shape=[
            jax.ShapeDtypeStruct((own, depth), F32),
            jax.ShapeDtypeStruct((chips, own, depth), BF16),
            jax.ShapeDtypeStruct((pieces, 3 * units, depth // pieces), BF16),
        ],
        scratch_shapes=[
            pltpu.VMEM((chips, 2, own, depth), BF16),
            pltpu.VMEM((chips, 2, own, depth), BF16),
            pltpu.VMEM((units, depth), BF16),
            pltpu.VMEM((units, depth), BF16),
            pltpu.VMEM((units, depth), BF16),
            pltpu.VMEM((units, seq), BF16),
            pltpu.VMEM((units, seq), BF16),
            pltpu.VMEM((units, seq), BF16),
            pltpu.VMEM((2, own, depth), BF16),
            pltpu.VMEM((2, own, depth), BF16),
            pltpu.VMEM((2, own, depth), BF16),
            pltpu.VMEM((2, own, depth), BF16),
            pltpu.VMEM((2, own, depth), BF16),
            pltpu.VMEM((chips, own, depth), BF16),
            dma((4 + len(grad_chunks),)),
            dma((chips,)), dma((chips,)), dma((chips,)), dma((chips,)), dma((2,)), dma((2,)),
            dma((chips,)), dma((chips,)), dma((2,)), dma((2,)), dma((1,)), dma((3, pieces)), dma((chips,)), dma((chips,)),
        ],
        compiler_params=pltpu.CompilerParams(
            collective_id=1, has_side_effects=True, vmem_limit_bytes=60 * 2**20
        ),
        cost_estimate=pl.CostEstimate(
            flops=18 * seq * depth * units, bytes_accessed=64 * 2**20, transcendentals=seq * units
        ),
        name="feed_forward",
    )(hidden_own, gate_t, up_t, down, *grad_chunks)


def mesh_copy(src, dst, send, recv, peer):
    return pltpu.make_async_remote_copy(
        src_ref=src, dst_ref=dst, send_sem=send, recv_sem=recv, device_id=peer,
        device_id_type=pl.DeviceIdType.MESH,
    )


def add_into(dst, src, rows):
    band = max(b for b in range(16, 353, 16) if rows % b == 0)

    def step(i, _):
        at = pl.ds(pl.multiple_of(i * band, band), band)
        dst[at, :] = (dst[at, :].astype(F32) + src[at, :].astype(F32)).astype(BF16)
        return 0

    lax.fori_loop(0, rows // band, step, 0)


class DpSum:
    def __init__(self, links, send, me, buf, got, free, first=0, rows=None):
        self.first, self.rows = first, rows or buf.shape[1]
        self.links, self.send, self.me, self.buf, self.got, self.free = links, send, me, buf, got, free
        self.n = links.n_dp
        self.ways = [links.bits, links.bits[::-1]]
        self.pending = []

    def at(self, way, rel):
        return way * self.n + (self.me ^ rel)

    def view(self, way, rel):
        return self.buf.at[self.at(way, rel), pl.ds(0, self.rows)]

    def kept(self, way, step):
        done = sum(self.ways[way][: step + 1])
        return [r for r in range(self.n) if r & done == 0]

    def first_slot(self, step):
        return sum(self.n >> (i + 1) for i in range(self.first, step))

    def peer(self, bit):
        return {"dp": self.me ^ bit}

    def start_halving(self, step):
        self.pending = []
        for rank in range(self.n >> (step + 1)):
            for way in (0, 1):
                bit = self.ways[way][step]
                rel = self.kept(way, step)[rank]
                slot = self.first_slot(step) + rank
                copy = self.send(self.buf.at[self.at(way, rel ^ bit)], self.got.at[way, slot], self.peer(bit), False)
                self.pending.append((copy, way, rel, slot))
        self.step = step

    def finish_halving(self):
        for copy, way, rel, slot in self.pending:
            copy.wait_recv()
            add_into(self.buf.at[self.at(way, rel)], self.got.at[way, slot], self.buf.shape[1])
        for copy, _, _, _ in self.pending:
            copy.wait_send()
        for way in (0, 1):
            pl.semaphore_signal(
                self.free.at[way, self.step], inc=1, device_id=self.peer(self.ways[way][self.step]),
                device_id_type=pl.DeviceIdType.MESH,
            )

    def start_doubling(self, step):
        self.pending = []
        if step >= self.first:
            for way in (0, 1):
                pl.semaphore_wait(self.free.at[way, step], 1)
        for rank in range(self.n >> (step + 1)):
            for way in (0, 1):
                bit = self.ways[way][step]
                rel = self.kept(way, step)[rank]
                where = self.view(way, rel)
                self.pending.append((self.send(where, where, self.peer(bit)), way, rel ^ bit))

    def finish_doubling(self):
        for copy, _, _ in self.pending:
            copy.wait_recv()
        return [(way, rel) for _, way, rel in self.pending]

    def chain(self, done, middle=()):
        rounds = len(self.links.bits)
        for step in range(self.first, rounds):
            self.start_halving(step)
            yield
            self.finish_halving()
        yield from middle
        for step in reversed(range(rounds)):
            self.start_doubling(step)
            if step == rounds - 1:
                done(0, 0)
                done(1, 0)
            yield
            for way, rel in self.finish_doubling():
                done(way, rel)


def first_halving(links, parts, me):
    n = links.n_dp
    stay, came, names = [], [], []
    for way, bits in enumerate((links.bits, links.bits[::-1])):
        for rel in range(n):
            if rel & bits[0] == 0:
                stay.append(lax.dynamic_index_in_dim(parts, way * n + (me ^ rel), 0, keepdims=False))
                other = lax.dynamic_index_in_dim(parts, way * n + (me ^ rel ^ bits[0]), 0, keepdims=False)
                came.append(links.across(other, bits[0]))
                names.append((way, rel))
    return stay, came, names


def tail_kernel(
    links, names, *refs,
):
    w_hbm, refs = refs[: len(names)], refs[len(names) :]
    (
        o_hbm, q_hbm, m_hbm, kv_keep, kv_send, gn_keep, gn_send, tokens, normed, w_kv, cosine, sine, gain_part,
        gain, grad_hidden, hidden, terms,
        ws_hbm, ow_hbm, qw_hbm, kvw_hbm, block_ref, grad_ref, gains_ref,
        o_buf, o_in, o_ring, q_buf, q_in, w_buf, w_in, c_buf, c_in, b_buf, b_in, b_turned, got, mine, m_sem,
        kv_got, kv_ring, kv_in, gn_got, kvw_half, kvw_got, kvw_in, kvw_all, gains_in,
        ss, rs, o_sem, q_sem, w_sem, out_sem, w_free, o_free, b_free,
    ) = refs
    chips, bits = links.chips, links.bits
    n_dp = links.n_dp
    width = q_buf.shape[1]
    piece = w_buf.shape[2]
    me = lax.axis_index("tensor")
    me_dp = lax.axis_index("dp")
    chip, core = me // 2, lax.rem(me, 2)
    ahead, behind = links.neighbours(chip)
    right = {"tensor": ahead * 2 + core}
    left = {"tensor": behind * 2 + core}
    sibling = {"tensor": me ^ 1}
    column = [None] + [{"tensor": me ^ (2 * k)} for k in range(1, chips)]
    group = [{"tensor": me ^ k} for k in range(1, links.n_tensor)]
    replicas = [{"dp": me_dp ^ k} for k in range(1, n_dp)]

    w_loads = [
        pltpu.make_async_copy(ref, w_buf.at[way * n_dp + (me_dp ^ rel)], w_sem.at[i])
        for i, (ref, (way, rel)) in enumerate(zip(w_hbm, names))
    ]
    loads = {}
    for k in list(range(1, chips)) + [0]:
        loads["q", k] = pltpu.make_async_copy(q_hbm.at[k], q_buf.at[k], q_sem.at[k])
    o_loads = [
        pltpu.make_async_copy(o_hbm.at[:, pl.ds(j * piece, piece)], o_buf.at[j], o_sem.at[j]) for j in range(2 * n_dp)
    ]
    for load in o_loads + list(loads.values()) + w_loads:
        load.start()
    barrier = pltpu.get_barrier_semaphore()
    peers = [right, left] + group + replicas
    for peer in peers:
        pl.semaphore_signal(barrier, inc=1, device_id=peer, device_id_type=pl.DeviceIdType.MESH)
    pl.semaphore_wait(barrier, len(peers))

    copies, opened, locals_ = [], [], []

    def send(src, dst, peer, later=True):
        number = len(copies)
        copy = mesh_copy(src, dst, ss.at[number], rs.at[number], peer)
        copy.start()
        copies.append(copy)
        if later:
            opened.append(copy)
        return copy

    def put(src, dst):
        copy = pltpu.make_async_copy(src, dst, out_sem.at[len(locals_)])
        copy.start()
        locals_.append(copy)

    def ring_chain(name, buf, got):
        copy = None
        for k in list(range(1, chips)) + [0]:
            loads[name, k].wait()
            if copy is not None:
                copy.wait_recv()
                add_into(buf.at[k], got.at[(k - 1) % chips - 1], buf.shape[1])
            if k:
                copy = send(buf.at[k], got.at[k - 1], right)
            yield

    kv_swap = send(kv_send, kv_got, sibling)
    gn_swap = send(gn_send, gn_got, sibling)
    held = {}

    def kv_chain():
        kv_swap.wait_recv()
        sent = []
        for k in range(1, chips):
            kv_ring[k - 1] = (kv_keep[k] + kv_got[k].astype(F32)).astype(BF16)
            sent.append(send(kv_ring.at[k - 1], kv_in.at[k - 1], column[k]))
        yield
        total = kv_keep[0] + kv_got[0].astype(F32)
        for k, copy in enumerate(sent):
            copy.wait_recv()
            total = total + kv_in[k].astype(F32)
        key_grad = total[:, :HD]
        key_grad = key_grad * cosine[...] - pltpu.roll(key_grad, HD // 2, 1) * sine[...]
        kv_lin = jnp.concatenate([key_grad, total[:, HD:]], axis=1).astype(BF16)
        kv_lin_t = kv_lin.T
        for half in (0, 1):
            kvw_half[half] = mm(kv_lin_t[half * HD : (half + 1) * HD], normed[...], NN).astype(BF16)
        held["swap"] = send(kvw_half.at[1 - core], kvw_got, sibling)
        yield
        gn_swap.wait_recv()
        grad = gn_keep[...] + gn_got[...].astype(F32) + mm(kv_lin, w_kv[...], NT)
        x = tokens[...].astype(F32)
        factor = lax.rsqrt(jnp.mean(x * x, axis=1, keepdims=True) + EPSILON)
        x = x * factor
        part = jnp.sum(grad * x, axis=0, keepdims=True)
        scaled = grad * gain[...]
        back = scaled - x * jnp.mean(scaled * x, axis=1, keepdims=True)
        grad_ref[...] = (grad_hidden[...] + factor * back).astype(BF16)
        lanes = gains_ref.shape[1]
        gains_ref[...] = jnp.concatenate(
            [v[:, i * lanes : (i + 1) * lanes] for v in (part, gain_part[...]) for i in range(4)], axis=0
        )

    def gains_chain():
        done = 0
        for stage in (group, replicas):
            sent = [send(gains_ref, gains_in.at[done + i], peer, False) for i, peer in enumerate(stage)]
            yield
            total = gains_ref[...]
            for i, copy in enumerate(sent):
                copy.wait_recv()
                copy.wait_send()
                total = total + gains_in[done + i]
            gains_ref[...] = total
            done += len(stage)

    band = HD // chips

    def rows_of(k):
        return pl.ds(pl.multiple_of((chip ^ k) * band, band), band)

    def kvw_chain():
        held["swap"].wait_recv()
        add_into(kvw_half.at[core], kvw_got, HD)
        sent = [send(kvw_half.at[core, rows_of(k)], kvw_in.at[k - 1], column[k]) for k in range(1, chips)]
        yield
        total = kvw_half[core, rows_of(0)].astype(F32)
        for k, copy in enumerate(sent):
            copy.wait_recv()
            total = total + kvw_in[k].astype(F32)
        c_buf[...] = total.astype(BF16)

    sum_w = DpSum(links, send, me_dp, w_buf, w_in, w_free, 1)
    sum_o = DpSum(links, send, me_dp, o_buf, o_in, o_free, 0, width)
    sum_b = DpSum(links, send, me_dp, b_buf, b_in, b_free)

    def columns(ref, number):
        return ref.at[:, pl.ds(pl.multiple_of(number * piece, piece), piece)]

    def w_chain():
        for load in w_loads:
            load.wait()
        yield from sum_w.chain(lambda way, rel: put(w_buf.at[sum_w.at(way, rel)], columns(ws_hbm, sum_w.at(way, rel))))

    def o_ring_chain():
        sent = []
        for k in list(range(1, chips)) + [0]:
            rows = pl.ds(k * width, width)
            for way, copy in enumerate(sent):
                copy.wait_recv()
                add_into(o_buf.at[sum_o.at(way, 0), rows], o_ring.at[(k - 1) % chips - 1, way], width)
            if k:
                sent = [
                    send(o_buf.at[sum_o.at(way, 0), rows], o_ring.at[k - 1, way], right) for way in (0, 1)
                ]
                yield

    def o_chain():
        for load in o_loads:
            load.wait()
        yield from sum_o.chain(
            lambda way, rel: put(sum_o.view(way, rel), columns(ow_hbm, sum_o.at(way, rel))), o_ring_chain()
        )

    def c_chain():
        sent = [send(c_buf, c_in.at[i], peer) for i, peer in enumerate(replicas)]
        yield
        total = c_buf[...].astype(F32)
        for i, copy in enumerate(sent):
            copy.wait_recv()
            total = total + c_in[i].astype(F32)
        kvw_all[0, core] = total.astype(BF16)
        sent = [send(kvw_all.at[0, core], kvw_all.at[k, core], column[k]) for k in range(1, chips)]
        yield
        for copy in sent:
            copy.wait_recv()
        copy = send(kvw_all.at[:, core], kvw_all.at[:, core], sibling)
        yield
        copy.wait_recv()
        for k in range(chips):
            for half in (0, 1):
                to = pl.ds(pl.multiple_of(half * HD + (chip ^ k) * band, band), band)
                put(kvw_all.at[k, half], kvw_hbm.at[to])

    def b_chain():
        for j in range(2 * n_dp):
            b_buf[j] = q_buf[0, :, pl.ds(j * piece, piece)]

        def turn_over(way, rel):
            at = sum_b.at(way, rel)
            b_turned[at] = b_buf[at].T
            put(b_turned.at[at], qw_hbm.at[pl.ds(pl.multiple_of(at * piece, piece), piece)])

        yield from sum_b.chain(turn_over)

    def m_chain():
        copy = send(m_hbm, got, right)
        load = pltpu.make_async_copy(terms.at[0], mine, m_sem.at[0])
        load.start()
        yield
        load.wait()
        copy.wait_recv()
        block_ref[...] = (hidden[...] + mine[...].astype(F32) + got[...].astype(F32)).astype(BF16)

    chains = {
        "w": w_chain(), "o": o_chain(), "q": ring_chain("q", q_buf, q_in), "kv": kv_chain(),
        "g": gains_chain(), "kvw": kvw_chain(), "m": m_chain(), "c": c_chain(), "b": b_chain(),
    }

    take_turns(chains, TAIL_ORDER)
    for copy in opened:
        copy.wait_send()
    for copy in locals_:
        copy.wait()


TAIL_ORDER = (
    "o kv w kv", "kvw kvw q c", "o c w o", "c o q kv", "g o w q", "g q m g", "b o b c", "o b o b", "b w m",
)


def tail(
    links, o_parts, q_parts, m_part, w_pieces, names, kv_keep, kv_send, gn_keep, gn_send, tokens, normed, w_kv, cosine,
    sine, gain_part, gain, grad_hidden, hidden, terms,
):
    chips, width, depth = q_parts.shape
    own = tokens.shape[0]
    rows, piece = w_pieces[0].shape
    band = HD // chips
    n = links.n_dp
    pieces = 2 * n
    anywhere = pl.BlockSpec(memory_space=pl.ANY)
    here = pl.BlockSpec(memory_space=pltpu.VMEM)
    dma = pltpu.SemaphoreType.DMA
    shape = jax.ShapeDtypeStruct
    count = 20 * chips + 20 * n + 16
    return pl.pallas_call(
        functools.partial(tail_kernel, links, names),
        in_specs=[anywhere] * (3 + len(names)) + [here] * 13 + [anywhere],
        out_specs=[anywhere] * 4 + [here] * 3,
        out_shape=[
            shape((rows, depth), BF16), shape((width, depth), BF16),
            shape((depth, width), BF16), shape((2 * HD, depth), BF16), shape((own, depth), BF16),
            shape((own, depth), BF16), shape((8, depth // 4), F32),
        ],
        scratch_shapes=[
            pltpu.VMEM((pieces, chips * width, piece), BF16), pltpu.VMEM((2, n - 1, chips * width, piece), BF16),
            pltpu.VMEM((chips - 1, 2, width, piece), BF16),
            pltpu.VMEM((chips, width, depth), BF16), pltpu.VMEM((chips - 1, width, depth), BF16),
            pltpu.VMEM((pieces, rows, piece), BF16), pltpu.VMEM((2, max(1, n // 2 - 1), rows, piece), BF16),
            pltpu.VMEM((band, depth), BF16), pltpu.VMEM((n - 1, band, depth), BF16),
            pltpu.VMEM((pieces, width, piece), BF16), pltpu.VMEM((2, n - 1, width, piece), BF16),
            pltpu.VMEM((pieces, piece, width), BF16), pltpu.VMEM((own, depth), BF16),
            pltpu.VMEM((own, depth), BF16), dma((1,)),
            pltpu.VMEM((chips, own, 2 * HD), BF16),
            pltpu.VMEM((chips - 1, own, 2 * HD), BF16), pltpu.VMEM((chips - 1, own, 2 * HD), BF16),
            pltpu.VMEM((own, depth), BF16),
            pltpu.VMEM((2, HD, depth), BF16), pltpu.VMEM((HD, depth), BF16),
            pltpu.VMEM((chips - 1, band, depth), BF16),
            pltpu.VMEM((chips, 2, band, depth), BF16),
            pltpu.VMEM((links.n_tensor + n, 8, depth // 4), F32),
            dma((count,)), dma((count,)), dma((pieces,)), dma((chips,)), dma((len(names),)),
            dma((3 * pieces + 2 * chips,)),
        ]
        + [pltpu.SemaphoreType.REGULAR((2, len(links.bits)))] * 3,
        compiler_params=pltpu.CompilerParams(
            collective_id=2, has_side_effects=True, vmem_limit_bytes=60 * 2**20
        ),
        cost_estimate=pl.CostEstimate(flops=10**9, bytes_accessed=64 * 2**20, transcendentals=0),
        name="tail",
    )(
        *w_pieces, o_parts, q_parts, m_part, kv_keep, kv_send, gn_keep, gn_send, tokens, normed, w_kv, cosine, sine,
        gain_part, gain, grad_hidden, hidden, terms,
    )


def rms_factor(values):
    return lax.rsqrt(jnp.mean(values * values, axis=-1, keepdims=True) + EPSILON)


def local(
    n_tensor, n_dp,
    tokens, out_grad, query_two, grad_two, doc_split, attn_gain, mlp_gain, w_query, w_kv, w_out, w_gate, w_up, w_down,
):
    links = Links(n_tensor, n_dp)
    chips = links.chips
    own = tokens.shape[0]
    rows = 2 * own
    seq = own * n_tensor
    width = w_query.shape[1]
    me_dp = lax.axis_index("dp")
    me_t = lax.axis_index("tensor")
    chip, core = me_t // 2, me_t % 2
    two_docs = doc_split[0]
    sp = jnp.stack([chip, two_docs, core]).astype(jnp.int32)
    place = jnp.array(links.place, jnp.int32)
    order = jnp.array(links.order, jnp.int32)

    spot = jnp.arange(rows, dtype=jnp.int32) + core * own
    spot = chip * rows + jnp.where(spot >= rows, spot - rows, spot)
    position = jnp.where(two_docs > 0, spot % SEQ_SHORT, spot)
    frequency = 10000.0 ** (-jnp.arange(HD // 2, dtype=F32) * 2.0 / HD)
    phases = position.astype(F32)[:, None] * frequency[None, :]
    cos, sin = jnp.cos(phases), jnp.sin(phases)
    cosine = jnp.concatenate([cos, cos], axis=1)
    sine = jnp.concatenate([-sin, sin], axis=1)

    residual = tokens.astype(F32)

    normed, wq, wo, kv_all, key_rows_t, dk2, dv2, *grad_chunks = front(
        links, doc_split, tokens, attn_gain[None], w_kv, cosine[:own], sine[:own], query_two, grad_two, w_query, w_out,
        out_grad,
    )
    normed_own = normed[:own]
    grad_chunks = [out_grad] + grad_chunks

    q_lin = mm(normed, wq, NN)
    some = q_lin.shape[1] // HD // 2
    tables = (cosine * SCALE2, sine * SCALE2)
    results = attend(sp, q_lin, *tables, kv_all, 0, some)
    results, further = lax.optimization_barrier((results, links.ring(grad_chunks[-2])))
    later_chunks = [further]
    for _ in range(3 + FRONT_HOPS, chips + 1):
        later_chunks.append(links.ring(later_chunks[-1]))
    queries, context, lse = attend(sp, q_lin, *tables, kv_all, some, q_lin.shape[1] // HD - some, results)
    branch, later_chunks = lax.optimization_barrier((mm(context, wo, NN), later_chunks))
    branch = pair_sum(links, branch)
    hidden = residual + branch
    mlp_scale = rms_factor(hidden)
    mlp_pre = hidden * mlp_scale
    hidden_own = (mlp_pre * mlp_gain).astype(BF16)

    grad_hn, mlp_terms, ffn_parts = feed_forward(links, hidden_own, grad_chunks + later_chunks, w_gate.T, w_up.T, w_down)
    mlp_came = links.ring(mlp_terms[1])
    ffn_stay, ffn_came, ffn_names = first_halving(links, ffn_parts, me_dp)

    mlp_gain_part = jnp.sum(grad_hn * mlp_pre, axis=0)
    scaled_mlp = grad_hn * mlp_gain
    grad_hidden = out_grad.astype(F32) + mlp_scale * (
        scaled_mlp - mlp_pre * jnp.mean(scaled_mlp * mlp_pre, axis=-1, keepdims=True)
    )

    grad_branch = both(links, grad_hidden.astype(BF16))
    grad_context = mm(grad_branch, wo, NT).astype(BF16)
    query_grad, dk, dv = attend_back(
        sp, queries, grad_context, context, lse, cosine * SCALE, sine * SCALE, kv_all, key_rows_t, dk2, dv2
    )
    for k in range(2, chips - 1):
        query_grad, mlp_came = lax.optimization_barrier((query_grad, mlp_came))
        mlp_sent = (mlp_terms[k].astype(F32) + mlp_came.astype(F32)).astype(BF16)
        mlp_came = links.ring(mlp_sent)
    out_parts = mm(context, grad_branch, TN).astype(BF16)
    query_parts = mm(query_grad, normed, TN).astype(BF16).reshape(chips, width, -1)

    kv_part = jnp.concatenate([dk * (SCALE / SCALE2), dv], axis=1).reshape(chips, 2, own, 2 * HD)
    kv_part = jnp.stack(
        [
            lax.dynamic_index_in_dim(kv_part, chip ^ k, 0, keepdims=False)
            for k in range(chips)
        ]
    )
    kv_keep = lax.dynamic_index_in_dim(kv_part, core, 1, keepdims=False)
    kv_send = lax.dynamic_index_in_dim(kv_part, 1 - core, 1, keepdims=False).astype(BF16)
    gn_part = mm(query_grad, wq, NT)
    mlp_sent = (mlp_terms[chips - 1].astype(F32) + mlp_came.astype(F32)).astype(BF16)
    ffn_pieces = [(a.astype(F32) + b.astype(F32)).astype(BF16) for a, b in zip(ffn_stay, ffn_came)]
    gain_part = mlp_gain_part[None]
    ffn_w, out_w, query_w, kv_w, block_output, tokens_grad, gains = tail(
        links, out_parts, query_parts, mlp_sent, ffn_pieces, ffn_names, kv_keep, kv_send, gn_part[:own],
        gn_part[own:].astype(BF16), tokens, normed_own, w_kv, cosine[:own], sine[:own], gain_part,
        attn_gain[None], grad_hidden, hidden, mlp_terms,
    )
    units = w_down.shape[0]

    gate_w_grad = ffn_w[:units].astype(F32).T
    up_w_grad = ffn_w[units : 2 * units].astype(F32).T
    down_w_grad = ffn_w[2 * units :].astype(F32)
    out_w_grad = out_w.astype(F32)
    query_w_grad = query_w.astype(F32)
    kv_w_grad = kv_w.astype(F32).T
    attn_gain_grad, mlp_gain_grad = gains[:4].reshape(-1), gains[4:].reshape(-1)

    return (
        block_output,
        tokens_grad,
        attn_gain_grad,
        mlp_gain_grad,
        query_w_grad,
        kv_w_grad,
        out_w_grad,
        gate_w_grad,
        up_w_grad,
        down_w_grad,
    )


def solution(mesh):
    both_axes = P(("dp", "tensor"), None)
    return jax.shard_map(
        functools.partial(local, mesh.shape["tensor"], mesh.shape["dp"]),
        mesh=mesh,
        in_specs=(
            both_axes,
            both_axes,
            P("dp", "tensor"),
            P("dp", "tensor"),
            P("dp"),
            P(),
            P(),
            P(None, "tensor"),
            P(),
            P("tensor", None),
            P(None, "tensor"),
            P(None, "tensor"),
            P("tensor", None),
        ),
        out_specs=(
            both_axes,
            both_axes,
            P(),
            P(),
            P(None, "tensor"),
            P(),
            P("tensor", None),
            P(None, "tensor"),
            P(None, "tensor"),
            P("tensor", None),
        ),
        check_vma=False,
    )
```

```python
import functools

import jax
import jax.numpy as jnp
from jax import lax
from jax.experimental import pallas as pl
from jax.experimental.pallas import tpu as pltpu
from jax.sharding import PartitionSpec as P

HD = 128
SEQ_SHORT = 1024
EPSILON = 1e-05
MASKED = -1e30
SCALE = HD ** (-0.5)
SCALE2 = SCALE * 1.4426950408889634
F32 = jnp.float32
BF16 = jnp.bfloat16
VMEM_LIMIT = 56 * 2**20


def mm(left, right, dims):
    return lax.dot_general(left, right, (dims, ((), ())), preferred_element_type=F32)


NN = ((1,), (0,))
NT = ((1,), (1,))
TN = ((0,), (0,))


class Links:
    def __init__(self, n_tensor, n_dp):
        self.n_tensor, self.n_dp = n_tensor, n_dp
        self.chips = n_tensor // 2
        odd = list(range(1, self.chips, 2))
        even = list(range(2, self.chips, 2))
        self.order = [0] + odd + even[::-1]
        nxt = {c: self.order[(i + 1) % self.chips] for i, c in enumerate(self.order)}
        self.place = [self.order.index(c) for c in range(self.chips)]
        self.ring_pairs = [(2 * c + k, 2 * nxt[c] + k) for c in range(self.chips) for k in (0, 1)]
        self.swap_pairs = [(i, i ^ 1) for i in range(n_tensor)]
        self.bits = [1 << b for b in range(n_dp.bit_length() - 1)]

    def ring(self, x):
        return lax.ppermute(x, "tensor", self.ring_pairs)

    def swap(self, x):
        return lax.ppermute(x, "tensor", self.swap_pairs)

    def across(self, x, bit):
        return lax.ppermute(x, "dp", [(i, i ^ bit) for i in range(self.n_dp)])

    def neighbours(self, chip):
        ahead, behind = chip * 0, chip * 0
        for i, c in enumerate(self.order):
            ahead = jnp.where(chip == c, self.order[(i + 1) % self.chips], ahead)
            behind = jnp.where(chip == c, self.order[i - 1], behind)
        return ahead, behind


def both(links, own):
    return jnp.concatenate([own, links.swap(own)], axis=0)


def pair_sum(links, part):
    rows = part.shape[0] // 2
    return part[:rows].astype(F32) + links.swap(part[rows:].astype(BF16)).astype(F32)


def diagonal(shape, row_axis, shift):
    size = shape[row_axis]
    row = lax.broadcasted_iota(jnp.int32, shape, row_axis) + shift
    row = jnp.where(row >= size, row - size, row)
    return lax.broadcasted_iota(jnp.int32, shape, 1 - row_axis) <= row


def span(block, two_docs, rows):
    per_doc = SEQ_SHORT // rows
    inner = jnp.where(two_docs > 0, lax.rem(block, per_doc), block)
    return inner + 1, pl.multiple_of((block - inner) * rows, rows)


HEADS = 2


def fwd_kernel(blocks, sp_ref, q_ref, c_ref, s_ref, k_ref, v_ref, *refs):
    qo_ref, ctx_ref, lse_ref = refs[-3:]
    rows = q_ref.shape[0]
    chip, two_docs, core = sp_ref[0], sp_ref[1], sp_ref[2]
    heads = [slice(h * HD, (h + 1) * HD) for h in range(HEADS)]
    for at in heads:
        x = q_ref[:, at]
        qo_ref[:, at] = (x * c_ref[...] + pltpu.roll(x, HD // 2, 1) * s_ref[...]).astype(BF16)
    count, low = span(chip, two_docs, rows)
    mask = diagonal((rows, rows), 0, core * (rows // 2))
    for n in range(1, blocks + 1):

        @pl.when(count == n)
        def _(n=n):
            near = (n - 1) * rows
            keys = [pl.ds(low + near, rows)] + ([pl.ds(low, near)] if n > 1 else [])
            scores = [[mm(qo_ref[:, at], k_ref[at_keys, :], NT) for at_keys in keys] for at in heads]
            for h, at in enumerate(heads):
                score = scores[h]
                score[0] = jnp.where(mask, score[0], MASKED)
                top = functools.reduce(jnp.maximum, [jnp.max(v, axis=1, keepdims=True) for v in score])
                lifted = [jnp.exp2(v - top) for v in score]
                total = sum(jnp.sum(p, axis=1, keepdims=True) for p in lifted)
                out = sum(mm(p.astype(BF16), v_ref[at_keys, :], NN) for p, at_keys in zip(lifted, keys))
                ctx_ref[:, at] = (out / total).astype(BF16)
                lse = jnp.broadcast_to(top + jnp.log2(total), (rows, HD))
                lse_ref[h] = lse.T[:8]


def bwd_kernel(
    blocks, sp_ref, q_ref, do_ref, ctx_ref, lse_ref, c_ref, s_ref, k_ref, kt_ref, v_ref, dk0_ref, dv0_ref,
    dq_ref, dk_ref, dv_ref,
):
    rows = q_ref.shape[0]
    chip, two_docs, core = sp_ref[0], sp_ref[1], sp_ref[2]

    @pl.when(pl.program_id(0) == 0)
    def _():
        dk_ref[...] = dk0_ref[...]
        dv_ref[...] = dv0_ref[...]

    heads = [slice(h * HD, (h + 1) * HD) for h in range(HEADS)]
    dots = []
    for at in heads:
        dot = jnp.sum(do_ref[:, at].astype(F32) * ctx_ref[:, at].astype(F32), axis=1, keepdims=True)
        dots.append(jnp.broadcast_to(dot, (rows, HD)).T[:1])
    count, low = span(chip, two_docs, rows)
    mask = diagonal((rows, rows), 1, core * (rows // 2))
    for n in range(1, blocks + 1):

        @pl.when(count == n)
        def _(n=n):
            near = (n - 1) * rows
            dqt = [jnp.zeros((HD, rows), F32) for _ in heads]
            for keys, masked in ((pl.ds(low, near), False), (pl.ds(low + near, rows), True)):
                if not masked and n == 1:
                    continue
                scores = [mm(k_ref[keys, :], q_ref[:, at], NT) for at in heads]
                backs = [mm(v_ref[keys, :], do_ref[:, at], NT) for at in heads]
                dv, dk = 0.0, 0.0
                for h, at in enumerate(heads):
                    p = jnp.exp2(scores[h] - lse_ref[h, :1])
                    if masked:
                        p = jnp.where(mask, p, 0.0)
                    ds = (p * (backs[h] - dots[h])).astype(BF16)
                    dv = dv + mm(p.astype(BF16), do_ref[:, at], NN)
                    dk = dk + mm(ds, q_ref[:, at], NN)
                    dqt[h] = dqt[h] + mm(kt_ref[:, keys], ds, NN)
                dv_ref[keys, :] += dv
                dk_ref[keys, :] += dk
            for h, at in enumerate(heads):
                g = dqt[h].T
                dq_ref[:, at] = (g * c_ref[...] - pltpu.roll(g, HD // 2, 1) * s_ref[...]).astype(BF16)


def whole(shape):
    return pl.BlockSpec(shape, lambda *_: (0,) * len(shape))


def second_half(seq):
    return pl.BlockSpec((seq, HD), lambda *_: (0, 1))


def attend(sp, q_lin, cosine, sine, kv_all, first, count, before=()):
    rows, width = q_lin.shape
    seq = kv_all.shape[0]
    heads = width // HD
    column = pl.BlockSpec((rows, HEADS * HD), lambda h, *_: (0, h + first // HEADS))
    return pl.pallas_call(
        functools.partial(fwd_kernel, seq // rows),
        grid_spec=pltpu.PrefetchScalarGridSpec(
            num_scalar_prefetch=1,
            grid=(count // HEADS,),
            in_specs=[column, whole((rows, HD)), whole((rows, HD)), whole((seq, HD)), second_half(seq)]
            + [pl.BlockSpec(memory_space=pl.ANY)] * len(before),
            out_specs=[column, column, pl.BlockSpec((HEADS, 8, rows), lambda h, *_: (h + first // HEADS, 0, 0))],
        ),
        out_shape=[
            jax.ShapeDtypeStruct((rows, width), BF16),
            jax.ShapeDtypeStruct((rows, width), BF16),
            jax.ShapeDtypeStruct((heads, 8, rows), F32),
        ],
        input_output_aliases={6 + i: i for i in range(len(before))},
        compiler_params=pltpu.CompilerParams(vmem_limit_bytes=VMEM_LIMIT),
        cost_estimate=pl.CostEstimate(
            flops=8 * count * rows * seq * HD, bytes_accessed=16 * rows * width, transcendentals=count * rows * seq
        ),
        name="attend",
    )(sp, q_lin, cosine, sine, kv_all, kv_all, *before)


def attend_back(sp, queries, grad_context, context, lse, cosine, sine, kv_all, key_rows_t, dk0, dv0):
    rows, width = queries.shape
    seq = kv_all.shape[0]
    heads = width // HD
    column = pl.BlockSpec((rows, HEADS * HD), lambda h, *_: (0, h))
    return pl.pallas_call(
        functools.partial(bwd_kernel, seq // rows),
        grid_spec=pltpu.PrefetchScalarGridSpec(
            num_scalar_prefetch=1,
            grid=(heads // HEADS,),
            in_specs=[
                column, column, column, pl.BlockSpec((HEADS, 8, rows), lambda h, *_: (h, 0, 0)),
                whole((rows, HD)), whole((rows, HD)), whole((seq, HD)), whole((HD, seq)), second_half(seq),
                whole((seq, HD)), whole((seq, HD)),
            ],
            out_specs=[column, whole((seq, HD)), whole((seq, HD))],
        ),
        out_shape=[
            jax.ShapeDtypeStruct((rows, width), BF16),
            jax.ShapeDtypeStruct((seq, HD), F32),
            jax.ShapeDtypeStruct((seq, HD), F32),
        ],
        compiler_params=pltpu.CompilerParams(vmem_limit_bytes=VMEM_LIMIT),
        cost_estimate=pl.CostEstimate(
            flops=20 * heads * rows * seq * HD, bytes_accessed=16 * rows * width, transcendentals=heads * rows * seq
        ),
        name="attend_back",
    )(sp, queries, grad_context, context, lse, cosine, sine, kv_all, key_rows_t, kv_all, dk0, dv0)


def second_unit(block, rows, q, do, kv, dk_ref, dv_ref, late):
    mask = diagonal((rows, rows), 1, 0)
    first = block * rows
    parts = [(pl.ds(first, rows), True, False)]
    middle = SEQ_SHORT * (first // SEQ_SHORT)
    if first > middle:
        parts.append((pl.ds(middle, first - middle), False, False))
    if middle:
        parts.append((pl.ds(0, middle), False, True))
    scores = []
    for keys, masked, far in parts:
        score = mm(kv[keys, :HD], q, NT) * SCALE2
        scores.append(jnp.where(mask, score, MASKED) if masked else score + late if far else score)
    top = functools.reduce(jnp.maximum, [jnp.max(score, axis=0, keepdims=True) for score in scores])
    lifted = [jnp.exp2(score - top) for score in scores]
    inverse = 1.0 / sum(jnp.sum(p, axis=0, keepdims=True) for p in lifted)
    back = [mm(kv[keys, HD:], do, NT) for keys, _, _ in parts]
    dot = sum(jnp.sum(p * b, axis=0, keepdims=True) for p, b in zip(lifted, back)) * inverse
    for (keys, _, _), p, b in zip(parts, lifted, back):
        p = p * inverse
        dv_ref[keys, :] += mm(p.astype(BF16), do, NN)
        dk_ref[keys, :] += mm((p * (b - dot)).astype(BF16), q, NN)


FRONT_HOPS = 1
FRONT_ORDER = (
    "kv q1 o1 kv", "q1 q2 o1 o2", "kv q1 q2 q3", "kv o1 o2 o3", "g kv* s q2", "q3 s o2 o3", "s g q2 q3",
    "s o2 o3 s", "q3 s g s", "o3 s q1* o1*", "q2* o2* q3* o3*", "s* g*",
)


def front_kernel(
    links, docs, tokens, gain, w_kv, cosine, sine, q_two, g_two, wq_hbm, wo_hbm, og_hbm,
    normed, wq_out, wo_out, kv_out, kt_ref, dk_ref, dv_ref, *refs,
):
    og_outs, (kv, ss, rs, ls) = refs[:-4], refs[-4:]
    chips, bits, n_dp = links.chips, links.bits, links.n_dp
    own, depth = tokens.shape
    seq = own * links.n_tensor
    width = wq_hbm.shape[1]
    me = lax.axis_index("tensor")
    me_dp = lax.axis_index("dp")
    chip, core = me // 2, lax.rem(me, 2)
    ahead, behind = links.neighbours(chip)
    right = {"tensor": ahead * 2 + core}
    left = {"tensor": behind * 2 + core}
    sibling = {"tensor": me ^ 1}
    barrier = pltpu.get_barrier_semaphore()
    peers = [right, left, sibling] + [{"dp": me_dp ^ bit} for bit in bits]
    for peer in peers:
        pl.semaphore_signal(barrier, inc=1, device_id=peer, device_id_type=pl.DeviceIdType.MESH)

    copies = []

    def send(src, dst, peer):
        number = len(copies)
        copy = mesh_copy(src, dst, ss.at[number], rs.at[number], peer)
        copy.start()
        copies.append(copy)
        return copy

    def q_piece(ref, k, j, way, size=1):
        rows = depth // n_dp // 2
        at = pl.ds(pl.multiple_of((2 * j + way) * rows, rows), size * rows)
        return ref.at[at, :] if k is None else ref.at[at, pl.ds(k * width, width)]

    def o_piece(ref, k, j, way, size=1):
        rows, half = width // n_dp, depth // 2
        at = pl.ds(pl.multiple_of((k or 0) * width + j * rows, rows), rows)
        return ref.at[at, pl.ds(way * half, size * half)]

    pl.semaphore_wait(barrier, len(peers))
    locals_ = [
        pltpu.make_async_copy(wq_hbm, wq_out.at[:, pl.ds(0, width)], ls.at[0]),
        pltpu.make_async_copy(wo_hbm, wo_out.at[pl.ds(0, width), :], ls.at[1]),
    ]
    for copy in locals_:
        copy.start()
    hops = {}
    for name, piece, src, dst in (("q", q_piece, wq_hbm, wq_out), ("o", o_piece, wo_hbm, wo_out)):
        hops[name, 1] = send(piece(src, None, me_dp, 0, 2), piece(dst, 1, me_dp, 0, 2), right)

    x = tokens[...].astype(F32)
    own_rows = pl.ds(0, own)
    normed[own_rows] = (x * lax.rsqrt(jnp.mean(x * x, axis=1, keepdims=True) + EPSILON) * gain[...]).astype(BF16)
    normed_swap = send(normed.at[own_rows], normed.at[pl.ds(own, own)], sibling)
    lin = mm(normed[own_rows], w_kv[...], NN)
    key = lin[:, :HD] * cosine[...] + pltpu.roll(lin[:, :HD], HD // 2, 1) * sine[...]

    def chip_up(k):
        found = chip * 0
        for i, c in enumerate(links.order):
            found = jnp.where(chip == c, links.order[(i - k) % chips], found)
        return found

    def kv_at(k):
        return kv.at[pl.ds(pl.multiple_of((chip_up(k) * 2 + core) * own, own), own)]

    kv_at(0)[...] = jnp.concatenate([key, lin[:, HD:]], axis=1).astype(BF16)
    late = jnp.where(docs[0] > 0, MASKED, 0.0)
    dk_ref[...] = jnp.zeros_like(dk_ref)
    dv_ref[...] = jnp.zeros_like(dv_ref)

    def kv_chain():
        swaps = []
        for k in range(chips):
            copy = send(kv_at(k), kv_at(k), right) if k + 1 < chips else None
            swaps.append(send(kv_at(k), kv_at(k), sibling))
            yield
            if copy is not None:
                copy.wait_recv()
        for copy in swaps:
            copy.wait_recv()
        store = pltpu.make_async_copy(kv, kv_out, ls.at[2])
        store.start()
        locals_.append(store)
        kt_ref[...] = kv[:, :HD].T

    def block_chain(name, piece, dst, k):
        hops[name, k].wait_recv()
        if k + 1 < chips:
            hops[name, k + 1] = send(piece(dst, k, me_dp, 0, 2), piece(dst, k + 1, me_dp, 0, 2), right)
        held = [[0], [0]]
        for step in range(len(bits)):
            sent = []
            for rank in range(len(held[0])):
                for way, order in enumerate((bits, bits[::-1])):
                    bit, rel = order[step], held[way][rank]
                    where = piece(dst, k, me_dp ^ rel, way)
                    sent.append((send(where, where, {"dp": me_dp ^ bit}), way, rel ^ bit))
            yield
            for copy, way, rel in sent:
                copy.wait_recv()
                held[way].append(rel)

    def grad_chain():
        source = og_hbm
        swaps = [send(og_hbm, og_outs[0], sibling)]
        for i in range(1, len(og_outs), 2):
            hop = send(source, og_outs[i], right)
            yield
            hop.wait_recv()
            source = og_outs[i]
            swaps.append(send(source, og_outs[i + 1], sibling))
        yield
        for copy in swaps:
            copy.wait_recv()

    rows = min(512, SEQ_SHORT)
    heads = q_two.shape[1] // HD

    def second_chain():
        for block in reversed(range(seq // rows)):
            for head in range(heads):
                at = (pl.ds(block * rows, rows), pl.ds(head * HD, HD))
                second_unit(block, rows, q_two[at], g_two[at], kv, dk_ref, dv_ref, late)
                yield
        dk_ref[...] *= SCALE2

    chains = {"kv": kv_chain(), "s": second_chain(), "g": grad_chain()}
    for k in range(1, chips):
        chains["q%d" % k] = block_chain("q", q_piece, wq_out, k)
        chains["o%d" % k] = block_chain("o", o_piece, wo_out, k)
    take_turns(chains, FRONT_ORDER)
    normed_swap.wait_recv()
    for copy in copies:
        copy.wait_send()
    for copy in locals_:
        copy.wait()


def take_turns(chains, order):
    def turn(name):
        if name in chains and next(chains[name], chains) is chains:
            del chains[name]

    for name in " ".join(order).split():
        turn(name.rstrip("*"))
        while name.endswith("*") and name.rstrip("*") in chains:
            turn(name.rstrip("*"))
    while chains:
        for name in list(chains):
            turn(name)


def front(links, docs, tokens, gain, w_kv, cosine, sine, q_two, g_two, w_query, w_out, out_grad):
    chips = links.chips
    own, depth = tokens.shape
    seq = own * links.n_tensor
    width = w_query.shape[1]
    anywhere = pl.BlockSpec(memory_space=pl.ANY)
    here = pl.BlockSpec(memory_space=pltpu.VMEM)
    dma = pltpu.SemaphoreType.DMA
    shape = jax.ShapeDtypeStruct
    count = 2 * chips * (2 * links.n_dp) + 4 * chips + 8
    hops = min(FRONT_HOPS, chips - 1)
    return pl.pallas_call(
        functools.partial(front_kernel, links),
        in_specs=[pl.BlockSpec(memory_space=pltpu.SMEM)] + [here] * 7 + [anywhere] * 3,
        out_specs=[here] + [anywhere] * 3 + [here] * 3 + [anywhere] * (1 + 2 * hops),
        out_shape=[
            shape((2 * own, depth), BF16), shape((depth, chips * width), BF16), shape((chips * width, depth), BF16),
            shape((seq, 2 * HD), BF16), shape((HD, seq), BF16), shape((seq, HD), F32), shape((seq, HD), F32),
        ]
        + [shape((own, depth), BF16)] * (1 + 2 * hops),
        scratch_shapes=[pltpu.VMEM((seq, 2 * HD), BF16), dma((count,)), dma((count,)), dma((3,))],
        compiler_params=pltpu.CompilerParams(
            collective_id=3, has_side_effects=True, vmem_limit_bytes=VMEM_LIMIT
        ),
        cost_estimate=pl.CostEstimate(flops=10**10, bytes_accessed=64 * 2**20, transcendentals=0),
        name="front",
    )(docs, tokens, gain, w_kv, cosine, sine, q_two, g_two, w_query, w_out, out_grad)


def mlp_kernel(
    links, h_hbm, wg_hbm, wu_hbm, wd_hbm, *refs,
):
    paired = 1 + min(FRONT_HOPS, links.chips - 1)
    given = [(k, half) for k in range(links.chips) for half in ((0, 1) if k < paired else (0,))]
    g_hbm, refs = refs[: len(given)], refs[len(given) :]
    (
    ghn_ref, mlp_hbm, grads_hbm, h_all, g_all, wg, wu, wd, act_t, gg_t, gu_t, mlp_in, stage, pair_out, pair_in, ring_out, ring_in,
    load_sem, ring_s, ring_r, swap_s, swap_r, pair_s, pair_r, rs_s, rs_r, mlp_s, mlp_r,
    stage_sem, store_sem, g_s, g_r,
    ) = refs
    chips = links.chips
    own, depth = h_hbm.shape
    seq = chips * 2 * own
    me = lax.axis_index("tensor")
    chip, core = me // 2, lax.rem(me, 2)
    ahead, behind = links.neighbours(chip)
    right = {"tensor": ahead * 2 + core}
    left = {"tensor": behind * 2 + core}
    sibling = {"tensor": chip * 2 + 1 - core}

    loads = [
        pltpu.make_async_copy(h_hbm, h_all.at[0, 0], load_sem.at[0]),
        pltpu.make_async_copy(wg_hbm, wg, load_sem.at[1]),
        pltpu.make_async_copy(wu_hbm, wu, load_sem.at[2]),
        pltpu.make_async_copy(wd_hbm, wd, load_sem.at[3]),
    ] + [
        pltpu.make_async_copy(ref, g_all.at[at], load_sem.at[4 + i]) for i, (ref, at) in enumerate(zip(g_hbm, given))
    ]
    for load in loads:
        load.start()
    barrier = pltpu.get_barrier_semaphore()
    for peer in (right, left, sibling):
        pl.semaphore_signal(barrier, inc=1, device_id=peer, device_id_type=pl.DeviceIdType.MESH)
    pl.semaphore_wait(barrier, 3)

    def remote(src, dst, send, recv, peer):
        return pltpu.make_async_remote_copy(
            src_ref=src, dst_ref=dst, send_sem=send, recv_sem=recv, device_id=peer,
            device_id_type=pl.DeviceIdType.MESH,
        )

    def ring(k):
        return remote(h_all.at[k, 0], h_all.at[k + 1, 0], ring_s.at[k], ring_r.at[k], right)

    def swap(k):
        return remote(h_all.at[k, 0], h_all.at[k, 1], swap_s.at[k], swap_r.at[k], sibling)

    def g_swap(k):
        return remote(g_all.at[k, 0], g_all.at[k, 1], g_s.at[k], g_r.at[k], sibling)

    def pair(k):
        slot = lax.rem(k, 2)
        return remote(pair_out.at[slot], pair_in.at[slot], pair_s.at[slot], pair_r.at[slot], sibling)

    def scatter(k):
        slot = lax.rem(k, 2)
        return remote(ring_out.at[slot], ring_in.at[k], rs_s.at[k], rs_r.at[k], right)

    def mlp_pair(k):
        slot = lax.rem(k, 2)
        return remote(stage.at[1], mlp_in.at[slot], mlp_s.at[slot], mlp_r.at[slot], sibling)

    def store(k):
        return pltpu.make_async_copy(stage.at[0], mlp_hbm.at[k], stage_sem.at[0])

    loads[0].wait()
    ring(0).start()
    swap(0).start()
    for load in loads[1:]:
        load.wait()
    for k in range(paired, chips):
        g_swap(k).start()

    def hidden_units(k, half):
        h, g = h_all[k, half], g_all[k, half]
        gate = mm(h, wg[...], NT)
        upward = mm(h, wu[...], NT)
        grad_act = mm(g, wd[...], NT)
        sigma = jax.nn.sigmoid(gate)
        swish = gate * sigma
        act = (swish * upward).astype(BF16)
        gg = (grad_act * upward * sigma * (1.0 + gate * (1.0 - sigma))).astype(BF16)
        gu = (grad_act * swish).astype(BF16)
        return act, gg, gu

    def keep_units(k, half, act, gg, gu):
        columns = pl.ds(pl.multiple_of((2 * k + half) * own, own), own)
        act_t[:, columns] = act.T
        gg_t[:, columns] = gg.T
        gu_t[:, columns] = gu.T

    def chunk(k, _):
        @pl.when(k >= 1)
        def _():
            ring(k - 1).wait_recv()

            @pl.when(k < chips - 1)
            def _():
                ring(k).start()

            swap(k).start()

        act0, gg0, gu0 = hidden_units(k, 0)
        swap(k).wait_recv()

        @pl.when(k >= paired)
        def _():
            g_swap(k).wait_recv()

        act1, gg1, gu1 = hidden_units(k, 1)

        @pl.when(k >= 2)
        def _():
            pair(k - 2).wait_send()

        pair_out[lax.rem(k, 2)] = (mm(gg1, wg[...], NN) + mm(gu1, wu[...], NN)).astype(BF16)
        pair(k).start()
        part = mm(gg0, wg[...], NN) + mm(gu0, wu[...], NN)
        pair(k).wait_recv()
        total = part + pair_in[lax.rem(k, 2)].astype(F32)

        @pl.when(k == 0)
        def _():
            ghn_ref[...] = total

        @pl.when(k == 1)
        def _():
            ring_out[1] = total.astype(BF16)
            scatter(k).start()

        @pl.when(k >= 2)
        def _():
            scatter(k - 1).wait_recv()

            @pl.when(k >= 3)
            def _():
                scatter(k - 2).wait_send()

            ring_out[lax.rem(k, 2)] = (total + ring_in[k - 1].astype(F32)).astype(BF16)
            scatter(k).start()

        @pl.when(k >= 1)
        def _():
            mlp_pair(k - 1).wait_send()

        stage[1] = mm(act1, wd[...], NN).astype(BF16)
        mlp_pair(k).start()
        keep_units(k, 0, act0, gg0, gu0)
        keep_units(k, 1, act1, gg1, gu1)
        mine = mm(act0, wd[...], NN)
        mlp_pair(k).wait_recv()

        @pl.when(k >= 1)
        def _():
            store(k - 1).wait()

        stage[0] = (mine + mlp_in[lax.rem(k, 2)].astype(F32)).astype(BF16)
        store(k).start()
        return 0

    lax.fori_loop(0, chips, chunk, 0)

    tile = 512

    def columns_of(j, _):
        at = pl.ds(pl.multiple_of(j * tile, tile), tile)
        h = h_all[:, :, :, at].reshape(seq, tile)
        g = g_all[:, :, :, at].reshape(seq, tile)
        wg[:, at] = mm(gg_t[...], h, NN).astype(BF16)
        wu[:, at] = mm(gu_t[...], h, NN).astype(BF16)
        wd[:, at] = mm(act_t[...], g, NN).astype(BF16)
        return 0

    lax.fori_loop(0, depth // tile, columns_of, 0)
    units, (pieces, _, piece) = wg.shape[0], grads_hbm.shape
    stores = [
        pltpu.make_async_copy(
            w.at[:, pl.ds(j * piece, piece)], grads_hbm.at[j, pl.ds(i * units, units)], store_sem.at[i, j]
        )
        for i, w in enumerate((wg, wu, wd))
        for j in range(pieces)
    ]
    for copy in stores:
        copy.start()
    scatter(chips - 1).wait_recv()
    ghn_ref[...] += ring_in[chips - 1].astype(F32)

    for copy in stores:
        copy.wait()
    store(chips - 1).wait()
    mlp_pair(chips - 1).wait_send()
    for k in (chips - 2, chips - 1):
        pair(k).wait_send()
        scatter(k).wait_send()
    for k in range(chips):
        swap(k).wait_send()
    for k in range(paired, chips):
        g_swap(k).wait_send()
    for k in range(chips - 1):
        ring(k).wait_send()


def feed_forward(links, hidden_own, grad_chunks, gate_t, up_t, down):
    own, depth = hidden_own.shape
    chips, units = links.chips, down.shape[0]
    seq = chips * 2 * own
    pieces = 2 * links.n_dp
    anywhere = pl.BlockSpec(memory_space=pl.ANY)
    dma = pltpu.SemaphoreType.DMA
    return pl.pallas_call(
        functools.partial(mlp_kernel, links),
        in_specs=[anywhere] * (4 + len(grad_chunks)),
        out_specs=[pl.BlockSpec(memory_space=pltpu.VMEM)] + [anywhere] * 2,
        out_shape=[
            jax.ShapeDtypeStruct((own, depth), F32),
            jax.ShapeDtypeStruct((chips, own, depth), BF16),
            jax.ShapeDtypeStruct((pieces, 3 * units, depth // pieces), BF16),
        ],
        scratch_shapes=[
            pltpu.VMEM((chips, 2, own, depth), BF16),
            pltpu.VMEM((chips, 2, own, depth), BF16),
            pltpu.VMEM((units, depth), BF16),
            pltpu.VMEM((units, depth), BF16),
            pltpu.VMEM((units, depth), BF16),
            pltpu.VMEM((units, seq), BF16),
            pltpu.VMEM((units, seq), BF16),
            pltpu.VMEM((units, seq), BF16),
            pltpu.VMEM((2, own, depth), BF16),
            pltpu.VMEM((2, own, depth), BF16),
            pltpu.VMEM((2, own, depth), BF16),
            pltpu.VMEM((2, own, depth), BF16),
            pltpu.VMEM((2, own, depth), BF16),
            pltpu.VMEM((chips, own, depth), BF16),
            dma((4 + len(grad_chunks),)),
            dma((chips,)), dma((chips,)), dma((chips,)), dma((chips,)), dma((2,)), dma((2,)),
            dma((chips,)), dma((chips,)), dma((2,)), dma((2,)), dma((1,)), dma((3, pieces)), dma((chips,)), dma((chips,)),
        ],
        compiler_params=pltpu.CompilerParams(
            collective_id=1, has_side_effects=True, vmem_limit_bytes=60 * 2**20
        ),
        cost_estimate=pl.CostEstimate(
            flops=18 * seq * depth * units, bytes_accessed=64 * 2**20, transcendentals=seq * units
        ),
        name="feed_forward",
    )(hidden_own, gate_t, up_t, down, *grad_chunks)


def mesh_copy(src, dst, send, recv, peer):
    return pltpu.make_async_remote_copy(
        src_ref=src, dst_ref=dst, send_sem=send, recv_sem=recv, device_id=peer,
        device_id_type=pl.DeviceIdType.MESH,
    )


def add_into(dst, src, rows):
    band = max(b for b in range(16, 353, 16) if rows % b == 0)

    def step(i, _):
        at = pl.ds(pl.multiple_of(i * band, band), band)
        dst[at, :] = (dst[at, :].astype(F32) + src[at, :].astype(F32)).astype(BF16)
        return 0

    lax.fori_loop(0, rows // band, step, 0)


class DpSum:
    def __init__(self, links, send, me, buf, got, free, first=0, rows=None):
        self.first, self.rows = first, rows or buf.shape[1]
        self.links, self.send, self.me, self.buf, self.got, self.free = links, send, me, buf, got, free
        self.n = links.n_dp
        self.ways = [links.bits, links.bits[::-1]]
        self.pending = []

    def at(self, way, rel):
        return way * self.n + (self.me ^ rel)

    def view(self, way, rel):
        return self.buf.at[self.at(way, rel), pl.ds(0, self.rows)]

    def kept(self, way, step):
        done = sum(self.ways[way][: step + 1])
        return [r for r in range(self.n) if r & done == 0]

    def first_slot(self, step):
        return sum(self.n >> (i + 1) for i in range(self.first, step))

    def peer(self, bit):
        return {"dp": self.me ^ bit}

    def start_halving(self, step):
        self.pending = []
        for rank in range(self.n >> (step + 1)):
            for way in (0, 1):
                bit = self.ways[way][step]
                rel = self.kept(way, step)[rank]
                slot = self.first_slot(step) + rank
                copy = self.send(self.buf.at[self.at(way, rel ^ bit)], self.got.at[way, slot], self.peer(bit), False)
                self.pending.append((copy, way, rel, slot))
        self.step = step

    def finish_halving(self):
        for copy, way, rel, slot in self.pending:
            copy.wait_recv()
            add_into(self.buf.at[self.at(way, rel)], self.got.at[way, slot], self.buf.shape[1])
        for copy, _, _, _ in self.pending:
            copy.wait_send()
        for way in (0, 1):
            pl.semaphore_signal(
                self.free.at[way, self.step], inc=1, device_id=self.peer(self.ways[way][self.step]),
                device_id_type=pl.DeviceIdType.MESH,
            )

    def start_doubling(self, step):
        self.pending = []
        if step >= self.first:
            for way in (0, 1):
                pl.semaphore_wait(self.free.at[way, step], 1)
        for rank in range(self.n >> (step + 1)):
            for way in (0, 1):
                bit = self.ways[way][step]
                rel = self.kept(way, step)[rank]
                where = self.view(way, rel)
                self.pending.append((self.send(where, where, self.peer(bit)), way, rel ^ bit))

    def finish_doubling(self):
        for copy, _, _ in self.pending:
            copy.wait_recv()
        return [(way, rel) for _, way, rel in self.pending]

    def chain(self, done, middle=()):
        rounds = len(self.links.bits)
        for step in range(self.first, rounds):
            self.start_halving(step)
            yield
            self.finish_halving()
        yield from middle
        for step in reversed(range(rounds)):
            self.start_doubling(step)
            if step == rounds - 1:
                done(0, 0)
                done(1, 0)
            yield
            for way, rel in self.finish_doubling():
                done(way, rel)


def first_halving(links, parts, me):
    n = links.n_dp
    stay, came, names = [], [], []
    for way, bits in enumerate((links.bits, links.bits[::-1])):
        for rel in range(n):
            if rel & bits[0] == 0:
                stay.append(lax.dynamic_index_in_dim(parts, way * n + (me ^ rel), 0, keepdims=False))
                other = lax.dynamic_index_in_dim(parts, way * n + (me ^ rel ^ bits[0]), 0, keepdims=False)
                came.append(links.across(other, bits[0]))
                names.append((way, rel))
    return stay, came, names


def tail_kernel(
    links, names, *refs,
):
    w_hbm, refs = refs[: len(names)], refs[len(names) :]
    (
        o_hbm, q_hbm, m_hbm, kv_keep, kv_send, gn_hbm, gn_send, tokens, normed_hbm, w_kv, cosine, sine, gain_part,
        gain, grad_hidden, hidden, terms,
        ws_hbm, ow_hbm, qw_hbm, kvw_hbm, block_ref, grad_ref, gains_ref,
        o_buf, o_in, o_ring, q_buf, q_in, w_buf, w_in, c_buf, c_in, b_buf, b_in, b_turned, got, mine, m_sem, gn_keep, normed, own_sem,
        kv_got, kv_ring, kv_in, gn_got, kvw_half, kvw_got, kvw_in, kvw_all, gains_in,
        ss, rs, o_sem, q_sem, w_sem, out_sem, w_free, o_free, b_free,
    ) = refs
    chips, bits = links.chips, links.bits
    n_dp = links.n_dp
    width = q_buf.shape[1]
    piece = w_buf.shape[2]
    me = lax.axis_index("tensor")
    me_dp = lax.axis_index("dp")
    chip, core = me // 2, lax.rem(me, 2)
    ahead, behind = links.neighbours(chip)
    right = {"tensor": ahead * 2 + core}
    left = {"tensor": behind * 2 + core}
    sibling = {"tensor": me ^ 1}
    column = [None] + [{"tensor": me ^ (2 * k)} for k in range(1, chips)]
    group = [{"tensor": me ^ k} for k in range(1, links.n_tensor)]
    replicas = [{"dp": me_dp ^ k} for k in range(1, n_dp)]

    w_loads = [
        pltpu.make_async_copy(ref, w_buf.at[way * n_dp + (me_dp ^ rel)], w_sem.at[i])
        for i, (ref, (way, rel)) in enumerate(zip(w_hbm, names))
    ]
    loads = {}
    for k in list(range(1, chips)) + [0]:
        loads["q", k] = pltpu.make_async_copy(q_hbm.at[k], q_buf.at[k], q_sem.at[k])
    o_loads = [
        pltpu.make_async_copy(o_hbm.at[:, pl.ds(j * piece, piece)], o_buf.at[j], o_sem.at[j]) for j in range(2 * n_dp)
    ]
    own_rows = pl.ds(0, gn_keep.shape[0])
    own_loads = [
        pltpu.make_async_copy(gn_hbm.at[own_rows], gn_keep, own_sem.at[0]),
        pltpu.make_async_copy(normed_hbm.at[own_rows], normed, own_sem.at[1]),
    ]
    for load in own_loads + o_loads + list(loads.values()) + w_loads:
        load.start()
    barrier = pltpu.get_barrier_semaphore()
    peers = [right, left] + group + replicas
    for peer in peers:
        pl.semaphore_signal(barrier, inc=1, device_id=peer, device_id_type=pl.DeviceIdType.MESH)
    pl.semaphore_wait(barrier, len(peers))

    copies, opened, locals_ = [], [], []

    def send(src, dst, peer, later=True):
        number = len(copies)
        copy = mesh_copy(src, dst, ss.at[number], rs.at[number], peer)
        copy.start()
        copies.append(copy)
        if later:
            opened.append(copy)
        return copy

    def put(src, dst):
        copy = pltpu.make_async_copy(src, dst, out_sem.at[len(locals_)])
        copy.start()
        locals_.append(copy)

    def ring_chain(name, buf, got):
        copy = None
        for k in list(range(1, chips)) + [0]:
            loads[name, k].wait()
            if copy is not None:
                copy.wait_recv()
                add_into(buf.at[k], got.at[(k - 1) % chips - 1], buf.shape[1])
            if k:
                copy = send(buf.at[k], got.at[k - 1], right)
            yield

    kv_swap = send(kv_send, kv_got, sibling)
    gn_swap = send(gn_send, gn_got, sibling)
    held = {}

    def kv_chain():
        for load in own_loads:
            load.wait()
        kv_swap.wait_recv()
        sent = []
        for k in range(1, chips):
            kv_ring[k - 1] = (kv_keep[k] + kv_got[k].astype(F32)).astype(BF16)
            sent.append(send(kv_ring.at[k - 1], kv_in.at[k - 1], column[k]))
        yield
        total = kv_keep[0] + kv_got[0].astype(F32)
        for k, copy in enumerate(sent):
            copy.wait_recv()
            total = total + kv_in[k].astype(F32)
        key_grad = total[:, :HD]
        key_grad = key_grad * cosine[...] - pltpu.roll(key_grad, HD // 2, 1) * sine[...]
        kv_lin = jnp.concatenate([key_grad, total[:, HD:]], axis=1).astype(BF16)
        kv_lin_t = kv_lin.T
        for half in (0, 1):
            kvw_half[half] = mm(kv_lin_t[half * HD : (half + 1) * HD], normed[...], NN).astype(BF16)
        held["swap"] = send(kvw_half.at[1 - core], kvw_got, sibling)
        yield
        gn_swap.wait_recv()
        grad = gn_keep[...] + gn_got[...].astype(F32) + mm(kv_lin, w_kv[...], NT)
        x = tokens[...].astype(F32)
        factor = lax.rsqrt(jnp.mean(x * x, axis=1, keepdims=True) + EPSILON)
        x = x * factor
        part = jnp.sum(grad * x, axis=0, keepdims=True)
        scaled = grad * gain[...]
        back = scaled - x * jnp.mean(scaled * x, axis=1, keepdims=True)
        grad_ref[...] = (grad_hidden[...] + factor * back).astype(BF16)
        lanes = gains_ref.shape[1]
        gains_ref[...] = jnp.concatenate(
            [v[:, i * lanes : (i + 1) * lanes] for v in (part, gain_part[...]) for i in range(4)], axis=0
        )

    def gains_chain():
        done = 0
        for stage in (group, replicas):
            sent = [send(gains_ref, gains_in.at[done + i], peer, False) for i, peer in enumerate(stage)]
            yield
            total = gains_ref[...]
            for i, copy in enumerate(sent):
                copy.wait_recv()
                copy.wait_send()
                total = total + gains_in[done + i]
            gains_ref[...] = total
            done += len(stage)

    band = HD // chips

    def rows_of(k):
        return pl.ds(pl.multiple_of((chip ^ k) * band, band), band)

    def kvw_chain():
        held["swap"].wait_recv()
        add_into(kvw_half.at[core], kvw_got, HD)
        sent = [send(kvw_half.at[core, rows_of(k)], kvw_in.at[k - 1], column[k]) for k in range(1, chips)]
        yield
        total = kvw_half[core, rows_of(0)].astype(F32)
        for k, copy in enumerate(sent):
            copy.wait_recv()
            total = total + kvw_in[k].astype(F32)
        c_buf[...] = total.astype(BF16)

    sum_w = DpSum(links, send, me_dp, w_buf, w_in, w_free, 1)
    sum_o = DpSum(links, send, me_dp, o_buf, o_in, o_free, 0, width)
    sum_b = DpSum(links, send, me_dp, b_buf, b_in, b_free)

    def columns(ref, number):
        return ref.at[:, pl.ds(pl.multiple_of(number * piece, piece), piece)]

    def w_chain():
        for load in w_loads:
            load.wait()
        yield from sum_w.chain(lambda way, rel: put(w_buf.at[sum_w.at(way, rel)], columns(ws_hbm, sum_w.at(way, rel))))

    def o_ring_chain():
        sent = []
        for k in list(range(1, chips)) + [0]:
            rows = pl.ds(k * width, width)
            for way, copy in enumerate(sent):
                copy.wait_recv()
                add_into(o_buf.at[sum_o.at(way, 0), rows], o_ring.at[(k - 1) % chips - 1, way], width)
            if k:
                sent = [
                    send(o_buf.at[sum_o.at(way, 0), rows], o_ring.at[k - 1, way], right) for way in (0, 1)
                ]
                yield

    def o_chain():
        for load in o_loads:
            load.wait()
        yield from sum_o.chain(
            lambda way, rel: put(sum_o.view(way, rel), columns(ow_hbm, sum_o.at(way, rel))), o_ring_chain()
        )

    def c_chain():
        sent = [send(c_buf, c_in.at[i], peer) for i, peer in enumerate(replicas)]
        yield
        total = c_buf[...].astype(F32)
        for i, copy in enumerate(sent):
            copy.wait_recv()
            total = total + c_in[i].astype(F32)
        kvw_all[0, core] = total.astype(BF16)
        sent = [send(kvw_all.at[0, core], kvw_all.at[k, core], column[k]) for k in range(1, chips)]
        yield
        for copy in sent:
            copy.wait_recv()
        copy = send(kvw_all.at[:, core], kvw_all.at[:, core], sibling)
        yield
        copy.wait_recv()
        for k in range(chips):
            for half in (0, 1):
                to = pl.ds(pl.multiple_of(half * HD + (chip ^ k) * band, band), band)
                put(kvw_all.at[k, half], kvw_hbm.at[to])

    def b_chain():
        for j in range(2 * n_dp):
            b_buf[j] = q_buf[0, :, pl.ds(j * piece, piece)]

        def turn_over(way, rel):
            at = sum_b.at(way, rel)
            b_turned[at] = b_buf[at].T
            put(b_turned.at[at], qw_hbm.at[pl.ds(pl.multiple_of(at * piece, piece), piece)])

        yield from sum_b.chain(turn_over)

    def m_chain():
        copy = send(m_hbm, got, right)
        load = pltpu.make_async_copy(terms.at[0], mine, m_sem.at[0])
        load.start()
        yield
        load.wait()
        copy.wait_recv()
        block_ref[...] = (hidden[...] + mine[...].astype(F32) + got[...].astype(F32)).astype(BF16)

    chains = {
        "w": w_chain(), "o": o_chain(), "q": ring_chain("q", q_buf, q_in), "kv": kv_chain(),
        "g": gains_chain(), "kvw": kvw_chain(), "m": m_chain(), "c": c_chain(), "b": b_chain(),
    }

    take_turns(chains, TAIL_ORDER)
    for copy in opened:
        copy.wait_send()
    for copy in locals_:
        copy.wait()


TAIL_ORDER = (
    "o kv w kv", "kvw kvw q c", "o c w o", "c o q kv", "g o w q", "g q m g", "b o b c", "o b o b", "b w m",
)


def tail(
    links, o_parts, q_parts, m_part, w_pieces, names, kv_keep, kv_send, gn_keep, gn_send, tokens, normed, w_kv, cosine,
    sine, gain_part, gain, grad_hidden, hidden, terms,
):
    chips, width, depth = q_parts.shape
    own = tokens.shape[0]
    rows, piece = w_pieces[0].shape
    band = HD // chips
    n = links.n_dp
    pieces = 2 * n
    anywhere = pl.BlockSpec(memory_space=pl.ANY)
    here = pl.BlockSpec(memory_space=pltpu.VMEM)
    dma = pltpu.SemaphoreType.DMA
    shape = jax.ShapeDtypeStruct
    count = 20 * chips + 20 * n + 16
    return pl.pallas_call(
        functools.partial(tail_kernel, links, names),
        in_specs=[anywhere] * (3 + len(names))
        + [here, here, anywhere, here, here, anywhere]
        + [here] * 7
        + [anywhere],
        out_specs=[anywhere] * 4 + [here] * 3,
        out_shape=[
            shape((rows, depth), BF16), shape((width, depth), BF16),
            shape((depth, width), BF16), shape((2 * HD, depth), BF16), shape((own, depth), BF16),
            shape((own, depth), BF16), shape((8, depth // 4), F32),
        ],
        scratch_shapes=[
            pltpu.VMEM((pieces, chips * width, piece), BF16), pltpu.VMEM((2, n - 1, chips * width, piece), BF16),
            pltpu.VMEM((chips - 1, 2, width, piece), BF16),
            pltpu.VMEM((chips, width, depth), BF16), pltpu.VMEM((chips - 1, width, depth), BF16),
            pltpu.VMEM((pieces, rows, piece), BF16), pltpu.VMEM((2, max(1, n // 2 - 1), rows, piece), BF16),
            pltpu.VMEM((band, depth), BF16), pltpu.VMEM((n - 1, band, depth), BF16),
            pltpu.VMEM((pieces, width, piece), BF16), pltpu.VMEM((2, n - 1, width, piece), BF16),
            pltpu.VMEM((pieces, piece, width), BF16), pltpu.VMEM((own, depth), BF16),
            pltpu.VMEM((own, depth), BF16), dma((1,)),
            pltpu.VMEM((own, depth), F32), pltpu.VMEM((own, depth), BF16), dma((2,)),
            pltpu.VMEM((chips, own, 2 * HD), BF16),
            pltpu.VMEM((chips - 1, own, 2 * HD), BF16), pltpu.VMEM((chips - 1, own, 2 * HD), BF16),
            pltpu.VMEM((own, depth), BF16),
            pltpu.VMEM((2, HD, depth), BF16), pltpu.VMEM((HD, depth), BF16),
            pltpu.VMEM((chips - 1, band, depth), BF16),
            pltpu.VMEM((chips, 2, band, depth), BF16),
            pltpu.VMEM((links.n_tensor + n, 8, depth // 4), F32),
            dma((count,)), dma((count,)), dma((pieces,)), dma((chips,)), dma((len(names),)),
            dma((3 * pieces + 2 * chips,)),
        ]
        + [pltpu.SemaphoreType.REGULAR((2, len(links.bits)))] * 3,
        compiler_params=pltpu.CompilerParams(
            collective_id=2, has_side_effects=True, vmem_limit_bytes=60 * 2**20
        ),
        cost_estimate=pl.CostEstimate(flops=10**9, bytes_accessed=64 * 2**20, transcendentals=0),
        name="tail",
    )(
        *w_pieces, o_parts, q_parts, m_part, kv_keep, kv_send, gn_keep, gn_send, tokens, normed, w_kv, cosine, sine,
        gain_part, gain, grad_hidden, hidden, terms,
    )


def rms_factor(values):
    return lax.rsqrt(jnp.mean(values * values, axis=-1, keepdims=True) + EPSILON)


def local(
    n_tensor, n_dp,
    tokens, out_grad, query_two, grad_two, doc_split, attn_gain, mlp_gain, w_query, w_kv, w_out, w_gate, w_up, w_down,
):
    links = Links(n_tensor, n_dp)
    chips = links.chips
    own = tokens.shape[0]
    rows = 2 * own
    seq = own * n_tensor
    width = w_query.shape[1]
    me_dp = lax.axis_index("dp")
    me_t = lax.axis_index("tensor")
    chip, core = me_t // 2, me_t % 2
    two_docs = doc_split[0]
    sp = jnp.stack([chip, two_docs, core]).astype(jnp.int32)
    place = jnp.array(links.place, jnp.int32)
    order = jnp.array(links.order, jnp.int32)

    spot = jnp.arange(rows, dtype=jnp.int32) + core * own
    spot = chip * rows + jnp.where(spot >= rows, spot - rows, spot)
    position = jnp.where(two_docs > 0, spot % SEQ_SHORT, spot)
    frequency = 10000.0 ** (-jnp.arange(HD // 2, dtype=F32) * 2.0 / HD)
    phases = position.astype(F32)[:, None] * frequency[None, :]
    cos, sin = jnp.cos(phases), jnp.sin(phases)
    cosine = jnp.concatenate([cos, cos], axis=1)
    sine = jnp.concatenate([-sin, sin], axis=1)

    residual = tokens.astype(F32)

    normed, wq, wo, kv_all, key_rows_t, dk2, dv2, *grad_chunks = front(
        links, doc_split, tokens, attn_gain[None], w_kv, cosine[:own], sine[:own], query_two, grad_two, w_query, w_out,
        out_grad,
    )
    grad_chunks = [out_grad] + grad_chunks

    q_lin = mm(normed, wq, NN)
    some = q_lin.shape[1] // HD // 2
    tables = (cosine * SCALE2, sine * SCALE2)
    results = attend(sp, q_lin, *tables, kv_all, 0, some)
    results, further = lax.optimization_barrier((results, links.ring(grad_chunks[-2])))
    later_chunks = [further]
    for _ in range(3 + FRONT_HOPS, chips + 1):
        later_chunks.append(links.ring(later_chunks[-1]))
    queries, context, lse = attend(sp, q_lin, *tables, kv_all, some, q_lin.shape[1] // HD - some, results)
    branch, later_chunks = lax.optimization_barrier((mm(context, wo, NN), later_chunks))
    branch = pair_sum(links, branch)
    hidden = residual + branch
    mlp_scale = rms_factor(hidden)
    mlp_pre = hidden * mlp_scale
    hidden_own = (mlp_pre * mlp_gain).astype(BF16)

    grad_hn, mlp_terms, ffn_parts = feed_forward(links, hidden_own, grad_chunks + later_chunks, w_gate.T, w_up.T, w_down)
    mlp_came = links.ring(mlp_terms[1])
    ffn_stay, ffn_came, ffn_names = first_halving(links, ffn_parts, me_dp)

    mlp_gain_part = jnp.sum(grad_hn * mlp_pre, axis=0)
    scaled_mlp = grad_hn * mlp_gain
    grad_hidden = out_grad.astype(F32) + mlp_scale * (
        scaled_mlp - mlp_pre * jnp.mean(scaled_mlp * mlp_pre, axis=-1, keepdims=True)
    )

    grad_branch = both(links, grad_hidden.astype(BF16))
    grad_context = mm(grad_branch, wo, NT).astype(BF16)
    query_grad, dk, dv = attend_back(
        sp, queries, grad_context, context, lse, cosine * SCALE, sine * SCALE, kv_all, key_rows_t, dk2, dv2
    )
    for k in range(2, chips - 1):
        query_grad, mlp_came = lax.optimization_barrier((query_grad, mlp_came))
        mlp_sent = (mlp_terms[k].astype(F32) + mlp_came.astype(F32)).astype(BF16)
        mlp_came = links.ring(mlp_sent)
    out_parts = mm(context, grad_branch, TN).astype(BF16)
    query_parts = mm(query_grad, normed, TN).astype(BF16).reshape(chips, width, -1)

    kv_part = jnp.concatenate([dk * (SCALE / SCALE2), dv], axis=1).reshape(chips, 2, own, 2 * HD)
    kv_part = jnp.stack(
        [
            lax.dynamic_index_in_dim(kv_part, chip ^ k, 0, keepdims=False)
            for k in range(chips)
        ]
    )
    kv_keep = lax.dynamic_index_in_dim(kv_part, core, 1, keepdims=False)
    kv_send = lax.dynamic_index_in_dim(kv_part, 1 - core, 1, keepdims=False).astype(BF16)
    gn_part = mm(query_grad, wq, NT)
    mlp_sent = (mlp_terms[chips - 1].astype(F32) + mlp_came.astype(F32)).astype(BF16)
    ffn_pieces = [(a.astype(F32) + b.astype(F32)).astype(BF16) for a, b in zip(ffn_stay, ffn_came)]
    gain_part = mlp_gain_part[None]
    ffn_w, out_w, query_w, kv_w, block_output, tokens_grad, gains = tail(
        links, out_parts, query_parts, mlp_sent, ffn_pieces, ffn_names, kv_keep, kv_send, gn_part,
        gn_part[own:].astype(BF16), tokens, normed, w_kv, cosine[:own], sine[:own], gain_part,
        attn_gain[None], grad_hidden, hidden, mlp_terms,
    )
    units = w_down.shape[0]

    gate_w_grad = ffn_w[:units].astype(F32).T
    up_w_grad = ffn_w[units : 2 * units].astype(F32).T
    down_w_grad = ffn_w[2 * units :].astype(F32)
    out_w_grad = out_w.astype(F32)
    query_w_grad = query_w.astype(F32)
    kv_w_grad = kv_w.astype(F32).T
    attn_gain_grad, mlp_gain_grad = gains[:4].reshape(-1), gains[4:].reshape(-1)

    return (
        block_output,
        tokens_grad,
        attn_gain_grad,
        mlp_gain_grad,
        query_w_grad,
        kv_w_grad,
        out_w_grad,
        gate_w_grad,
        up_w_grad,
        down_w_grad,
    )


def solution(mesh):
    both_axes = P(("dp", "tensor"), None)
    return jax.shard_map(
        functools.partial(local, mesh.shape["tensor"], mesh.shape["dp"]),
        mesh=mesh,
        in_specs=(
            both_axes,
            both_axes,
            P("dp", "tensor"),
            P("dp", "tensor"),
            P("dp"),
            P(),
            P(),
            P(None, "tensor"),
            P(),
            P("tensor", None),
            P(None, "tensor"),
            P(None, "tensor"),
            P("tensor", None),
        ),
        out_specs=(
            both_axes,
            both_axes,
            P(),
            P(),
            P(None, "tensor"),
            P(),
            P("tensor", None),
            P(None, "tensor"),
            P(None, "tensor"),
            P("tensor", None),
        ),
        check_vma=False,
    )
```
